32 devices in a mesh: narrow: 4 (over y, x), wide: 8 (over z, core).
Axes of the slice: x: 2, y: 2, z: 4, core: 2. Of those that a mesh axis runs over, the one named last changes fastest.
Arguments:
- tokens: float32 [32768, 1152], P(('narrow', 'wide')), may hold values from -6 to 6
- conditioning: bfloat16 [128, 1152], P(('narrow', 'wide')), may hold values from -6 to 6
- row_items: int32 [32], P(('narrow', 'wide')), may hold values from 1 to 4, as said below
- head_mask: int32 [128, 16], P(('narrow', 'wide')), may hold values 0 or 1
- chan_mask: int32 [128, 32], P(('narrow', 'wide')), may hold values 0 or 1
- skip_mask: int32 [32768], P(('narrow', 'wide')), may hold values 0 or 1
- ada_weight: bfloat16 [1152, 6912], P(None, ('narrow', 'wide')), may hold values from -0.25 to 0.25
- ada_bias: bfloat16 [6912], P(('narrow', 'wide')), may hold values from -3 to 3
- qkv_weight: bfloat16 [1152, 3456], P(('narrow', 'wide')), may hold values from -0.1875 to 0.1875
- query_bias: bfloat16 [1152], replicated, may hold values from -3 to 3
- value_bias: bfloat16 [1152], replicated, may hold values from -3 to 3
- proj_weight: bfloat16 [1152, 1152], P(('narrow', 'wide')), may hold values from -3.5 to 3.5
- proj_bias: bfloat16 [1152], replicated, may hold values from -3 to 3
- fc1_weight: bfloat16 [4608, 1152], P('wide', 'narrow'), may hold values from -0.1875 to 0.1875
- fc1_bias: bfloat16 [4608], replicated, may hold values from -3 to 3
- fc2_weight: bfloat16 [4608, 1152], P('wide', 'narrow'), may hold values from -0.5 to 0.5
- fc2_bias: bfloat16 [1152], replicated, may hold values from -3 to 3
- head_router: bfloat16 [1152, 16], replicated, may hold values from -0.375 to 0.375
- head_router_bias: bfloat16 [16], replicated, may hold values from -3 to 3
- chan_router: bfloat16 [1152, 32], replicated, may hold values from -0.375 to 0.375
- chan_router_bias: bfloat16 [32], replicated, may hold values from -3 to 3
- token_router: bfloat16 [1152], replicated, may hold values from -0.1875 to 0.1875
- cotangent: float32 [32768, 1152], P(('narrow', 'wide')), may hold values from -6 to 6
Outputs:
- output: float32 [32768, 1152], P(('narrow', 'wide'))
- grad_tokens: float32 [32768, 1152], P(('narrow', 'wide'))
- grad_ada_weight: float32 [1152, 6912], P(None, ('narrow', 'wide'))
- grad_ada_bias: float32 [6912], P(('narrow', 'wide'))
- grad_qkv_weight: float32 [1152, 3456], P(('narrow', 'wide'))
- grad_query_bias: float32 [1152], replicated
- grad_value_bias: float32 [1152], replicated
- grad_proj_weight: float32 [1152, 1152], P(('narrow', 'wide'))
- grad_proj_bias: float32 [1152], replicated
- grad_fc1_weight: float32 [4608, 1152], P('wide', 'narrow')
- grad_fc1_bias: float32 [4608], replicated
- grad_fc2_weight: float32 [4608, 1152], P('wide', 'narrow')
- grad_fc2_bias: float32 [1152], replicated
- grad_head_router: float32 [1152, 16], replicated
- grad_head_router_bias: float32 [16], replicated
- grad_chan_router: float32 [1152, 32], replicated
- grad_chan_router_bias: float32 [32], replicated
- grad_token_router: float32 [1152], replicated
The draws below stay inside these ranges and needn't reach their ends.
Inputs may be any that keep to these rules, and one draw needn't show every extreme that they name: `row_items`: each row holds 1 or 4 items of equal length; exactly half of the rows hold one item. Slots of a one-item row beyond the first are not read.
All inputs are finite; a program needn't handle non-finite values. No bound on the sum of `head_mask` or of `chan_mask` or of `skip_mask` on one device may be relied on, other than what follows from the above.
Results may differ from the reference program's by a relative error of at most 0.018.
The reference program's roundings to bfloat16 on the way count: a program that leaves them out, or rounds other values in their place, can miss the bound.
Values may be sent and summed in bfloat16 or wider, within the bound.
A program may use at most 448 MiB of HBM per device.

```python
import jax
import jax.numpy as jnp
from jax import lax

D = 1152
HEADS = 16
HEAD_DIM = 72
FF = 4608
CGROUPS = 32
LEN = 1024
ITEMS = 4
ROWS = 32
TOKENS = 32768
SLOTS = 128
MODS = 6912


def draw_row_items(key, part):
    key = jax.random.fold_in(key, 7)
    shuffled = jax.random.permutation(key, ROWS)
    return jnp.where(shuffled < ROWS // 2, 1, ITEMS).astype(jnp.int32)


def with_ends(result, stream_key, low, high):
    place = [jax.random.randint(jax.random.fold_in(stream_key, axis), (), 0, length) for axis, length in enumerate(result.shape)]
    longest = result.shape.index(max(result.shape))
    next_to = place[:longest] + [(place[longest] + 1) % result.shape[longest]] + place[longest + 1:]
    return result.at[tuple(place)].set(low).at[tuple(next_to)].set(high)


def block_levels(key, extent, pieces, low, high):
    def one(dim, parts):
        draws = jax.random.uniform(jax.random.fold_in(jax.random.fold_in(key, 6), dim), (parts,), jnp.float32, low / len(pieces), high / len(pieces))
        return jnp.repeat(jnp.exp(draws), extent[dim] // parts).reshape((-1,) + (1,) * (len(extent) - dim - 1))

    level = one(*pieces[0])
    for cut in pieces[1:]:
        level = level * one(*cut)
    return level


def noise(key, shape, spread, bound, shards=(), held_as=jnp.bfloat16):
    array = jax.random.normal(key, shape, jnp.float32) * spread
    if len(shards) > 0:
        array = block_levels(key, shape, shards, -0.22, 0.18) * array
    return jnp.clip(array, min=-bound, max=bound).astype(held_as)


def setup_inputs(seed: int = 0) -> dict:
    key_list = jax.random.split(jax.random.key(seed), 24)
    tokens = noise(key_list[0], (TOKENS, D), 1.0, 6.0, ((0, 32),), jnp.float32)
    conditioning = noise(key_list[1], (SLOTS, D), 1.0, 6.0, ((0, 32),))
    row_items = draw_row_items(jax.random.fold_in(key_list[23], 71), 0)
    head_mask = with_ends((jax.random.randint(key_list[3], (SLOTS, HEADS), 0, 4) < 3).astype(jnp.int32), jax.random.fold_in(key_list[3], 1), 0, 1)
    chan_mask = with_ends((jax.random.randint(key_list[4], (SLOTS, CGROUPS), 0, 4) < 3).astype(jnp.int32), jax.random.fold_in(key_list[4], 1), 0, 1)
    skip_mask = with_ends((jax.random.randint(key_list[5], (TOKENS,), 0, 4) < 1).astype(jnp.int32), jax.random.fold_in(key_list[5], 1), 0, 1)
    ada_weight = noise(key_list[6], (D, MODS), (D // 2) ** -0.5, 0.25, ((1, 32),))
    ada_bias = noise(key_list[7], (MODS,), 0.5, 3.0, ((0, 32),))
    qkv_weight = noise(key_list[8], (D, 3 * D), D ** -0.5, 0.1875, ((0, 32),))
    query_bias = noise(key_list[9], (D,), 0.5, 3.0)
    value_bias = noise(key_list[10], (D,), 0.5, 3.0)
    proj_weight = noise(key_list[11], (D, D), (max(1, D // 384)) ** -0.5, 3.5, ((0, 32),))
    proj_bias = noise(key_list[12], (D,), 0.5, 3.0)
    fc1_weight = noise(key_list[13], (FF, D), D ** -0.5, 0.1875, ((0, 8), (1, 4)))
    fc1_bias = noise(key_list[14], (FF,), 0.5, 3.0)
    fc2_weight = noise(key_list[15], (FF, D), (FF // 32) ** -0.5, 0.5, ((0, 8), (1, 4)))
    fc2_bias = noise(key_list[16], (D,), 0.5, 3.0)
    head_router = noise(key_list[17], (D, HEADS), (D // 4) ** -0.5, 0.375)
    head_router_bias = noise(key_list[18], (HEADS,), 1.0, 3.0)
    chan_router = noise(key_list[19], (D, CGROUPS), (D // 4) ** -0.5, 0.375)
    chan_router_bias = noise(key_list[20], (CGROUPS,), 1.0, 3.0)
    token_router = noise(key_list[21], (D,), D ** -0.5, 0.1875)
    cotangent = noise(key_list[22], (TOKENS, D), 1.0, 6.0, ((0, 32),), jnp.float32)
    return {"tokens": tokens, "conditioning": conditioning, "row_items": row_items, "head_mask": head_mask, "chan_mask": chan_mask, "skip_mask": skip_mask, "ada_weight": ada_weight, "ada_bias": ada_bias, "qkv_weight": qkv_weight, "query_bias": query_bias, "value_bias": value_bias, "proj_weight": proj_weight, "proj_bias": proj_bias, "fc1_weight": fc1_weight, "fc1_bias": fc1_bias, "fc2_weight": fc2_weight, "fc2_bias": fc2_bias, "head_router": head_router, "head_router_bias": head_router_bias, "chan_router": chan_router, "chan_router_bias": chan_router_bias, "token_router": token_router, "cotangent": cotangent}


@jax.custom_vjp
def low(v):
    return lax.optimization_barrier(v.astype(jnp.bfloat16)).astype(jnp.float32)

@jax.custom_vjp
def low_back(v):
    return v

def low_keep(v):
    return (low(v), None)

def low_pass(kept, grad):
    return (grad,)

def back_keep(v):
    return (v, None)

def back_low(kept, grad):
    return (low(grad),)
low.defvjp(low_keep, low_pass)
low_back.defvjp(back_keep, back_low)
HIGHEST = lax.Precision.HIGHEST
EPSILON = 1e-06
MASKED = -1e+30

def matmul_high(former, latter):
    return jnp.dot(former, latter, precision=HIGHEST)

def layer_norm(values):
    centered = values - lax.optimization_barrier(jnp.mean(values, axis=-1, keepdims=True))
    variance = lax.optimization_barrier(jnp.mean(centered * centered, axis=-1, keepdims=True))
    return centered * lax.rsqrt(variance + EPSILON)

def forward_layer(tokens, ada_weight, ada_bias, qkv_weight, query_bias, value_bias, proj_weight, proj_bias, fc1_weight, fc1_bias, fc2_weight, fc2_bias, head_router, head_router_bias, chan_router, chan_router_bias, token_router, silu_cond, row_items, head_mask, chan_mask, skip_mask):
    modulation = low(low_back(matmul_high(silu_cond, ada_weight) + ada_bias))
    head_gate = head_mask.astype(jnp.float32) * jax.nn.sigmoid(matmul_high(silu_cond, head_router) + head_router_bias)
    chan_gate = chan_mask.astype(jnp.float32) * jax.nn.sigmoid(matmul_high(silu_cond, chan_router) + chan_router_bias)
    qkv_bias = jnp.concatenate([query_bias, jnp.zeros_like(query_bias), value_bias])
    position = jnp.arange(LEN, dtype=jnp.int32)
    slot_index = jnp.arange(ITEMS, dtype=jnp.int32)

    def one_row(inputs):
        row_tokens, row_mod, row_head, row_chan, row_count, row_skip = inputs
        segment = jnp.where(row_count == 1, 0, position // (LEN // ITEMS)).astype(jnp.int32)
        slot_table = (segment[:, None] == slot_index[None, :]).astype(jnp.float32)
        spans = jnp.split(matmul_high(slot_table, row_mod), 6, axis=1)
        normed_one = low(layer_norm(row_tokens) * (1.0 + spans[1]) + spans[0])
        qkv = low(low_back(matmul_high(normed_one, qkv_weight) + qkv_bias))
        thirds = jnp.split(qkv, 3, axis=1)
        queries = thirds[0].reshape(LEN, HEADS, HEAD_DIM)
        keys_all = thirds[1].reshape(LEN, HEADS, HEAD_DIM)
        values_all = thirds[2].reshape(LEN, HEADS, HEAD_DIM)
        scores = jnp.einsum('qhd,khd->hqk', queries, keys_all, precision=HIGHEST) * HEAD_DIM ** (-0.5)
        scores = low_back(scores)
        same_item = segment[:, None] == segment[None, :]
        scores = jnp.where(same_item[None, :, :], scores, MASKED)
        probabilities = low(jax.nn.softmax(scores, axis=-1))
        attended = low_back(jnp.einsum('hqk,khd->qhd', probabilities, values_all, precision=HIGHEST))
        head_scale = matmul_high(slot_table, row_head)
        gated = low((attended * head_scale[:, :, None]).reshape(LEN, HEADS * HEAD_DIM))
        attn_out = low_back(matmul_high(gated, proj_weight) + proj_bias)
        after_attn = row_tokens + spans[2] * attn_out
        normed_two = layer_norm(after_attn) * (1.0 + spans[4]) + spans[3]
        token_gate = jax.nn.sigmoid(matmul_high(normed_two, token_router))
        pre_act = low_back(matmul_high(low(normed_two), fc1_weight.T) + fc1_bias)
        chan_scale = jnp.repeat(matmul_high(slot_table, row_chan), FF // CGROUPS, axis=1)
        scaled = low(jax.nn.gelu(pre_act, approximate=True) * chan_scale)
        mlp_out = low_back(matmul_high(scaled, fc2_weight) + fc2_bias)
        keep_scale = 1.0 - row_skip.astype(jnp.float32)
        return after_attn + spans[5] * (keep_scale * token_gate)[:, None] * mlp_out
    stacked = lax.map(jax.checkpoint(one_row), (tokens.reshape(ROWS, LEN, D), modulation.reshape(ROWS, ITEMS, MODS), head_gate.reshape(ROWS, ITEMS, HEADS), chan_gate.reshape(ROWS, ITEMS, CGROUPS), row_items, skip_mask.reshape(ROWS, LEN)))
    return stacked.reshape(TOKENS, D)

def reference(tokens, conditioning, row_items, head_mask, chan_mask, skip_mask, ada_weight, ada_bias, qkv_weight, query_bias, value_bias, proj_weight, proj_bias, fc1_weight, fc1_bias, fc2_weight, fc2_bias, head_router, head_router_bias, chan_router, chan_router_bias, token_router, cotangent):
    silu_cond = low(jax.nn.silu(conditioning.astype(jnp.float32)))
    floats = [tokens, ada_weight, ada_bias, qkv_weight, query_bias, value_bias, proj_weight, proj_bias, fc1_weight, fc1_bias, fc2_weight, fc2_bias, head_router, head_router_bias, chan_router, chan_router_bias, token_router]
    floats = [entry.astype(jnp.float32) for entry in floats]

    def forward_only(*params):
        return forward_layer(*params, silu_cond, row_items, head_mask, chan_mask, skip_mask)
    output, pull_back = jax.vjp(forward_only, *floats)
    grads = pull_back(cotangent.astype(jnp.float32))
    return (output, grads[0], grads[1], grads[2], grads[3], grads[4], grads[5], grads[6], grads[7], grads[8], grads[9], grads[10], grads[11], grads[12], grads[13], grads[14], grads[15], grads[16])
```

```python
import functools

import jax
import jax.numpy as jnp
from jax import lax
from jax.experimental import pallas as pl
from jax.experimental.pallas import tpu as pltpu
from jax.sharding import PartitionSpec as P

HIGHEST = lax.Precision.HIGHEST
F32 = jnp.float32
BF = jnp.bfloat16
EPSILON = 1e-06
MASKED = -1e30
LOG2E = 1.4426950408889634
WINDOW = 256
NN = (((1,), (0,)), ((), ()))
NT = (((1,), (1,)), ((), ()))
TN = (((0,), (0,)), ((), ()))
VMEM_SPEC = pl.BlockSpec(memory_space=pltpu.VMEM)
SMEM_SPEC = pl.BlockSpec(memory_space=pltpu.SMEM)


def dg(a, b, dims):
    return lax.dot_general(a, b, dims, preferred_element_type=F32)


def params(mib=60):
    return pltpu.CompilerParams(vmem_limit_bytes=mib << 20)


def shape(dims, dtype=F32):
    return jax.ShapeDtypeStruct(dims, dtype)


def whole(*dims):
    return pl.BlockSpec(dims, lambda i: (0,) * len(dims))


def rows_of(block, width):
    return pl.BlockSpec((block, width), lambda i: (i, 0))


def row_vec(width):
    return pl.BlockSpec((1, 1, width), lambda i: (i, 0, 0))


def ln_parts(x):
    centered = x - jnp.mean(x, axis=-1, keepdims=True)
    rstd = lax.rsqrt(jnp.mean(centered * centered, axis=-1, keepdims=True) + EPSILON)
    return centered * rstd, rstd


def ln_back(grad_y, normed, rstd, scale):
    m = grad_y * (1.0 + scale)
    mean_m = jnp.mean(m, axis=-1, keepdims=True)
    mean_mn = jnp.mean(m * normed, axis=-1, keepdims=True)
    return (m - mean_m - normed * mean_mn) * rstd


def col_sum(x):
    return jnp.sum(x, axis=0, keepdims=True)


def gelu_parts(x):
    k0 = 0.7978845608028654
    k1 = 0.044715
    x2 = x * x
    t = jnp.tanh(k0 * x * (1.0 + k1 * x2))
    half = 0.5 * (1.0 + t)
    return x * half, half + 0.5 * x * (1.0 - t * t) * (k0 * (1.0 + 3.0 * k1 * x2))


def qkv_kernel(tokens_ref, shift_ref, scale_ref, w_ref, bias_ref, n1_ref, qkv_ref):
    normed, _ = ln_parts(tokens_ref[...])
    low = (normed * (1.0 + scale_ref[0]) + shift_ref[0]).astype(BF)
    n1_ref[...] = low
    qkv_ref[...] = (dg(low, w_ref[...], NN) + bias_ref[...]).astype(BF)


def qkv_call(tokens, shift, scale, w, bias, blk):
    t, d = tokens.shape
    n = w.shape[1]
    return pl.pallas_call(
        qkv_kernel,
        grid=(t // blk,),
        out_shape=(shape((t, d), BF), shape((t, n), BF)),
        in_specs=[rows_of(blk, d), row_vec(d), row_vec(d), whole(d, n), whole(1, n)],
        out_specs=(rows_of(blk, d), rows_of(blk, n)),
        compiler_params=params(),
        name="qkv_forward",
    )(tokens, shift, scale, w, bias)


def head_window(h, hd, width):
    a = pl.multiple_of(jnp.minimum((h * hd) // 128, (width - WINDOW) // 128) * 128, 128)
    lane = lax.broadcasted_iota(jnp.int32, (1, WINDOW), 1) + a
    return a, (lane >= h * hd) & (lane < h * hd + hd)


def attn_fwd_kernel(off_ref, gate_ref, qkv_ref, att_ref, gated_ref, lse_ref, lse_sc, *, heads, blk):
    t, d = att_ref.shape
    hd = d // heads
    nb = t // blk
    c = hd**-0.5 * LOG2E
    off = off_ref[0]
    lane128 = lax.broadcasted_iota(jnp.int32, (1, 128), 1)

    def body(h, carry):
        a, mask = head_window(h, hd, d)
        keys = qkv_ref[:, pl.ds(pl.multiple_of(d + a, 128), WINDOW)]
        values = qkv_ref[:, pl.ds(pl.multiple_of(2 * d + a, 128), WINDOW)]
        cols = pl.ds(a, WINDOW)
        for i in range(nb):
            rows = pl.ds(i * blk, blk)
            q = qkv_ref[rows, cols]
            q = jnp.where(mask, q, jnp.zeros_like(q))
            s = dg(q, keys, NT)
            parts = [s[:, j * blk : (j + 1) * blk] for j in range(nb)]
            own = jnp.max(parts[i], axis=1, keepdims=True) * c
            others = functools.reduce(jnp.maximum, [parts[j] for j in range(nb) if j != i])
            m = jnp.maximum(own, jnp.max(others, axis=1, keepdims=True) * c + off)
            m_off = m - off
            ps = [jnp.exp2(parts[j] * c - (m if j == i else m_off)) for j in range(nb)]
            total = jnp.sum(functools.reduce(jnp.add, ps), axis=1, keepdims=True)
            p = jnp.concatenate([x.astype(BF) for x in ps], axis=1)
            o = dg(p, values, NN) * (1.0 / total)
            og = (o * gate_ref[i, :, cols]).astype(BF)
            att_ref[rows, cols] = jnp.where(mask, o, att_ref[rows, cols])
            gated_ref[rows, cols] = jnp.where(mask, og, gated_ref[rows, cols])
            lse_sc[rows, :] = jnp.where(lane128 == h, m + jnp.log2(total), lse_sc[rows, :])
        return carry

    lax.fori_loop(0, heads, body, 0)
    lse_ref[...] = lse_sc[...].T[:heads, :]


def attn_fwd(off, gate_rows, qkv, heads, blk):
    t = qkv.shape[0]
    d = qkv.shape[1] // 3
    return pl.pallas_call(
        functools.partial(attn_fwd_kernel, heads=heads, blk=blk),
        out_shape=(shape((t, d)), shape((t, d), BF), shape((heads, t))),
        in_specs=[SMEM_SPEC, VMEM_SPEC, VMEM_SPEC],
        out_specs=(VMEM_SPEC,) * 3,
        scratch_shapes=[pltpu.VMEM((t, 128), F32)],
        compiler_params=params(),
        name="attention_forward",
    )(off, gate_rows, qkv)


def attn_bwd_kernel(
    off_ref, qkv_ref, do_ref, lse_ref, delta_ref, dqkv_ref, kt_sc, dqt_sc, *, heads, blk
):
    t, d = do_ref.shape
    hd = d // heads
    nb = t // blk
    scale = hd**-0.5
    c = scale * LOG2E
    off = off_ref[0]
    kt_sc[...] = qkv_ref[:, d : 2 * d].T

    def body(h, carry):
        a, mask = head_window(h, hd, d)
        cols = pl.ds(a, WINDOW)
        key_cols = pl.ds(pl.multiple_of(d + a, 128), WINDOW)
        value_cols = pl.ds(pl.multiple_of(2 * d + a, 128), WINDOW)
        keys = qkv_ref[:, key_cols]
        values = qkv_ref[:, value_cols]
        keys_t = kt_sc[cols, :]
        dk_sum = None
        dv_sum = None
        for i in range(nb):
            rows = pl.ds(i * blk, blk)
            span = slice(i * blk, (i + 1) * blk)
            q = qkv_ref[rows, cols]
            q = jnp.where(mask, q, jnp.zeros_like(q))
            do = do_ref[rows, cols]
            do = jnp.where(mask, do, jnp.zeros_like(do))
            lse = lse_ref[pl.ds(h, 1), span]
            delta = delta_ref[pl.ds(h, 1), span]
            s_t = dg(keys, q, NT)
            dp_t = dg(values, do, NT)
            ps = []
            ds = []
            for j in range(nb):
                part = slice(j * blk, (j + 1) * blk)
                p = jnp.exp2(s_t[part] * c - (lse if j == i else lse - off))
                ps.append(p.astype(BF))
                ds.append((p * (dp_t[part] - delta)).astype(BF))
            p = jnp.concatenate(ps, axis=0)
            grad_s = jnp.concatenate(ds, axis=0)
            dv = dg(p, do, NN)
            dk = dg(grad_s, q, NN)
            dv_sum = dv if dv_sum is None else dv_sum + dv
            dk_sum = dk if dk_sum is None else dk_sum + dk
            dqt_sc[:, span] = (dg(keys_t, grad_s, NN) * scale).astype(BF)
        dk = (dk_sum * scale).astype(BF)
        dqkv_ref[:, key_cols] = jnp.where(mask, dk, dqkv_ref[:, key_cols])
        dqkv_ref[:, value_cols] = jnp.where(mask, dv_sum.astype(BF), dqkv_ref[:, value_cols])
        dqkv_ref[:, cols] = jnp.where(mask, dqt_sc[...].T, dqkv_ref[:, cols])
        return carry

    lax.fori_loop(0, heads, body, 0)


def attn_bwd(off, qkv, do, lse, delta, heads, blk):
    t, d = do.shape
    return pl.pallas_call(
        functools.partial(attn_bwd_kernel, heads=heads, blk=blk),
        out_shape=shape((t, 3 * d), BF),
        in_specs=[SMEM_SPEC] + [VMEM_SPEC] * 4,
        out_specs=VMEM_SPEC,
        scratch_shapes=[pltpu.VMEM((d, t), BF), pltpu.VMEM((WINDOW, t), BF)],
        compiler_params=params(),
        name="attention_backward",
    )(off, qkv, do, lse, delta)


def middle_kernel(
    gated_ref,
    w_ref,
    bias_ref,
    tokens_ref,
    cot_ref,
    keep_ref,
    router_ref,
    gate1_ref,
    shift2_ref,
    scale2_ref,
    gate2_ref,
    attn_ref,
    after_ref,
    n2_ref,
    gm_ref,
    tg_ref,
):
    attn = dg(gated_ref[...], w_ref[...], NN) + bias_ref[...]
    attn_ref[...] = attn
    after = tokens_ref[...] + gate1_ref[0] * attn
    after_ref[...] = after
    normed, _ = ln_parts(after)
    y = normed * (1.0 + scale2_ref[0]) + shift2_ref[0]
    n2_ref[...] = y.astype(BF)
    token_gate = jax.nn.sigmoid(jnp.sum(y * router_ref[...], axis=1, keepdims=True))
    tg_ref[...] = token_gate
    gm_ref[...] = (cot_ref[...] * (gate2_ref[0] * (keep_ref[...] * token_gate))).astype(BF)


def middle_call(gated, w, bias, tokens, cot, keep, router, gate1, shift2, scale2, gate2, blk):
    t, d = tokens.shape
    r, v = rows_of(blk, d), row_vec(d)
    column = rows_of(blk, 1)
    return pl.pallas_call(
        middle_kernel,
        grid=(t // blk,),
        out_shape=(shape((t, d)), shape((t, d)), shape((t, d), BF), shape((t, d), BF), shape((t, 1))),
        in_specs=[r, whole(d, d), whole(1, d), r, r, column, whole(1, d), v, v, v, v],
        out_specs=(r, r, r, r, column),
        compiler_params=params(),
        name="middle_forward",
    )(gated, w, bias, tokens, cot, keep, router, gate1, shift2, scale2, gate2)


def mlp_kernel(
    n2_ref, gm_ref, w1_ref, w2_ref, b1_ref, cs_ref, mlp_ref, gn2_ref, g1_ref, g2_ref, gb1_ref, gch_ref, sc_s, gp_s, *, blk
):
    nb = n2_ref.shape[0] // blk

    @pl.when(pl.program_id(0) == 0)
    def _():
        mlp_ref[...] = jnp.zeros_like(mlp_ref)
        gn2_ref[...] = jnp.zeros_like(gn2_ref)

    w1 = w1_ref[...]
    w2 = w2_ref[...]
    grad_bias = None
    for i in range(nb):
        rows = slice(i * blk, (i + 1) * blk)
        pre = dg(n2_ref[rows, :], w1, NT) + b1_ref[...]
        grad_scaled = dg(gm_ref[rows, :], w2, NT)
        act, slope = gelu_parts(pre)
        gate = cs_ref[i]
        scaled = (act * gate).astype(BF)
        grad_pre = (grad_scaled * gate * slope).astype(BF)
        gch_ref[i] = col_sum(grad_scaled * act)
        part = col_sum(grad_pre.astype(F32))
        grad_bias = part if grad_bias is None else grad_bias + part
        sc_s[rows, :] = scaled
        gp_s[rows, :] = grad_pre
        mlp_ref[rows, :] += dg(scaled, w2, NN)
        gn2_ref[rows, :] += dg(grad_pre, w1, NN)
    gb1_ref[...] = grad_bias
    g1_ref[...] = dg(gp_s[...], n2_ref[...], TN).astype(BF)
    g2_ref[...] = dg(sc_s[...], gm_ref[...], TN).astype(BF)


def mlp_call(n2, gm, w1, w2, b1, gates, hb, blk):
    t, d = n2.shape
    ff = w1.shape[0]
    nb = t // blk
    w_spec = pl.BlockSpec((hb, d), lambda j: (j, 0))
    b_spec = pl.BlockSpec((1, hb), lambda j: (0, j))
    c_spec = pl.BlockSpec((nb, 1, hb), lambda j: (0, 0, j))
    return pl.pallas_call(
        functools.partial(mlp_kernel, blk=blk),
        grid=(ff // hb,),
        out_shape=(
            shape((t, d)),
            shape((t, d)),
            shape((ff, d), BF),
            shape((ff, d), BF),
            shape((1, ff)),
            shape((nb, 1, ff)),
        ),
        in_specs=[whole(t, d), whole(t, d), w_spec, w_spec, b_spec, c_spec],
        out_specs=(whole(t, d), whole(t, d), w_spec, w_spec, b_spec, c_spec),
        scratch_shapes=[pltpu.VMEM((t, hb), BF), pltpu.VMEM((t, hb), BF)],
        compiler_params=params(),
        name="feed_forward",
    )(n2, gm, w1, w2, b1, gates)


def middle_back_kernel(
    mlp_ref,
    gn2_ref,
    after_ref,
    attn_ref,
    cot_ref,
    gm_ref,
    gated_ref,
    att_ref,
    tg_ref,
    keep_ref,
    w_ref,
    b2_ref,
    router_ref,
    gate1_ref,
    shift2_ref,
    scale2_ref,
    gate2_ref,
    head_ref,
    out_ref,
    ga_ref,
    do_ref,
    delta_ref,
    gw_ref,
    mod_ref,
    sums_ref,
    *,
    heads,
):
    d = after_ref.shape[1]
    hd = d // heads
    first = pl.program_id(0) == 0
    after = after_ref[...]
    cot = cot_ref[...]
    gate2 = gate2_ref[0]
    tg = tg_ref[...]
    keep = keep_ref[...]
    normed, rstd = ln_parts(after)
    scale2 = scale2_ref[0]
    y = normed * (1.0 + scale2) + shift2_ref[0]
    mlp_out = mlp_ref[...] + b2_ref[...]
    open_gate = keep * tg
    out_ref[...] = after + (gate2 * open_gate) * mlp_out
    weighted = cot * mlp_out
    grad_tg = jnp.sum(weighted * gate2, axis=1, keepdims=True) * keep
    coef = grad_tg * tg * (1.0 - tg)
    gy = gn2_ref[...] + coef * router_ref[...]
    ga = cot + ln_back(gy, normed, rstd, scale2)
    ga_ref[...] = ga
    attn = attn_ref[...]
    g_attn = (ga * gate1_ref[0]).astype(BF)
    mod_ref[0] = jnp.concatenate(
        [col_sum(ga * attn), col_sum(gy), col_sum(gy * normed), col_sum(weighted * open_gate)], axis=0
    )
    sums = jnp.concatenate(
        [
            col_sum(coef * y),
            col_sum(g_attn.astype(F32)),
            col_sum(gm_ref[...].astype(F32)),
        ],
        axis=0,
    )
    g_gated = dg(g_attn, w_ref[...], NT)
    att = att_ref[...]
    mod_ref[1] = jnp.concatenate([col_sum(g_gated * att), jnp.zeros((3, d), F32)], axis=0)
    do = (g_gated * head_ref[0]).astype(BF)
    do_ref[...] = do
    lane = lax.broadcasted_iota(jnp.int32, (heads, d), 1)
    head = lax.broadcasted_iota(jnp.int32, (heads, d), 0) * hd
    pick = jnp.where((lane >= head) & (lane < head + hd), 1.0, 0.0)
    delta_ref[...] = lax.dot_general(
        pick, do.astype(F32) * att, NT, precision=HIGHEST, preferred_element_type=F32
    )
    gw = dg(gated_ref[...], g_attn, TN)

    @pl.when(first)
    def _():
        sums_ref[...] = sums
        gw_ref[...] = gw

    @pl.when(jnp.logical_not(first))
    def _():
        sums_ref[...] += sums
        gw_ref[...] += gw


def middle_back_call(
    mlp, gn2, after, attn, cot, gm, gated, att, tg, keep, w, b2, router, gate1, shift2, scale2, gate2, head_rows, heads, blk
):
    t, d = after.shape
    nb = t // blk
    r, v, column = rows_of(blk, d), row_vec(d), rows_of(blk, 1)
    return pl.pallas_call(
        functools.partial(middle_back_kernel, heads=heads),
        grid=(nb,),
        out_shape=(
            shape((t, d)),
            shape((t, d)),
            shape((t, d), BF),
            shape((heads, t)),
            shape((d, d)),
            shape((nb * 2, 4, d)),
            shape((3, d)),
        ),
        in_specs=[r] * 8 + [column, column, whole(d, d), whole(1, d), whole(1, d), v, v, v, v, v],
        out_specs=(
            r,
            r,
            r,
            pl.BlockSpec((heads, blk), lambda i: (0, i)),
            whole(d, d),
            pl.BlockSpec((2, 4, d), lambda i: (i, 0, 0)),
            whole(3, d),
        ),
        compiler_params=params(),
        name="middle_backward",
    )(mlp, gn2, after, attn, cot, gm, gated, att, tg, keep, w, b2, router, gate1, shift2, scale2, gate2, head_rows)


def qkv_weight_kernel(n1_ref, dqkv_ref, gw_ref, bias_ref, n1t):
    @pl.when(pl.program_id(0) == 0)
    def _():
        n1t[...] = n1_ref[...].T

    dqkv = dqkv_ref[...]
    gw_ref[...] = dg(n1t[...], dqkv, NN).astype(gw_ref.dtype)
    bias_ref[...] = col_sum(dqkv.astype(F32))


def qkv_weight_call(n1, dqkv, width, dtype):
    t, d = n1.shape
    n = dqkv.shape[1]
    return pl.pallas_call(
        qkv_weight_kernel,
        grid=(n // width,),
        out_shape=(shape((d, n), dtype), shape((1, n))),
        in_specs=[whole(t, d), pl.BlockSpec((t, width), lambda j: (0, j))],
        out_specs=(
            pl.BlockSpec((d, width), lambda j: (0, j)),
            pl.BlockSpec((1, width), lambda j: (0, j)),
        ),
        scratch_shapes=[pltpu.VMEM((d, t), BF)],
        compiler_params=params(),
        name="qkv_weight_gradient",
    )(n1, dqkv)


def qkv_back_kernel(dqkv_ref, w_ref, tokens_ref, ga_ref, scale_ref, out_ref, mod_ref):
    gy = dg(dqkv_ref[...], w_ref[...], NT)
    normed, rstd = ln_parts(tokens_ref[...])
    out_ref[...] = ga_ref[...] + ln_back(gy, normed, rstd, scale_ref[0])
    mod_ref[0] = jnp.concatenate([col_sum(gy), col_sum(gy * normed)], axis=0)


def qkv_back_call(dqkv, w, tokens, ga, scale, blk):
    t, d = tokens.shape
    n = dqkv.shape[1]
    r = rows_of(blk, d)
    return pl.pallas_call(
        qkv_back_kernel,
        grid=(t // blk,),
        out_shape=(shape((t, d)), shape((t // blk, 2, d))),
        in_specs=[rows_of(blk, n), whole(d, n), r, r, row_vec(d)],
        out_specs=(r, pl.BlockSpec((1, 2, d), lambda i: (i, 0, 0))),
        compiler_params=params(),
        name="qkv_backward",
    )(dqkv, w, tokens, ga, scale)


def on_device(
    tokens,
    conditioning,
    row_items,
    head_mask,
    chan_mask,
    skip_mask,
    ada_weight,
    ada_bias,
    qkv_weight,
    query_bias,
    value_bias,
    proj_weight,
    proj_bias,
    fc1_weight,
    fc1_bias,
    fc2_weight,
    fc2_bias,
    head_router,
    head_router_bias,
    chan_router,
    chan_router_bias,
    token_router,
    cotangent,
):
    axes = ("narrow", "wide")
    t, d = tokens.shape
    slots = conditioning.shape[0]
    heads = head_mask.shape[1]
    groups = chan_mask.shape[1]
    hidden = fc1_bias.shape[0]
    hd = d // heads
    unit = hidden // groups
    blk = t // slots
    single = row_items[0] == 1
    off = jnp.where(single, 0.0, MASKED).astype(F32).reshape(1)

    def per_block(table):
        return jnp.where(single, table[:1], table)

    def per_slot(blocks):
        total = jnp.sum(blocks, axis=0, keepdims=True)
        first = (jnp.arange(slots) == 0).reshape((slots,) + (1,) * (blocks.ndim - 1))
        return jnp.where(single, jnp.where(first, total, 0.0), blocks)

    silu_cond = jax.nn.silu(conditioning.astype(F32)).astype(BF)
    every_cond = lax.all_gather(silu_cond, axes, axis=0, tiled=True)
    mod_columns = jnp.dot(every_cond, ada_weight, preferred_element_type=F32) + ada_bias.astype(F32)
    modulation = lax.all_to_all(
        mod_columns.astype(BF), axes, split_axis=0, concat_axis=1, tiled=True
    )
    mod_rows = per_block(modulation.astype(F32)).reshape(slots, 6, 1, d)
    shift1, scale1, gate1, shift2, scale2, gate2 = [mod_rows[:, k] for k in range(6)]
    cond_float = silu_cond.astype(F32)

    def router(weight, bias, mask):
        gate = jax.nn.sigmoid(
            jnp.dot(cond_float, weight.astype(F32), precision=HIGHEST) + bias.astype(F32)
        )
        mask = mask.astype(F32)
        return mask * gate, mask * gate * (1.0 - gate)

    head_gate, head_slope = router(head_router, head_router_bias, head_mask)
    chan_gate, chan_slope = router(chan_router, chan_router_bias, chan_mask)
    head_rows = jnp.repeat(per_block(head_gate), hd, axis=1)[:, None, :]
    chan_rows = jnp.repeat(per_block(chan_gate), unit, axis=1)[:, None, :]
    keep = (1.0 - skip_mask.astype(F32))[:, None]

    full_qkv = lax.all_gather(qkv_weight, axes, axis=0, tiled=True)
    full_proj = lax.all_gather(proj_weight, axes, axis=0, tiled=True)
    fc1_rows = lax.all_gather(fc1_weight, "narrow", axis=1, tiled=True)
    fc2_rows = lax.all_gather(fc2_weight, "narrow", axis=1, tiled=True)
    full_fc1 = lax.all_gather(fc1_rows, "wide", axis=0, tiled=True)
    full_fc2 = lax.all_gather(fc2_rows, "wide", axis=0, tiled=True)

    qkv_bias = jnp.concatenate([query_bias, jnp.zeros_like(query_bias), value_bias])
    n1, qkv = qkv_call(tokens, shift1, scale1, full_qkv, qkv_bias.astype(F32)[None], blk)
    att, gated, lse = attn_fwd(off, head_rows, qkv, heads, blk)
    router_row = token_router.astype(F32)[None]
    attn, after, n2, gm, tg = middle_call(
        gated,
        full_proj,
        proj_bias.astype(F32)[None],
        tokens,
        cotangent,
        keep,
        router_row,
        gate1,
        shift2,
        scale2,
        gate2,
        blk,
    )
    mlp, gn2, g_fc1, g_fc2, gb1, gch = mlp_call(
        n2, gm, full_fc1, full_fc2, fc1_bias.astype(F32)[None], chan_rows, hidden // 6, blk
    )
    output, ga, do, delta, g_proj, mods, sums = middle_back_call(
        mlp,
        gn2,
        after,
        attn,
        cotangent,
        gm,
        gated,
        att,
        tg,
        keep,
        full_proj,
        fc2_bias.astype(F32)[None],
        router_row,
        gate1,
        shift2,
        scale2,
        gate2,
        head_rows,
        heads,
        blk,
    )
    mods = mods.reshape(slots, 8, d)
    fc_sum = lax.psum_scatter(
        jnp.stack([g_fc1, g_fc2], axis=1), "wide", scatter_dimension=0, tiled=True
    )
    fc_grads = lax.psum_scatter(fc_sum, "narrow", scatter_dimension=2, tiled=True).astype(F32)
    dqkv = attn_bwd(off, qkv, do, lse, delta, heads, blk)
    g_qkv, qkv_sums = qkv_weight_call(n1, dqkv, 3 * d // 9, BF)
    attn_grads = lax.psum_scatter(
        jnp.concatenate([g_qkv, g_proj.astype(BF)], axis=1), axes, scatter_dimension=0, tiled=True
    ).astype(F32)
    grad_tokens, mods1 = qkv_back_call(dqkv, full_qkv, tokens, ga, scale1, blk)
    block_mods = jnp.concatenate(
        [mods1[:, 0], mods1[:, 1], mods[:, 0], mods[:, 1], mods[:, 2], mods[:, 3]], axis=1
    )
    grad_slot_mod = per_slot(block_mods).astype(BF)
    grad_mod_columns = lax.all_to_all(
        grad_slot_mod, axes, split_axis=1, concat_axis=0, tiled=True
    )
    grad_ada_weight = dg(every_cond, grad_mod_columns, TN)
    grad_ada_bias = jnp.sum(grad_mod_columns.astype(F32), axis=0)
    g_head = per_slot(jnp.sum(mods[:, 4].reshape(slots, heads, hd), axis=2)) * head_slope
    g_chan = per_slot(jnp.sum(gch.reshape(slots, groups, unit), axis=2)) * chan_slope
    logits = lax.all_gather(
        jnp.concatenate([g_head, g_chan], axis=1), axes, axis=0, tiled=True
    )
    router_grads = lax.dot_general(
        every_cond.astype(F32), logits, TN, precision=HIGHEST, preferred_element_type=F32
    )
    logit_sums = jnp.sum(logits, axis=0)
    small = lax.psum(
        jnp.concatenate(
            [
                qkv_sums[0, :d],
                qkv_sums[0, 2 * d :],
                sums[1],
                gb1[0],
                sums[2],
                sums[0],
            ]
        ),
        axes,
    )
    ends = [d, 2 * d, 3 * d, 3 * d + hidden, 4 * d + hidden]
    g_query, g_value, g_proj_bias, g_b1, g_b2, g_router = jnp.split(small, ends)
    return (
        output,
        grad_tokens,
        grad_ada_weight,
        grad_ada_bias,
        attn_grads[:, : 3 * d],
        g_query,
        g_value,
        attn_grads[:, 3 * d :],
        g_proj_bias,
        fc_grads[:, 0],
        g_b1,
        fc_grads[:, 1],
        g_b2,
        router_grads[:, :heads],
        logit_sums[:heads],
        router_grads[:, heads:],
        logit_sums[heads:],
        g_router,
    )


def solution(mesh):
    return jax.shard_map(
        on_device,
        mesh=mesh,
        in_specs=(
            P(("narrow", "wide"), None),
            P(("narrow", "wide"), None),
            P(("narrow", "wide")),
            P(("narrow", "wide"), None),
            P(("narrow", "wide"), None),
            P(("narrow", "wide")),
            P(None, ("narrow", "wide")),
            P(("narrow", "wide")),
            P(("narrow", "wide"), None),
            P(),
            P(),
            P(("narrow", "wide"), None),
            P(),
            P("wide", "narrow"),
            P(),
            P("wide", "narrow"),
            P(),
            P(),
            P(),
            P(),
            P(),
            P(),
            P(("narrow", "wide"), None),
        ),
        out_specs=(
            P(("narrow", "wide"), None),
            P(("narrow", "wide"), None),
            P(None, ("narrow", "wide")),
            P(("narrow", "wide")),
            P(("narrow", "wide"), None),
            P(),
            P(),
            P(("narrow", "wide"), None),
            P(),
            P("wide", "narrow"),
            P(),
            P("wide", "narrow"),
            P(),
            P(),
            P(),
            P(),
            P(),
            P(),
        ),
        check_vma=False,
    )
```

```python
import functools

import jax
import jax.numpy as jnp
from jax import lax
from jax.experimental import pallas as pl
from jax.experimental.pallas import tpu as pltpu
from jax.sharding import PartitionSpec as P

HIGHEST = lax.Precision.HIGHEST
F32 = jnp.float32
BF = jnp.bfloat16
EPSILON = 1e-06
MASKED = -1e30
LOG2E = 1.4426950408889634
WINDOW = 256
NN = (((1,), (0,)), ((), ()))
NT = (((1,), (1,)), ((), ()))
TN = (((0,), (0,)), ((), ()))
VMEM_SPEC = pl.BlockSpec(memory_space=pltpu.VMEM)
ANY_SPEC = pl.BlockSpec(memory_space=pl.ANY)
MESH = pl.DeviceIdType.MESH
SMEM_SPEC = pl.BlockSpec(memory_space=pltpu.SMEM)


def dg(a, b, dims):
    return lax.dot_general(a, b, dims, preferred_element_type=F32)


def params(mib=60, collective_id=None):
    if collective_id is None:
        return pltpu.CompilerParams(vmem_limit_bytes=mib << 20)
    return pltpu.CompilerParams(
        vmem_limit_bytes=mib << 20, collective_id=collective_id, has_side_effects=True
    )


def up_to(count, multiple):
    return -(-count // multiple) * multiple


def pad_rows(x):
    return jnp.pad(x, ((0, up_to(x.shape[0], 16) - x.shape[0]), (0, 0)))


def spread_out(steps, count):
    groups = [[] for _ in range(count)]
    for i, step in enumerate(steps):
        groups[i * count // len(steps)].append(step)
    return groups


def run_at(index, groups):
    for i, group in enumerate(groups):
        if group:

            @pl.when(index == i)
            def _(group=group):
                for step in group:
                    step()


def shape(dims, dtype=F32):
    return jax.ShapeDtypeStruct(dims, dtype)


def whole(*dims):
    return pl.BlockSpec(dims, lambda i: (0,) * len(dims), pipeline_mode=pl.Buffered(1))


def rows_of(block, width):
    return pl.BlockSpec((block, width), lambda i: (i, 0))


def row_vec(width):
    return pl.BlockSpec((1, 1, width), lambda i: (i, 0, 0))


def ln_parts(x):
    centered = x - jnp.mean(x, axis=-1, keepdims=True)
    rstd = lax.rsqrt(jnp.mean(centered * centered, axis=-1, keepdims=True) + EPSILON)
    return centered * rstd, rstd


def ln_back(grad_y, normed, rstd, scale):
    m = grad_y * (1.0 + scale)
    mean_m = jnp.mean(m, axis=-1, keepdims=True)
    mean_mn = jnp.mean(m * normed, axis=-1, keepdims=True)
    return (m - mean_m - normed * mean_mn) * rstd


def col_sum(x):
    return jnp.sum(x, axis=0, keepdims=True)


def gelu_parts(x):
    k0 = 0.7978845608028654
    k1 = 0.044715
    x2 = x * x
    t = jnp.tanh(k0 * x * (1.0 + k1 * x2))
    half = 0.5 * (1.0 + t)
    return x * half, half + 0.5 * x * (1.0 - t * t) * (k0 * (1.0 + 3.0 * k1 * x2))


class Place:
    def __init__(self, planes):
        self.planes = planes
        self.n = lax.axis_index("narrow")
        w = lax.axis_index("wide")
        self.z = w // 2
        self.c = w % 2
        self.xn = self.n + 1 - 2 * (self.n % 2)
        self.yn = self.n + 2 - 4 * (self.n // 2)
        self.dn = 3 - self.n

    def dev(self, n, z, c):
        return (n, z * 2 + c)

    def barrier(self, every_plane=False):
        sem = pltpu.get_barrier_semaphore()

        def greet(n, z, c):
            pl.semaphore_signal(sem, inc=1, device_id=self.dev(n, z, c), device_id_type=MESH)

        greet(self.xn, self.z, self.c)
        greet(self.yn, self.z, self.c)
        greet(self.n, self.z, 1 - self.c)
        if every_plane:
            for k in range(1, self.planes):
                greet(self.n, lax.rem(self.z + k, self.planes), self.c)
            pl.semaphore_wait(sem, self.planes + 2)
            return
        for step in (-1, 1):

            @pl.when(self.has(step))
            def _(step=step):
                greet(self.n, self.z + step, self.c)

        ends = jnp.where(self.z > 0, 1, 0) + jnp.where(self.z < self.planes - 1, 1, 0)
        pl.semaphore_wait(sem, 3 + ends)

    def has(self, step):
        return self.z + step >= 0 if step < 0 else self.z + step < self.planes


def remote(src, dst, sems, idx, device):
    return pltpu.make_async_remote_copy(
        src_ref=src,
        dst_ref=dst,
        send_sem=sems.at[0, idx],
        recv_sem=sems.at[1, idx],
        device_id=device,
        device_id_type=MESH,
    )


class Gather:
    def __init__(self, place, src, out, own, zs, xs, ys, ds, cs):
        self.p, self.src, self.out = place, src, out
        self.own, self.zs, self.xs, self.ys, self.ds, self.cs = own, zs, xs, ys, ds, cs
        self.steps = [0]
        for k in range(1, place.planes):
            self.steps += [-k, k]

    def index(self, k):
        return k + self.p.planes - 1

    def at(self, n, k, c=None):
        p = self.p
        return self.out.at[n, p.z + k, p.c if c is None else c]

    def mine(self, k):
        return self.src if k == 0 else self.at(self.p.n, k)

    def via(self, k):
        p = self.p
        return (p.xn, p.yn) if k % 2 == 0 else (p.yn, p.xn)

    def copy(self, kind, k):
        p = self.p
        i = self.index(k)
        if kind == "x":
            return remote(self.mine(k), self.at(p.n, k), self.xs, i, p.dev(p.xn, p.z, p.c))
        if kind == "y":
            return remote(self.mine(k), self.at(p.n, k), self.ys, i, p.dev(p.yn, p.z, p.c))
        if kind == "d":
            via, to = self.via(k)
            return remote(self.at(via, k), self.at(via, k), self.ds, i, p.dev(to, p.z, p.c))
        if kind == "up" or kind == "down":
            step = 1 if kind == "up" else -1
            j = self.index(k - step)
            return remote(self.mine(k), self.at(p.n, k), self.zs, j, p.dev(p.n, p.z + step, p.c))
        j = ("c", "C", "d2", "D").index(kind)
        n = (p.n, p.xn, p.yn, p.dn)[j]
        shard = self.mine(k) if j == 0 else self.at(n, k)
        slot = j * (2 * p.planes - 1) + i
        return remote(shard, self.at(n, k), self.cs, slot, p.dev(p.n, p.z, 1 - p.c))

    def arrived(self, n, k, sems, idx, c=None):
        p = self.p
        dst = self.at(n, k, c)
        remote(dst, dst, sems, idx, p.dev(p.xn, p.z, p.c)).wait_recv()

    def run(self, part):
        if part == "begin":
            pltpu.make_async_copy(self.src, self.at(self.p.n, 0), self.own).start()
            self.spread(0)
        elif part == "end":
            pltpu.make_async_copy(self.src, self.at(self.p.n, 0), self.own).wait()
            for k in self.steps:
                self.when(self.p.has(k), functools.partial(self.finish, k))
        else:
            kind, k = part
            self.when(self.p.has(k), functools.partial(getattr(self, kind), k))

    def when(self, cond, do):
        pl.when(cond)(do)

    def onward(self, k, act):
        p = self.p
        if k <= 0:
            self.when(p.has(1), lambda: act(self.copy("up", k)))
        if k >= 0:
            self.when(p.has(-1), lambda: act(self.copy("down", k)))

    def spread(self, k):
        self.onward(k, lambda copy: copy.start())
        self.copy("x", k).start()
        self.copy("y", k).start()
        self.copy("c", k).start()

    def plane(self, k):
        self.arrived(self.p.n, k, self.zs, self.index(k))
        self.spread(k)

    def near(self, k):
        p = self.p
        self.arrived(p.xn, k, self.xs, self.index(k))
        if k % 2 == 0:
            self.copy("d", k).start()
        self.copy("C", k).start()
        self.arrived(p.yn, k, self.ys, self.index(k))
        if k % 2 == 1:
            self.copy("d", k).start()
        self.copy("d2", k).start()

    def far(self, k):
        self.arrived(self.p.dn, k, self.ds, self.index(k))
        self.copy("D", k).start()

    def finish(self, k):
        p = self.p
        for j, n in enumerate((p.n, p.xn, p.yn, p.dn)):
            self.arrived(n, k, self.cs, j * (2 * p.planes - 1) + self.index(k), 1 - p.c)
        for kind in ("x", "y", "d", "c", "C", "d2", "D"):
            self.copy(kind, k).wait_send()
        self.onward(k, lambda copy: copy.wait_send())

    def parts(self):
        found = ["begin"]
        rounds = [[0]] + [[-k, k] for k in range(1, self.p.planes)]
        for r in range(len(rounds) + 2):
            if 0 < r < len(rounds):
                found += [("plane", k) for k in rounds[r]]
            if 1 <= r <= len(rounds):
                found += [("near", k) for k in rounds[r - 1]]
            if 2 <= r:
                found += [("far", k) for k in rounds[r - 2]]
        return found + ["end"]

    @staticmethod
    def scratch(planes):
        dma = pltpu.SemaphoreType.DMA
        span = 2 * planes - 1
        return [dma(())] + [dma((2, span))] * 4 + [dma((2, 4 * span))]


class Scatter:
    def __init__(self, place, part, out, own, r1, r2, r3, r4, own_sem, s1, s2, s3, s4):
        self.p, self.part, self.out = place, part, out
        self.own, self.r1, self.r2, self.r3, self.r4 = own, r1, r2, r3, r4
        self.own_sem, self.s1, self.s2, self.s3, self.s4 = own_sem, s1, s2, s3, s4

    def owner(self, j):
        return lax.rem(self.p.z + 1 + j, self.p.planes)

    def load(self, j):
        p = self.p
        return pltpu.make_async_copy(
            self.part.at[:, self.owner(j), p.c], self.own.at[j % 2], self.own_sem.at[j % 2]
        )

    def sides(self, j):
        p = self.p
        return (p.xn, p.yn) if j % 2 == 0 else (p.yn, p.xn)

    def copies(self, stage, j):
        p = self.p
        side, other = self.sides(j)
        if stage == 1:
            to = p.dev(p.n, p.z, 1 - p.c)
            return [remote(self.part.at[:, self.owner(j), 1 - p.c], self.r1.at[j], self.s1, j, to)]
        if stage == 2:
            to = p.dev(side, p.z, p.c)
            return [
                remote(self.r1.at[j, side], self.r2.at[j, 0], self.s2, 2 * j, to),
                remote(self.r1.at[j, p.dn], self.r2.at[j, 1], self.s2, 2 * j + 1, to),
            ]
        if stage == 3:
            to = p.dev(other, p.z, p.c)
            return [remote(self.r1.at[j, other], self.r3.at[j], self.s3, j, to)]
        to = p.dev(p.n, self.owner(j), p.c)
        return [remote(self.r1.at[j, p.n], self.r4.at[j], self.s4, j, to)]

    def issue(self, stage, j):
        for copy in self.copies(stage, j):
            copy.start()

    def take(self, stage, j):
        p = self.p
        for copy in self.copies(stage, j):
            copy.wait_recv()
        side, other = self.sides(j)

        def add(n, value):
            self.r1[j, n] = (self.r1[j, n].astype(F32) + value.astype(F32)).astype(BF)

        if stage == 1:
            self.load(j).wait()
            if j + 1 < p.planes:
                self.load(j + 1).start()
            for n in range(4):
                add(n, self.own[j % 2, n])
        elif stage == 2:
            add(p.n, self.r2[j, 0])
            add(other, self.r2[j, 1])
        else:
            add(p.n, self.r3[j])
            if j + 1 < p.planes:
                self.issue(4, j)

    def end(self):
        planes = self.p.planes
        total = self.r1[planes - 1, self.p.n].astype(F32)
        for j in range(planes - 1):
            self.copies(4, j)[0].wait_recv()
            total = total + self.r4[j].astype(F32)
        self.out[...] = total
        for j in range(planes):
            for stage in (1, 2, 3, 4):
                if stage < 4 or j + 1 < planes:
                    for copy in self.copies(stage, j):
                        copy.wait_send()

    @staticmethod
    def scratch(planes, rows, cols):
        dma = pltpu.SemaphoreType.DMA
        return [
            pltpu.VMEM((2, 4, rows, cols), BF),
            pltpu.VMEM((planes, 4, rows, cols), BF),
            pltpu.VMEM((planes, 2, rows, cols), BF),
            pltpu.VMEM((planes, rows, cols), BF),
            pltpu.VMEM((planes - 1, rows, cols), BF),
            dma((2,)),
            dma((2, planes)),
            dma((2, 2 * planes)),
            dma((2, planes)),
            dma((2, planes)),
        ]


def scatter_steps(scatters, window=2):
    planes = scatters[0].p.planes
    count = len(scatters)
    queue = [(u, j) for j in range(planes) for u in range(count)]
    x_items, y_items = [], []
    for even in range(0, planes, 2):
        for stage, swap in ((2, 0), (3, 1)):
            x_items += [(stage, u, even + swap) for u in range(count)]
            y_items += [(stage, u, even + 1 - swap) for u in range(count)]
    sent = []
    done = []

    def begin():
        for s in scatters:
            s.load(0).start()
        for u, j in queue[:window]:
            scatters[u].issue(1, j)
            sent.append((u, j))

    def ready(stage, u, j):
        if stage == 2:
            while (u, j) not in done:
                v, i = queue[len(done)]
                scatters[v].take(1, i)
                done.append((v, i))
                if len(sent) < len(queue):
                    v, i = queue[len(sent)]
                    scatters[v].issue(1, i)
                    sent.append((v, i))

    def step(i):
        for items in (x_items, y_items):
            if i >= window:
                stage, u, j = items[i - window]
                scatters[u].take(stage, j)
        for items in (x_items, y_items):
            if i < len(items):
                stage, u, j = items[i]
                ready(stage, u, j)
                scatters[u].issue(stage, j)

    def end():
        for s in scatters:
            s.end()

    steps = [functools.partial(step, i) for i in range(len(x_items) + window)]
    return [begin] + steps + [end]


def prologue_kernel(
    shard_ref, cond_ref, ada_ref, ada_bias_ref, g_ref, conds_ref, mods_ref, mod_local, *sems, planes, items
):
    place = Place(planes)
    place.barrier()
    weights = Gather(place, shard_ref, g_ref, *sems[:6])
    conds = Gather(place, cond_ref, conds_ref, *sems[6:12])
    mods = Gather(place, mod_local, mods_ref, *sems[12:])
    parts = weights.parts()
    conds.run("begin")
    weights.run("begin")
    for part in parts[1:]:
        conds.run(part)
    devices = 8 * planes
    rows = cond_ref.shape[0]
    every = conds_ref[...].reshape(devices * rows, cond_ref.shape[1])
    columns = (dg(every, ada_ref[...], NN) + ada_bias_ref[...]).reshape(devices, rows, -1)
    width = columns.shape[2]
    mod_local[...] = jnp.zeros_like(mod_local)
    for i in range(devices):
        mod_local[i * items : (i + 1) * items, :width] = columns[i, :items].astype(BF)
    mods.run("begin")
    for part in parts[1:]:
        weights.run(part)
        mods.run(part)


def prologue_call(shard, cond, ada, ada_bias, planes, items):
    devices = 8 * planes
    rows, d = cond.shape
    lanes = up_to(ada.shape[1], 128)
    slots = devices * items
    spread = (4, planes, 2)
    return pl.pallas_call(
        functools.partial(prologue_kernel, planes=planes, items=items),
        out_shape=(
            shape(spread + shard.shape, BF),
            shape(spread + (rows, d), BF),
            shape(spread + (slots, lanes), BF),
        ),
        in_specs=[ANY_SPEC, VMEM_SPEC, VMEM_SPEC, VMEM_SPEC],
        out_specs=(ANY_SPEC, VMEM_SPEC, ANY_SPEC),
        scratch_shapes=[pltpu.VMEM((slots, lanes), BF)] + Gather.scratch(planes) * 3,
        compiler_params=params(collective_id=1),
        name="weights_and_modulation",
    )(shard, cond, ada, ada_bias)


def qkv_kernel(tokens_ref, shift_ref, scale_ref, g_ref, bias_ref, n1_ref, qkv_ref, w_ref, wp_ref):
    d = tokens_ref.shape[1]
    devices = g_ref.shape[0]
    r = d // devices

    @pl.when(pl.program_id(0) == 0)
    def _():
        for i in range(devices):
            rows = slice(i * r, (i + 1) * r)
            for b in range(3):
                w_ref[rows, b * d : (b + 1) * d] = g_ref[i, b * r : (b + 1) * r, :]
            wp_ref[rows, :] = g_ref[i, 3 * r : 4 * r, :]

    normed, _ = ln_parts(tokens_ref[...])
    low = (normed * (1.0 + scale_ref[0]) + shift_ref[0]).astype(BF)
    n1_ref[...] = low
    qkv_ref[...] = (dg(low, w_ref[...], NN) + bias_ref[...]).astype(BF)


def qkv_call(tokens, shift, scale, g, bias, blk):
    t, d = tokens.shape
    n = 3 * d
    return pl.pallas_call(
        qkv_kernel,
        grid=(t // blk,),
        out_shape=(shape((t, d), BF), shape((t, n), BF), shape((d, n), BF), shape((d, d), BF)),
        in_specs=[rows_of(blk, d), row_vec(d), row_vec(d), whole(*g.shape), whole(1, n)],
        out_specs=(rows_of(blk, d), rows_of(blk, n), whole(d, n), whole(d, d)),
        compiler_params=params(),
        name="qkv_forward",
    )(tokens, shift, scale, g, bias)


def head_window(h, hd, width):
    a = pl.multiple_of(jnp.minimum((h * hd) // 128, (width - WINDOW) // 128) * 128, 128)
    lane = lax.broadcasted_iota(jnp.int32, (1, WINDOW), 1) + a
    return a, (lane >= h * hd) & (lane < h * hd + hd)


def attn_fwd_kernel(
    off_ref,
    gate_ref,
    qkv_ref,
    up_ref,
    down_ref,
    att_ref,
    gated_ref,
    lse_ref,
    g_up_ref,
    g_down_ref,
    lse_sc,
    *sems,
    heads,
    blk,
    planes,
):
    place = Place(planes)
    place.barrier()
    gathers = [Gather(place, up_ref, g_up_ref, *sems[:6]), Gather(place, down_ref, g_down_ref, *sems[6:])]
    parts = gathers[0].parts()
    for g in gathers:
        g.run("begin")
    groups = spread_out(
        [functools.partial(g.run, part) for part in parts[1:-1] for g in gathers], heads
    )
    t, d = att_ref.shape
    hd = d // heads
    nb = t // blk
    c = hd**-0.5 * LOG2E
    off = off_ref[0]
    lane128 = lax.broadcasted_iota(jnp.int32, (1, 128), 1)

    def body(h, carry):
        a, mask = head_window(h, hd, d)
        keys = qkv_ref[:, pl.ds(pl.multiple_of(d + a, 128), WINDOW)]
        values = qkv_ref[:, pl.ds(pl.multiple_of(2 * d + a, 128), WINDOW)]
        cols = pl.ds(a, WINDOW)
        for i in range(nb):
            rows = pl.ds(i * blk, blk)
            q = qkv_ref[rows, cols]
            q = jnp.where(mask, q, jnp.zeros_like(q))
            s = dg(q, keys, NT)
            parts = [s[:, j * blk : (j + 1) * blk] for j in range(nb)]
            own = jnp.max(parts[i], axis=1, keepdims=True) * c
            others = functools.reduce(jnp.maximum, [parts[j] for j in range(nb) if j != i])
            m = jnp.maximum(own, jnp.max(others, axis=1, keepdims=True) * c + off)
            m_off = m - off
            ps = [jnp.exp2(parts[j] * c - (m if j == i else m_off)) for j in range(nb)]
            total = jnp.sum(functools.reduce(jnp.add, ps), axis=1, keepdims=True)
            p = jnp.concatenate([x.astype(BF) for x in ps], axis=1)
            o = dg(p, values, NN) * (1.0 / total)
            og = (o * gate_ref[i, :, cols]).astype(BF)
            att_ref[rows, cols] = jnp.where(mask, o, att_ref[rows, cols])
            gated_ref[rows, cols] = jnp.where(mask, og, gated_ref[rows, cols])
            lse_sc[rows, :] = jnp.where(lane128 == h, m + jnp.log2(total), lse_sc[rows, :])
        run_at(h, groups)
        return carry

    lax.fori_loop(0, heads, body, 0)
    lse_ref[...] = lse_sc[...].T[:heads, :]
    for g in gathers:
        g.run("end")


def attn_fwd(off, gate_rows, qkv, up, down, heads, blk, planes):
    t = qkv.shape[0]
    d = qkv.shape[1] // 3
    gathered = shape((4, planes, 2) + up.shape, BF)
    return pl.pallas_call(
        functools.partial(attn_fwd_kernel, heads=heads, blk=blk, planes=planes),
        out_shape=(shape((t, d)), shape((t, d), BF), shape((heads, t)), gathered, gathered),
        in_specs=[SMEM_SPEC, VMEM_SPEC, VMEM_SPEC, ANY_SPEC, ANY_SPEC],
        out_specs=(VMEM_SPEC,) * 3 + (ANY_SPEC,) * 2,
        scratch_shapes=[pltpu.VMEM((t, 128), F32)] + Gather.scratch(planes) * 2,
        compiler_params=params(collective_id=2),
        name="attention_forward",
    )(off, gate_rows, qkv, up, down)


def attn_bwd_kernel(
    off_ref,
    qkv_ref,
    do_ref,
    lse_ref,
    delta_ref,
    up_ref,
    down_ref,
    dqkv_ref,
    g_up_ref,
    g_down_ref,
    kt_sc,
    dqt_sc,
    *rest,
    heads,
    blk,
    planes,
):
    place = Place(planes)
    place.barrier(True)
    half = len(rest) // 2
    steps = scatter_steps(
        [Scatter(place, up_ref, g_up_ref, *rest[:half]), Scatter(place, down_ref, g_down_ref, *rest[half:])]
    )
    steps[0]()
    groups = spread_out(steps[1:-1], heads)
    t, d = do_ref.shape
    hd = d // heads
    nb = t // blk
    scale = hd**-0.5
    c = scale * LOG2E
    off = off_ref[0]
    kt_sc[...] = qkv_ref[:, d : 2 * d].T

    def body(h, carry):
        a, mask = head_window(h, hd, d)
        cols = pl.ds(a, WINDOW)
        key_cols = pl.ds(pl.multiple_of(d + a, 128), WINDOW)
        value_cols = pl.ds(pl.multiple_of(2 * d + a, 128), WINDOW)
        keys = qkv_ref[:, key_cols]
        values = qkv_ref[:, value_cols]
        keys_t = kt_sc[cols, :]
        dk_sum = None
        dv_sum = None
        for i in range(nb):
            rows = pl.ds(i * blk, blk)
            span = slice(i * blk, (i + 1) * blk)
            q = qkv_ref[rows, cols]
            q = jnp.where(mask, q, jnp.zeros_like(q))
            do = do_ref[rows, cols]
            do = jnp.where(mask, do, jnp.zeros_like(do))
            lse = lse_ref[pl.ds(h, 1), span]
            delta = delta_ref[pl.ds(h, 1), span]
            s_t = dg(keys, q, NT)
            dp_t = dg(values, do, NT)
            ps = []
            ds = []
            for j in range(nb):
                part = slice(j * blk, (j + 1) * blk)
                p = jnp.exp2(s_t[part] * c - (lse if j == i else lse - off))
                ps.append(p.astype(BF))
                ds.append((p * (dp_t[part] - delta)).astype(BF))
            p = jnp.concatenate(ps, axis=0)
            grad_s = jnp.concatenate(ds, axis=0)
            dv = dg(p, do, NN)
            dk = dg(grad_s, q, NN)
            dv_sum = dv if dv_sum is None else dv_sum + dv
            dk_sum = dk if dk_sum is None else dk_sum + dk
            dqt_sc[:, span] = (dg(keys_t, grad_s, NN) * scale).astype(BF)
        dk = (dk_sum * scale).astype(BF)
        dqkv_ref[:, key_cols] = jnp.where(mask, dk, dqkv_ref[:, key_cols])
        dqkv_ref[:, value_cols] = jnp.where(mask, dv_sum.astype(BF), dqkv_ref[:, value_cols])
        dqkv_ref[:, cols] = jnp.where(mask, dqt_sc[...].T, dqkv_ref[:, cols])
        run_at(h, groups)
        return carry

    lax.fori_loop(0, heads, body, 0)
    steps[-1]()


def attn_bwd(off, qkv, do, lse, delta, up, down, heads, blk, planes):
    t, d = do.shape
    rows, cols = up.shape[3:]
    return pl.pallas_call(
        functools.partial(attn_bwd_kernel, heads=heads, blk=blk, planes=planes),
        out_shape=(shape((t, 3 * d), BF), shape((rows, cols)), shape((rows, cols))),
        in_specs=[SMEM_SPEC] + [VMEM_SPEC] * 4 + [ANY_SPEC] * 2,
        out_specs=(VMEM_SPEC,) * 3,
        scratch_shapes=[pltpu.VMEM((d, t), BF), pltpu.VMEM((WINDOW, t), BF)]
        + Scatter.scratch(planes, rows, cols) * 2,
        compiler_params=params(collective_id=3),
        name="attention_backward",
    )(off, qkv, do, lse, delta, up, down)


def middle_kernel(
    gated_ref,
    w_ref,
    bias_ref,
    tokens_ref,
    cot_ref,
    keep_ref,
    router_ref,
    gate1_ref,
    shift2_ref,
    scale2_ref,
    gate2_ref,
    attn_ref,
    after_ref,
    n2_ref,
    gm_ref,
    tg_ref,
):
    attn = dg(gated_ref[...], w_ref[...], NN) + bias_ref[...]
    attn_ref[...] = attn
    after = tokens_ref[...] + gate1_ref[0] * attn
    after_ref[...] = after
    normed, _ = ln_parts(after)
    y = normed * (1.0 + scale2_ref[0]) + shift2_ref[0]
    n2_ref[...] = y.astype(BF)
    token_gate = jax.nn.sigmoid(jnp.sum(y * router_ref[...], axis=1, keepdims=True))
    tg_ref[...] = token_gate
    gm_ref[...] = (cot_ref[...] * (gate2_ref[0] * (keep_ref[...] * token_gate))).astype(BF)


def middle_call(gated, w, bias, tokens, cot, keep, router, gate1, shift2, scale2, gate2, blk):
    t, d = tokens.shape
    r, v = rows_of(blk, d), row_vec(d)
    column = rows_of(blk, 1)
    return pl.pallas_call(
        middle_kernel,
        grid=(t // blk,),
        out_shape=(shape((t, d)), shape((t, d)), shape((t, d), BF), shape((t, d), BF), shape((t, 1))),
        in_specs=[r, whole(d, d), whole(1, d), r, r, column, whole(1, d), v, v, v, v],
        out_specs=(r, r, r, r, column),
        compiler_params=params(),
        name="middle_forward",
    )(gated, w, bias, tokens, cot, keep, router, gate1, shift2, scale2, gate2)


def mlp_kernel(
    n2_ref,
    gm_ref,
    g1_ref,
    g2_ref,
    b1_ref,
    cs_ref,
    mlp_ref,
    gn2_ref,
    p1_ref,
    p2_ref,
    gb1_ref,
    gch_ref,
    w1_s,
    w2_s,
    sc_s,
    gp_s,
    *,
    blk,
):
    t, d = n2_ref.shape
    nb = t // blk
    hidden = w1_s.shape[0]
    quarter = hidden // 8
    piece = d // 4

    @pl.when(pl.program_id(0) == 0)
    def _():
        mlp_ref[...] = jnp.zeros_like(mlp_ref)
        gn2_ref[...] = jnp.zeros_like(gn2_ref)

    def places():
        for c in range(2):
            for k in range(4):
                yield c, slice((4 * c + k) * quarter, (4 * c + k + 1) * quarter), k

    for c, rows, k in places():
        cols = slice(k * piece, (k + 1) * piece)
        for w, g in ((w1_s, g1_ref), (w2_s, g2_ref)):
            w[rows, :] = jnp.concatenate([g[n, 0, c, :quarter, cols] for n in range(4)], axis=1)
    w1 = w1_s[...]
    w2 = w2_s[...]
    grad_bias = None
    for i in range(nb):
        rows = slice(i * blk, (i + 1) * blk)
        pre = dg(n2_ref[rows, :], w1, NT) + b1_ref[0]
        grad_scaled = dg(gm_ref[rows, :], w2, NT)
        act, slope = gelu_parts(pre)
        gate = cs_ref[0, i : i + 1]
        scaled = (act * gate).astype(BF)
        grad_pre = (grad_scaled * gate * slope).astype(BF)
        gch_ref[0, i : i + 1] = col_sum(grad_scaled * act)
        part = col_sum(grad_pre.astype(F32))
        grad_bias = part if grad_bias is None else grad_bias + part
        sc_s[rows, :] = scaled
        gp_s[rows, :] = grad_pre
        mlp_ref[rows, :] += dg(scaled, w2, NN)
        gn2_ref[rows, :] += dg(grad_pre, w1, NN)
    gb1_ref[0] = grad_bias
    for left, right, out in ((gp_s, n2_ref, p1_ref), (sc_s, gm_ref, p2_ref)):
        grad = dg(left[...], right[...], TN).astype(BF)
        for c, rows, k in places():
            for n in range(4):
                out[n, 0, c, :quarter, k * piece : (k + 1) * piece] = grad[rows, n * piece : (n + 1) * piece]


def mlp_call(n2, gm, g1, g2, b1, gates, blk):
    t, d = n2.shape
    planes, rows = g1.shape[1], g1.shape[3]
    nb, ff = gates.shape
    hb = ff // planes
    g_spec = pl.BlockSpec((4, 1, 2, rows, d), lambda j: (0, j, 0, 0, 0))
    b_spec = pl.BlockSpec((1, 1, hb), lambda j: (j, 0, 0))
    c_spec = pl.BlockSpec((1, nb, hb), lambda j: (j, 0, 0))
    mlp, gn2, p1, p2, gb1, gch = pl.pallas_call(
        functools.partial(mlp_kernel, blk=blk),
        grid=(planes,),
        out_shape=(
            shape((t, d)),
            shape((t, d)),
            shape(g1.shape, BF),
            shape(g1.shape, BF),
            shape((planes, 1, hb)),
            shape((planes, nb, hb)),
        ),
        in_specs=[whole(t, d), whole(t, d), g_spec, g_spec, b_spec, c_spec],
        out_specs=(whole(t, d), whole(t, d), g_spec, g_spec, b_spec, c_spec),
        scratch_shapes=[pltpu.VMEM((hb, d), BF)] * 2 + [pltpu.VMEM((t, hb), BF)] * 2,
        compiler_params=params(),
        name="feed_forward",
    )(n2, gm, g1, g2, b1.reshape(planes, 1, hb), gates.reshape(nb, planes, hb).transpose(1, 0, 2))
    return mlp, gn2, p1, p2, gb1.reshape(ff), gch.transpose(1, 0, 2).reshape(nb, ff)


def middle_back_kernel(
    mlp_ref,
    gn2_ref,
    after_ref,
    attn_ref,
    cot_ref,
    gm_ref,
    gated_ref,
    att_ref,
    tg_ref,
    keep_ref,
    w_ref,
    b2_ref,
    router_ref,
    gate1_ref,
    shift2_ref,
    scale2_ref,
    gate2_ref,
    head_ref,
    out_ref,
    ga_ref,
    do_ref,
    delta_ref,
    gw_ref,
    mod_ref,
    sums_ref,
    *,
    heads,
):
    d = after_ref.shape[1]
    hd = d // heads
    first = pl.program_id(0) == 0
    after = after_ref[...]
    cot = cot_ref[...]
    gate2 = gate2_ref[0]
    tg = tg_ref[...]
    keep = keep_ref[...]
    normed, rstd = ln_parts(after)
    scale2 = scale2_ref[0]
    y = normed * (1.0 + scale2) + shift2_ref[0]
    mlp_out = mlp_ref[...] + b2_ref[...]
    open_gate = keep * tg
    out_ref[...] = after + (gate2 * open_gate) * mlp_out
    weighted = cot * mlp_out
    grad_tg = jnp.sum(weighted * gate2, axis=1, keepdims=True) * keep
    coef = grad_tg * tg * (1.0 - tg)
    gy = gn2_ref[...] + coef * router_ref[...]
    ga = cot + ln_back(gy, normed, rstd, scale2)
    ga_ref[...] = ga
    attn = attn_ref[...]
    g_attn = (ga * gate1_ref[0]).astype(BF)
    mod_ref[0] = jnp.concatenate(
        [col_sum(ga * attn), col_sum(gy), col_sum(gy * normed), col_sum(weighted * open_gate)], axis=0
    )
    sums = jnp.concatenate(
        [
            col_sum(coef * y),
            col_sum(g_attn.astype(F32)),
            col_sum(gm_ref[...].astype(F32)),
        ],
        axis=0,
    )
    g_gated = dg(g_attn, w_ref[...], NT)
    att = att_ref[...]
    mod_ref[1] = jnp.concatenate([col_sum(g_gated * att), jnp.zeros((3, d), F32)], axis=0)
    do = (g_gated * head_ref[0]).astype(BF)
    do_ref[...] = do
    lane = lax.broadcasted_iota(jnp.int32, (heads, d), 1)
    head = lax.broadcasted_iota(jnp.int32, (heads, d), 0) * hd
    pick = jnp.where((lane >= head) & (lane < head + hd), 1.0, 0.0)
    delta_ref[...] = lax.dot_general(
        pick, do.astype(F32) * att, NT, precision=HIGHEST, preferred_element_type=F32
    )
    gw = dg(gated_ref[...], g_attn, TN)

    @pl.when(first)
    def _():
        sums_ref[...] = sums
        gw_ref[...] = gw

    @pl.when(jnp.logical_not(first))
    def _():
        sums_ref[...] += sums
        gw_ref[...] += gw


def middle_back_call(
    mlp, gn2, after, attn, cot, gm, gated, att, tg, keep, w, b2, router, gate1, shift2, scale2, gate2, head_rows, heads, blk
):
    t, d = after.shape
    nb = t // blk
    r, v, column = rows_of(blk, d), row_vec(d), rows_of(blk, 1)
    return pl.pallas_call(
        functools.partial(middle_back_kernel, heads=heads),
        grid=(nb,),
        out_shape=(
            shape((t, d)),
            shape((t, d)),
            shape((t, d), BF),
            shape((heads, t)),
            shape((d, d)),
            shape((nb * 2, 4, d)),
            shape((3, d)),
        ),
        in_specs=[r] * 8 + [column, column, whole(d, d), whole(1, d), whole(1, d), v, v, v, v, v],
        out_specs=(
            r,
            r,
            r,
            pl.BlockSpec((heads, blk), lambda i: (0, i)),
            whole(d, d),
            pl.BlockSpec((2, 4, d), lambda i: (i, 0, 0)),
            whole(3, d),
        ),
        compiler_params=params(),
        name="middle_backward",
    )(mlp, gn2, after, attn, cot, gm, gated, att, tg, keep, w, b2, router, gate1, shift2, scale2, gate2, head_rows)


def qkv_weight_kernel(n1_ref, q_ref, k_ref, v_ref, gp_ref, out_ref, bias_ref, n1t):
    @pl.when(pl.program_id(0) == 0)
    def _():
        n1t[...] = n1_ref[...].T

    width = q_ref.shape[1]
    devices = out_ref.shape[1]
    r = n1_ref.shape[1] // devices
    dqkv = jnp.concatenate([q_ref[...], k_ref[...], v_ref[...]], axis=1)
    grad = dg(n1t[...], dqkv, NN).astype(BF)
    bias_ref[0] = col_sum(dqkv.astype(F32))
    for i in range(devices):
        rows = slice(i * r, (i + 1) * r)
        for b in range(3):
            out_ref[0, i, b * r : (b + 1) * r, :] = grad[rows, b * width : (b + 1) * width]
        out_ref[0, i, 3 * r : 4 * r, :] = gp_ref[rows, :].astype(BF)


def qkv_weight_call(n1, dqkv, g_proj, devices, cuts):
    t, d = n1.shape
    width = d // cuts
    rows = up_to(4 * d // devices, 16)
    third = [pl.BlockSpec((t, width), lambda j, b=b: (0, b * cuts + j)) for b in range(3)]
    parts, bias = pl.pallas_call(
        qkv_weight_kernel,
        grid=(cuts,),
        out_shape=(shape((cuts, devices, rows, width), BF), shape((cuts, 1, 3 * width))),
        in_specs=[whole(t, d)] + third + [pl.BlockSpec((d, width), lambda j: (0, j))],
        out_specs=(
            pl.BlockSpec((1, devices, rows, width), lambda j: (j, 0, 0, 0)),
            pl.BlockSpec((1, 1, 3 * width), lambda j: (j, 0, 0)),
        ),
        scratch_shapes=[pltpu.VMEM((d, t), BF)],
        compiler_params=params(),
        name="qkv_weight_gradient",
    )(n1, dqkv, dqkv, dqkv, g_proj)
    return parts, bias.reshape(cuts, 3, width).transpose(1, 0, 2).reshape(3, d)


def qkv_back_kernel(dqkv_ref, w_ref, tokens_ref, ga_ref, scale_ref, out_ref, mod_ref):
    gy = dg(dqkv_ref[...], w_ref[...], NT)
    normed, rstd = ln_parts(tokens_ref[...])
    out_ref[...] = ga_ref[...] + ln_back(gy, normed, rstd, scale_ref[0])
    mod_ref[0] = jnp.concatenate([col_sum(gy), col_sum(gy * normed)], axis=0)


def qkv_back_call(dqkv, w, tokens, ga, scale, blk):
    t, d = tokens.shape
    n = dqkv.shape[1]
    r = rows_of(blk, d)
    return pl.pallas_call(
        qkv_back_kernel,
        grid=(t // blk,),
        out_shape=(shape((t, d)), shape((t // blk, 2, d))),
        in_specs=[rows_of(blk, n), whole(d, n), r, r, row_vec(d)],
        out_specs=(r, pl.BlockSpec((1, 2, d), lambda i: (i, 0, 0))),
        compiler_params=params(),
        name="qkv_backward",
    )(dqkv, w, tokens, ga, scale)


def final_kernel(part_ref, sums_ref, mods_ref, out_ref, all_sums_ref, all_mods_ref, *rest, planes, cuts):
    place = Place(planes)
    place.barrier(True)
    width = out_ref.shape[1] // cuts
    sums = Gather(place, sums_ref, all_sums_ref, *rest[:6])
    mods = Gather(place, mods_ref, all_mods_ref, *rest[6:12])
    rest = rest[12:]
    each = len(rest) // cuts
    scatters = [
        Scatter(
            place,
            part_ref.at[m],
            out_ref.at[:, pl.ds(m * width, width)],
            *rest[each * m : each * (m + 1)],
        )
        for m in range(cuts)
    ]
    steps = scatter_steps(scatters)
    parts = sums.parts()
    steps[0]()
    sums.run("begin")
    mods.run("begin")
    small = [functools.partial(g.run, part) for part in parts[1:-1] for g in (sums, mods)]
    for step, group in zip(steps[1:-1], spread_out(small, len(steps) - 2)):
        step()
        for part in group:
            part()
    steps[-1]()
    sums.run("end")
    mods.run("end")


def final_call(parts, sums, mods, planes):
    cuts, _, rows, width = parts.shape
    spread = (4, planes, 2)
    return pl.pallas_call(
        functools.partial(final_kernel, planes=planes, cuts=cuts),
        out_shape=(
            shape((rows, cuts * width)),
            shape(spread + sums.shape),
            shape(spread + mods.shape, BF),
        ),
        in_specs=[ANY_SPEC] * 3,
        out_specs=(VMEM_SPEC, ANY_SPEC, ANY_SPEC),
        scratch_shapes=Gather.scratch(planes) * 2 + Scatter.scratch(planes, rows, width) * cuts,
        compiler_params=params(collective_id=4),
        name="attention_weight_sums",
    )(parts.reshape((cuts,) + spread + (rows, width)), sums, mods)


def on_device(
    planes,
    tokens,
    conditioning,
    row_items,
    head_mask,
    chan_mask,
    skip_mask,
    ada_weight,
    ada_bias,
    qkv_weight,
    query_bias,
    value_bias,
    proj_weight,
    proj_bias,
    fc1_weight,
    fc1_bias,
    fc2_weight,
    fc2_bias,
    head_router,
    head_router_bias,
    chan_router,
    chan_router_bias,
    token_router,
    cotangent,
):
    t, d = tokens.shape
    slots = conditioning.shape[0]
    heads = head_mask.shape[1]
    groups = chan_mask.shape[1]
    hidden = fc1_bias.shape[0]
    hd = d // heads
    unit = hidden // groups
    blk = t // slots
    single = row_items[0] == 1
    off = jnp.where(single, 0.0, MASKED).astype(F32).reshape(1)

    def per_block(table):
        return jnp.where(single, table[:1], table)

    def per_slot(blocks):
        total = jnp.sum(blocks, axis=0, keepdims=True)
        first = (jnp.arange(slots) == 0).reshape((slots,) + (1,) * (blocks.ndim - 1))
        return jnp.where(single, jnp.where(first, total, 0.0), blocks)

    devices = 8 * planes
    me = lax.axis_index("narrow") * (2 * planes) + lax.axis_index("wide")

    def pack_rows(*blocks):
        return pad_rows(jnp.concatenate(blocks, axis=0))

    def pack_piece(weight):
        rows, cols = weight.shape
        return pad_rows(weight.reshape(4, rows // 4, cols).transpose(1, 0, 2).reshape(rows // 4, d))

    def unpack_piece(piece, rows):
        cols = d // 4
        return piece[: rows // 4].reshape(rows // 4, 4, cols).transpose(1, 0, 2).reshape(rows, cols)

    silu_cond = jax.nn.silu(conditioning.astype(F32)).astype(BF)
    shard = pack_rows(qkv_weight[:, :d], qkv_weight[:, d : 2 * d], qkv_weight[:, 2 * d :], proj_weight)
    g_attn, conds, mod_columns = prologue_call(
        shard, pad_rows(silu_cond), ada_weight, ada_bias.astype(F32)[None], planes, slots
    )
    every_cond = conds.reshape((devices,) + conds.shape[3:])[:, :slots].reshape(devices * slots, d)
    mod_width = ada_bias.shape[0]
    mod_columns = mod_columns.reshape((devices,) + mod_columns.shape[3:])
    mod_columns = lax.dynamic_slice_in_dim(mod_columns, me * slots, slots, axis=1)
    modulation = mod_columns[:, :, :mod_width].transpose(1, 0, 2).reshape(slots, devices * mod_width)
    mod_rows = per_block(modulation.astype(F32)).reshape(slots, 6, 1, d)
    shift1, scale1, gate1, shift2, scale2, gate2 = [mod_rows[:, k] for k in range(6)]
    cond_float = silu_cond.astype(F32)

    def router(weight, bias, mask):
        gate = jax.nn.sigmoid(
            jnp.dot(cond_float, weight.astype(F32), precision=HIGHEST) + bias.astype(F32)
        )
        mask = mask.astype(F32)
        return mask * gate, mask * gate * (1.0 - gate)

    head_gate, head_slope = router(head_router, head_router_bias, head_mask)
    chan_gate, chan_slope = router(chan_router, chan_router_bias, chan_mask)
    head_rows = jnp.repeat(per_block(head_gate), hd, axis=1)[:, None, :]
    chan_rows = jnp.repeat(per_block(chan_gate), unit, axis=1)
    keep = (1.0 - skip_mask.astype(F32))[:, None]

    qkv_bias = jnp.concatenate([query_bias, jnp.zeros_like(query_bias), value_bias])
    n1, qkv, full_qkv, full_proj = qkv_call(
        tokens,
        shift1,
        scale1,
        g_attn.reshape((devices,) + shard.shape),
        qkv_bias.astype(F32)[None],
        blk,
    )
    att, gated, lse, g_up, g_down = attn_fwd(
        off, head_rows, qkv, pack_piece(fc1_weight), pack_piece(fc2_weight), heads, blk, planes
    )
    router_row = token_router.astype(F32)[None]
    attn, after, n2, gm, tg = middle_call(
        gated,
        full_proj,
        proj_bias.astype(F32)[None],
        tokens,
        cotangent,
        keep,
        router_row,
        gate1,
        shift2,
        scale2,
        gate2,
        blk,
    )
    mlp, gn2, p_up, p_down, gb1, gch = mlp_call(
        n2, gm, g_up, g_down, fc1_bias.astype(F32), chan_rows, blk
    )
    output, ga, do, delta, g_proj, mods, sums = middle_back_call(
        mlp,
        gn2,
        after,
        attn,
        cotangent,
        gm,
        gated,
        att,
        tg,
        keep,
        full_proj,
        fc2_bias.astype(F32)[None],
        router_row,
        gate1,
        shift2,
        scale2,
        gate2,
        head_rows,
        heads,
        blk,
    )
    mods = mods.reshape(slots, 8, d)
    dqkv, g_up, g_down = attn_bwd(off, qkv, do, lse, delta, p_up, p_down, heads, blk, planes)
    parts, qkv_sums = qkv_weight_call(n1, dqkv, g_proj, devices, 3)
    grad_tokens, mods1 = qkv_back_call(dqkv, full_qkv, tokens, ga, scale1, blk)
    block_mods = jnp.concatenate(
        [mods1[:, 0], mods1[:, 1], mods[:, 0], mods[:, 1], mods[:, 2], mods[:, 3]], axis=1
    )
    grad_slot_mod = per_slot(block_mods).astype(BF)
    g_head = per_slot(jnp.sum(mods[:, 4].reshape(slots, heads, hd), axis=2)) * head_slope
    g_chan = per_slot(jnp.sum(gch.reshape(slots, groups, unit), axis=2)) * chan_slope
    logits = jnp.concatenate([g_head, g_chan], axis=1)
    vector = jnp.concatenate(
        [qkv_sums[0], qkv_sums[2], sums[1], gb1, sums[2], sums[0], logits.reshape(-1)]
    )
    length = vector.shape[0]
    vector = jnp.pad(vector, (0, up_to(length, 1024) - length)).reshape(-1, 128)
    g_attn, all_sums, all_mods = final_call(
        parts, vector, pad_rows(grad_slot_mod.reshape(-1, 128)), planes
    )
    g_attn = g_attn[: 4 * (d // devices)].reshape(4, d // devices, d)
    all_mods = all_mods.reshape(devices, -1)[:, : slots * 6 * d].reshape(devices * slots, 6 * d)
    grad_mod_columns = lax.dynamic_slice_in_dim(all_mods, me * mod_width, mod_width, axis=1)
    grad_ada_weight = dg(every_cond, grad_mod_columns, TN)
    grad_ada_bias = jnp.sum(grad_mod_columns.astype(F32), axis=0)
    all_sums = all_sums.reshape(devices, -1)
    logits = all_sums[:, length - logits.size : length].reshape(devices * slots, heads + groups)
    router_grads = lax.dot_general(
        every_cond.astype(F32), logits, TN, precision=HIGHEST, preferred_element_type=F32
    )
    logit_sums = jnp.sum(logits, axis=0)
    small = jnp.sum(all_sums[:, : length - slots * (heads + groups)], axis=0)
    ends = [d, 2 * d, 3 * d, 3 * d + hidden, 4 * d + hidden]
    g_query, g_value, g_proj_bias, g_b1, g_b2, g_router = jnp.split(small, ends)
    return (
        output,
        grad_tokens,
        grad_ada_weight,
        grad_ada_bias,
        g_attn[:3].transpose(1, 0, 2).reshape(d // devices, 3 * d),
        g_query,
        g_value,
        g_attn[3],
        g_proj_bias,
        unpack_piece(g_up, fc1_weight.shape[0]),
        g_b1,
        unpack_piece(g_down, fc2_weight.shape[0]),
        g_b2,
        router_grads[:, :heads],
        logit_sums[:heads],
        router_grads[:, heads:],
        logit_sums[heads:],
        g_router,
    )


def solution(mesh):
    planes = mesh.shape["wide"] // 2
    return jax.shard_map(
        functools.partial(on_device, planes),
        mesh=mesh,
        in_specs=(
            P(("narrow", "wide"), None),
            P(("narrow", "wide"), None),
            P(("narrow", "wide")),
            P(("narrow", "wide"), None),
            P(("narrow", "wide"), None),
            P(("narrow", "wide")),
            P(None, ("narrow", "wide")),
            P(("narrow", "wide")),
            P(("narrow", "wide"), None),
            P(),
            P(),
            P(("narrow", "wide"), None),
            P(),
            P("wide", "narrow"),
            P(),
            P("wide", "narrow"),
            P(),
            P(),
            P(),
            P(),
            P(),
            P(),
            P(("narrow", "wide"), None),
        ),
        out_specs=(
            P(("narrow", "wide"), None),
            P(("narrow", "wide"), None),
            P(None, ("narrow", "wide")),
            P(("narrow", "wide")),
            P(("narrow", "wide"), None),
            P(),
            P(),
            P(("narrow", "wide"), None),
            P(),
            P("wide", "narrow"),
            P(),
            P("wide", "narrow"),
            P(),
            P(),
            P(),
            P(),
            P(),
            P(),
        ),
        check_vma=False,
    )
```

```python
import functools

import jax
import jax.numpy as jnp
from jax import lax
from jax.experimental import pallas as pl
from jax.experimental.pallas import tpu as pltpu
from jax.sharding import PartitionSpec as P

HIGHEST = lax.Precision.HIGHEST
F32 = jnp.float32
BF = jnp.bfloat16
EPSILON = 1e-06
MASKED = -1e30
LOG2E = 1.4426950408889634
WINDOW = 256
NN = (((1,), (0,)), ((), ()))
NT = (((1,), (1,)), ((), ()))
TN = (((0,), (0,)), ((), ()))
VMEM_SPEC = pl.BlockSpec(memory_space=pltpu.VMEM)
ANY_SPEC = pl.BlockSpec(memory_space=pl.ANY)
MESH = pl.DeviceIdType.MESH
SMEM_SPEC = pl.BlockSpec(memory_space=pltpu.SMEM)


def dg(a, b, dims):
    return lax.dot_general(a, b, dims, preferred_element_type=F32)


def params(mib=60, collective_id=None):
    if collective_id is None:
        return pltpu.CompilerParams(vmem_limit_bytes=mib << 20)
    return pltpu.CompilerParams(
        vmem_limit_bytes=mib << 20, collective_id=collective_id, has_side_effects=True
    )


def up_to(count, multiple):
    return -(-count // multiple) * multiple


def pad_rows(x):
    return jnp.pad(x, ((0, up_to(x.shape[0], 16) - x.shape[0]), (0, 0)))


def spread_out(steps, count):
    groups = [[] for _ in range(count)]
    for i, step in enumerate(steps):
        groups[i * count // len(steps)].append(step)
    return groups


def run_at(index, groups):
    for i, group in enumerate(groups):
        if group:

            @pl.when(index == i)
            def _(group=group):
                for step in group:
                    step()


def shape(dims, dtype=F32):
    return jax.ShapeDtypeStruct(dims, dtype)


def whole(*dims):
    return pl.BlockSpec(dims, lambda i: (0,) * len(dims), pipeline_mode=pl.Buffered(1))


def rows_of(block, width):
    return pl.BlockSpec((block, width), lambda i: (i, 0))


def row_vec(width):
    return pl.BlockSpec((1, 1, width), lambda i: (i, 0, 0))


def ln_parts(x):
    centered = x - jnp.mean(x, axis=-1, keepdims=True)
    rstd = lax.rsqrt(jnp.mean(centered * centered, axis=-1, keepdims=True) + EPSILON)
    return centered * rstd, rstd


def ln_back(grad_y, normed, rstd, scale):
    m = grad_y * (1.0 + scale)
    mean_m = jnp.mean(m, axis=-1, keepdims=True)
    mean_mn = jnp.mean(m * normed, axis=-1, keepdims=True)
    return (m - mean_m - normed * mean_mn) * rstd


def col_sum(x):
    return jnp.sum(x, axis=0, keepdims=True)


def gelu_parts(x):
    k0 = 0.7978845608028654
    k1 = 0.044715
    x2 = x * x
    t = jnp.tanh(k0 * x * (1.0 + k1 * x2))
    half = 0.5 * (1.0 + t)
    return x * half, half + 0.5 * x * (1.0 - t * t) * (k0 * (1.0 + 3.0 * k1 * x2))


class Place:
    def __init__(self, planes):
        self.planes = planes
        self.n = lax.axis_index("narrow")
        w = lax.axis_index("wide")
        self.z = w // 2
        self.c = w % 2
        self.xn = self.n + 1 - 2 * (self.n % 2)
        self.yn = self.n + 2 - 4 * (self.n // 2)
        self.dn = 3 - self.n

    def dev(self, n, z, c):
        return (n, z * 2 + c)

    def barrier(self, every_plane=False):
        sem = pltpu.get_barrier_semaphore()

        def greet(n, z, c):
            pl.semaphore_signal(sem, inc=1, device_id=self.dev(n, z, c), device_id_type=MESH)

        greet(self.xn, self.z, self.c)
        greet(self.yn, self.z, self.c)
        greet(self.n, self.z, 1 - self.c)
        if every_plane:
            for k in range(1, self.planes):
                greet(self.n, lax.rem(self.z + k, self.planes), self.c)
            pl.semaphore_wait(sem, self.planes + 2)
            return
        for step in (-1, 1):

            @pl.when(self.has(step))
            def _(step=step):
                greet(self.n, self.z + step, self.c)

        ends = jnp.where(self.z > 0, 1, 0) + jnp.where(self.z < self.planes - 1, 1, 0)
        pl.semaphore_wait(sem, 3 + ends)

    def has(self, step):
        return self.z + step >= 0 if step < 0 else self.z + step < self.planes


def remote(src, dst, sems, idx, device):
    return pltpu.make_async_remote_copy(
        src_ref=src,
        dst_ref=dst,
        send_sem=sems.at[0, idx],
        recv_sem=sems.at[1, idx],
        device_id=device,
        device_id_type=MESH,
    )


class Gather:
    def __init__(self, place, src, out, own, zs, xs, ys, ds, cs):
        self.p, self.src, self.out = place, src, out
        self.own, self.zs, self.xs, self.ys, self.ds, self.cs = own, zs, xs, ys, ds, cs
        self.steps = [0]
        for k in range(1, place.planes):
            self.steps += [-k, k]

    def index(self, k):
        return k + self.p.planes - 1

    def at(self, n, k, c=None):
        p = self.p
        return self.out.at[n, p.z + k, p.c if c is None else c]

    def mine(self, k):
        return self.src if k == 0 else self.at(self.p.n, k)

    def via(self, k):
        p = self.p
        return (p.xn, p.yn) if k % 2 == 0 else (p.yn, p.xn)

    def copy(self, kind, k):
        p = self.p
        i = self.index(k)
        if kind == "x":
            return remote(self.mine(k), self.at(p.n, k), self.xs, i, p.dev(p.xn, p.z, p.c))
        if kind == "y":
            return remote(self.mine(k), self.at(p.n, k), self.ys, i, p.dev(p.yn, p.z, p.c))
        if kind == "d":
            via, to = self.via(k)
            return remote(self.at(via, k), self.at(via, k), self.ds, i, p.dev(to, p.z, p.c))
        if kind == "up" or kind == "down":
            step = 1 if kind == "up" else -1
            j = self.index(k - step)
            return remote(self.mine(k), self.at(p.n, k), self.zs, j, p.dev(p.n, p.z + step, p.c))
        j = ("c", "C", "d2", "D").index(kind)
        n = (p.n, p.xn, p.yn, p.dn)[j]
        shard = self.mine(k) if j == 0 else self.at(n, k)
        slot = j * (2 * p.planes - 1) + i
        return remote(shard, self.at(n, k), self.cs, slot, p.dev(p.n, p.z, 1 - p.c))

    def arrived(self, n, k, sems, idx, c=None):
        p = self.p
        dst = self.at(n, k, c)
        remote(dst, dst, sems, idx, p.dev(p.xn, p.z, p.c)).wait_recv()

    def run(self, part):
        if part == "begin":
            pltpu.make_async_copy(self.src, self.at(self.p.n, 0), self.own).start()
            self.spread(0)
        elif part == "end":
            pltpu.make_async_copy(self.src, self.at(self.p.n, 0), self.own).wait()
            for k in self.steps:
                self.when(self.p.has(k), functools.partial(self.finish, k))
        else:
            kind, k = part
            self.when(self.p.has(k), functools.partial(getattr(self, kind), k))

    def when(self, cond, do):
        pl.when(cond)(do)

    def onward(self, k, act):
        p = self.p
        if k <= 0:
            self.when(p.has(1), lambda: act(self.copy("up", k)))
        if k >= 0:
            self.when(p.has(-1), lambda: act(self.copy("down", k)))

    def spread(self, k):
        self.onward(k, lambda copy: copy.start())
        self.copy("x", k).start()
        self.copy("y", k).start()
        self.copy("c", k).start()

    def plane(self, k):
        self.arrived(self.p.n, k, self.zs, self.index(k))
        self.spread(k)

    def near(self, k):
        p = self.p
        self.arrived(p.xn, k, self.xs, self.index(k))
        if k % 2 == 0:
            self.copy("d", k).start()
        self.copy("C", k).start()
        self.arrived(p.yn, k, self.ys, self.index(k))
        if k % 2 == 1:
            self.copy("d", k).start()
        self.copy("d2", k).start()

    def far(self, k):
        self.arrived(self.p.dn, k, self.ds, self.index(k))
        self.copy("D", k).start()

    def finish(self, k):
        p = self.p
        for j, n in enumerate((p.n, p.xn, p.yn, p.dn)):
            self.arrived(n, k, self.cs, j * (2 * p.planes - 1) + self.index(k), 1 - p.c)
        for kind in ("x", "y", "d", "c", "C", "d2", "D"):
            self.copy(kind, k).wait_send()
        self.onward(k, lambda copy: copy.wait_send())

    def parts(self):
        found = ["begin"]
        rounds = [[0]] + [[-k, k] for k in range(1, self.p.planes)]
        for r in range(len(rounds) + 2):
            if 0 < r < len(rounds):
                found += [("plane", k) for k in rounds[r]]
            if 1 <= r <= len(rounds):
                found += [("near", k) for k in rounds[r - 1]]
            if 2 <= r:
                found += [("far", k) for k in rounds[r - 2]]
        return found + ["end"]

    @staticmethod
    def scratch(planes):
        dma = pltpu.SemaphoreType.DMA
        span = 2 * planes - 1
        return [dma(())] + [dma((2, span))] * 4 + [dma((2, 4 * span))]


class Scatter:
    def __init__(self, place, turn, js, source, own, r1, r2, r3, r4, own_sem, s1, s2, s3, s4):
        self.p, self.turn, self.js, self.source = place, turn, js, source
        self.own, self.r1, self.r2, self.r3, self.r4 = own, r1, r2, r3, r4
        self.own_sem, self.s1, self.s2, self.s3, self.s4 = own_sem, s1, s2, s3, s4

    def owner(self, j):
        return lax.rem(self.p.z + 1 + j, self.p.planes)

    def moves_on(self, j):
        return j + 1 < self.p.planes

    def load(self, j):
        slot = self.js.index(j) % 2
        return pltpu.make_async_copy(
            self.source(j, self.p.c), self.own.at[slot], self.own_sem.at[slot]
        )

    def x_first(self, j):
        return (self.js.index(j) + self.turn) % 2 == 0

    def sides(self, j):
        p = self.p
        return (p.xn, p.yn) if self.x_first(j) else (p.yn, p.xn)

    def copies(self, stage, j):
        p = self.p
        i = self.js.index(j)
        side, other = self.sides(j)
        if stage == 1:
            to = p.dev(p.n, p.z, 1 - p.c)
            return [remote(self.source(j, 1 - p.c), self.r1.at[i], self.s1, i, to)]
        if stage == 2:
            to = p.dev(side, p.z, p.c)
            return [
                remote(self.r1.at[i, side], self.r2.at[i, 0], self.s2, 2 * i, to),
                remote(self.r1.at[i, p.dn], self.r2.at[i, 1], self.s2, 2 * i + 1, to),
            ]
        if stage == 3:
            to = p.dev(other, p.z, p.c)
            return [remote(self.r1.at[i, other], self.r3.at[i], self.s3, i, to)]
        to = p.dev(p.n, self.owner(j), p.c)
        return [remote(self.r1.at[i, p.n], self.r4.at[i], self.s4, i, to)]

    def issue(self, stage, j):
        for copy in self.copies(stage, j):
            copy.start()

    def sent(self, stage, j):
        for copy in self.copies(stage, j):
            copy.wait_send()

    def begin(self):
        if self.own is not None:
            self.load(self.js[0]).start()

    def take(self, stage, j):
        p = self.p
        i = self.js.index(j)
        for copy in self.copies(stage, j):
            copy.wait_recv()
        side, other = self.sides(j)

        def add(n, value):
            self.r1[i, n] = (self.r1[i, n].astype(F32) + value.astype(F32)).astype(BF)

        if stage == 1:
            if self.own is None:
                mine = self.source(j, p.c)
            else:
                self.load(j).wait()
                if i + 1 < len(self.js):
                    self.load(self.js[i + 1]).start()
                mine = self.own.at[i % 2]
            for n in range(4):
                add(n, mine[n])
        elif stage == 2:
            add(p.n, self.r2[i, 0])
            add(other, self.r2[i, 1])
        else:
            add(p.n, self.r3[i])
            if self.moves_on(j):
                self.issue(4, j)

    def total(self, stages=(1, 2, 3, 4)):
        found = None
        for i, j in enumerate(self.js):
            if self.moves_on(j):
                self.copies(4, j)[0].wait_recv()
                part = self.r4[i].astype(F32)
            else:
                part = self.r1[i, self.p.n].astype(F32)
            found = part if found is None else found + part
        for j in self.js:
            for stage in stages:
                if stage < 4 or self.moves_on(j):
                    self.sent(stage, j)
        return found

    @staticmethod
    def scratch(count, rows, cols, load=True):
        dma = pltpu.SemaphoreType.DMA
        own = [pltpu.VMEM((2, 4, rows, cols), BF)] if load else []
        return own + [
            pltpu.VMEM((count, 4, rows, cols), BF),
            pltpu.VMEM((count, 2, rows, cols), BF),
            pltpu.VMEM((count, rows, cols), BF),
            pltpu.VMEM((count, rows, cols), BF),
            dma((2,)),
            dma((2, count)),
            dma((2, 2 * count)),
            dma((2, count)),
            dma((2, count)),
        ]


def scatter_steps(scatters, window=2):
    js = scatters[0].js
    units = range(len(scatters))
    queue = [(u, j) for j in js for u in units]
    x_items, y_items = [], []
    for i in range(0, len(js), 2):
        pair = [(u, j) for j in js[i : i + 2] for u in units]
        for stage in (2, 3):
            for u, j in pair:
                first = scatters[u].x_first(j)
                (x_items if first == (stage == 2) else y_items).append((stage, u, j))
    sent = []
    done = []

    def begin():
        for s in scatters:
            s.begin()
        for u, j in queue[:window]:
            scatters[u].issue(1, j)
            sent.append((u, j))

    def ready(stage, u, j):
        if stage == 2:
            while (u, j) not in done:
                v, i = queue[len(done)]
                scatters[v].take(1, i)
                done.append((v, i))
                if len(sent) < len(queue):
                    v, i = queue[len(sent)]
                    scatters[v].issue(1, i)
                    sent.append((v, i))

    def step(i):
        for items in (x_items, y_items):
            if window <= i < len(items) + window:
                stage, u, j = items[i - window]
                scatters[u].take(stage, j)
        for items in (x_items, y_items):
            if i < len(items):
                stage, u, j = items[i]
                ready(stage, u, j)
                scatters[u].issue(stage, j)

    count = max(len(x_items), len(y_items)) + window
    return [begin] + [functools.partial(step, i) for i in range(count)]


class Exchange:
    def __init__(self, place, src, out, sems, same):
        self.p, self.src, self.out, self.sems, self.same = place, src, out, sems, same
        self.wide = 2 * place.planes
        self.total = 4 * self.wide
        self.me = place.n * self.wide + place.z * 2 + place.c

    def device(self, i):
        other = lax.rem(self.me + i, self.total)
        return other // self.wide, lax.rem(other, self.wide)

    def greet(self):
        sem = pltpu.get_barrier_semaphore()

        def signal(i, carry):
            pl.semaphore_signal(sem, inc=1, device_id=self.device(i), device_id_type=MESH)
            return carry

        lax.fori_loop(1, self.total, signal, 0)
        pl.semaphore_wait(sem, self.total - 1)

    def copy(self, i):
        other = lax.rem(self.me + i, self.total)
        src = self.src if self.same else self.src.at[other]
        return remote(src, self.out.at[self.me], self.sems, i, self.device(i))

    def each(self, do):
        def body(i, carry):
            do(i)
            return carry

        lax.fori_loop(1, self.total, body, 0)

    def start(self):
        self.each(lambda i: self.copy(i).start())
        self.out[self.me] = self.src[...] if self.same else self.src[self.me]

    def arrive(self):
        def wait(i):
            dst = self.out.at[lax.rem(self.me + self.total - i, self.total)]
            remote(dst, dst, self.sems, i, self.device(i)).wait_recv()

        self.each(wait)

    def end(self):
        self.each(lambda i: self.copy(i).wait_send())

    @staticmethod
    def scratch(planes):
        return pltpu.SemaphoreType.DMA((2, 8 * planes))


class Stream:
    def __init__(self, slots, sems, out):
        self.slots, self.sems, self.out = slots, sems, out
        self.count = 0

    def copy(self, i):
        rows = self.slots.shape[1]
        return pltpu.make_async_copy(
            self.slots.at[i % 2], self.out.at[pl.ds(i * rows, rows)], self.sems.at[i % 2]
        )

    def put(self, value):
        i = self.count
        if i >= 2:
            self.copy(i - 2).wait()
        self.slots[i % 2] = value
        self.copy(i).start()
        self.count = i + 1

    def end(self):
        for i in range(max(self.count - 2, 0), self.count):
            self.copy(i).wait()

    @staticmethod
    def scratch(rows, width, dtype):
        return [pltpu.VMEM((2, rows, width), dtype), pltpu.SemaphoreType.DMA((2,))]


def prologue_kernel(
    shard_ref, cond_ref, ada_ref, ada_bias_ref, g_ref, conds_ref, mods_ref, mod_local, cond_sems, mod_sems, *sems, planes, slots
):
    place = Place(planes)
    weights = Gather(place, shard_ref, g_ref, *sems)
    conds = Exchange(place, cond_ref, conds_ref, cond_sems, True)
    mods = Exchange(place, mod_local, mods_ref, mod_sems, False)
    conds.greet()
    weights.run("begin")
    conds.start()
    mod_local[...] = jnp.zeros_like(mod_local)
    parts = weights.parts()
    for part in parts[1:4]:
        weights.run(part)
    conds.arrive()
    devices, rows, lanes = conds_ref.shape
    d, width = ada_ref.shape
    every = conds_ref[...].reshape(devices * rows, lanes)
    columns = ada_bias_ref[...]
    for j in range(d // lanes):
        piece = dg(every, ada_ref[j * lanes : (j + 1) * lanes, :], NN).reshape(devices, rows, width)
        columns = columns + piece[:, slots * j : slots * (j + 1)]
    mod_local[:, :slots, :width] = columns.astype(BF)
    mods.start()
    for part in parts[4:-1]:
        weights.run(part)
    mods.arrive()
    conds.end()
    mods.end()
    weights.run("end")


def prologue_call(shard, cond, ada, ada_bias, planes, slots):
    devices = 8 * planes
    lanes = up_to(ada.shape[1], 128)
    return pl.pallas_call(
        functools.partial(prologue_kernel, planes=planes, slots=slots),
        out_shape=(
            shape((4, planes, 2) + shard.shape, BF),
            shape((devices,) + cond.shape, BF),
            shape((devices, 16, lanes), BF),
        ),
        in_specs=[ANY_SPEC, VMEM_SPEC, VMEM_SPEC, VMEM_SPEC],
        out_specs=(ANY_SPEC, VMEM_SPEC, VMEM_SPEC),
        scratch_shapes=[pltpu.VMEM((devices, 16, lanes), BF)]
        + [Exchange.scratch(planes)] * 2
        + Gather.scratch(planes),
        compiler_params=params(collective_id=1),
        name="weights_and_modulation",
    )(shard, cond, ada, ada_bias)


def head_window(h, hd, width):
    a = pl.multiple_of(jnp.minimum((h * hd) // 128, (width - WINDOW) // 128) * 128, 128)
    lane = lax.broadcasted_iota(jnp.int32, (1, WINDOW), 1) + a
    return a, (lane >= h * hd) & (lane < h * hd + hd)


QUERY_BIAS, VALUE_BIAS, PROJ_BIAS, DOWN_BIAS, ROUTER = range(5)
SHIFT1, SCALE1, GATE1, SHIFT2, SCALE2, GATE2 = range(6)


def forward_kernel(
    off_ref,
    gate_ref,
    mod_ref,
    vec_ref,
    keep_ref,
    tokens_ref,
    cot_ref,
    g_ref,
    up_ref,
    down_ref,
    lse_ref,
    tg_ref,
    n1_ref,
    qkv_ref,
    w_ref,
    wp_ref,
    att_ref,
    gated_ref,
    attn_ref,
    after_ref,
    n2_ref,
    gm_ref,
    g_up_ref,
    g_down_ref,
    lse_sc,
    g_s,
    tok_s,
    w_s,
    wp_s,
    n1_s,
    qkv_s,
    att_s,
    gated_s,
    cot_s,
    cot_sems,
    sems,
    attn_slots,
    attn_sems,
    after_slots,
    after_sems,
    n2_slots,
    n2_sems,
    gm_slots,
    gm_sems,
    *gather_sems,
    heads,
    blk,
    planes,
):
    t, d = tok_s.shape
    hd = d // heads
    nb = t // blk
    c = hd**-0.5 * LOG2E
    place = Place(planes)
    place.barrier()
    half = len(gather_sems) // 2
    gathers = [
        Gather(place, up_ref, g_up_ref, *gather_sems[:half]),
        Gather(place, down_ref, g_down_ref, *gather_sems[half:]),
    ]
    parts = gathers[0].parts()
    for g in gathers:
        g.run("begin")
    groups = spread_out(
        [functools.partial(g.run, part) for part in parts[1:-1] for g in gathers], 2 * nb + heads
    )

    def run_group(i):
        for step in groups[i]:
            step()

    moves = {
        name: pltpu.make_async_copy(src, dst, sems.at[i])
        for i, (name, src, dst) in enumerate(
            (
                ("g", g_ref, g_s),
                ("tok", tokens_ref, tok_s),
                ("w", w_s, w_ref),
                ("wp", wp_s, wp_ref),
                ("n1", n1_s, n1_ref),
                ("qkv", qkv_s, qkv_ref),
                ("att", att_s, att_ref),
                ("gated", gated_s, gated_ref),
            )
        )
    }

    def cot_copy(i):
        return pltpu.make_async_copy(
            cot_ref.at[pl.ds(i * blk, blk)], cot_s.at[i % 2], cot_sems.at[i % 2]
        )

    moves["g"].start()
    moves["tok"].start()
    for i in range(2):
        cot_copy(i).start()
    devices = g_s.shape[0]
    r = d // devices
    moves["g"].wait()
    for i in range(devices):
        rows = slice(i * r, (i + 1) * r)
        for b in range(3):
            w_s[rows, b * d : (b + 1) * d] = g_s[i, b * r : (b + 1) * r, :]
        wp_s[rows, :] = g_s[i, 3 * r : 4 * r, :]
    moves["w"].start()
    moves["wp"].start()
    moves["tok"].wait()

    def vector(i):
        return vec_ref[i : i + 1, :]

    def mod(i, k):
        return mod_ref[i, k : k + 1, :]

    bias = jnp.concatenate(
        [vector(QUERY_BIAS), jnp.zeros((1, d), F32), vector(VALUE_BIAS)], axis=1
    )
    for i in range(nb):
        rows = slice(i * blk, (i + 1) * blk)
        normed, _ = ln_parts(tok_s[rows, :])
        low = (normed * (1.0 + mod(i, SCALE1)) + mod(i, SHIFT1)).astype(BF)
        n1_s[rows, :] = low
        qkv_s[rows, :] = (dg(low, w_s[...], NN) + bias).astype(BF)
        run_group(i)
    moves["n1"].start()
    moves["qkv"].start()
    off = off_ref[0]
    lane128 = lax.broadcasted_iota(jnp.int32, (1, 128), 1)

    def body(h, carry):
        a, mask = head_window(h, hd, d)
        keys = qkv_s[:, pl.ds(pl.multiple_of(d + a, 128), WINDOW)]
        values = qkv_s[:, pl.ds(pl.multiple_of(2 * d + a, 128), WINDOW)]
        cols = pl.ds(a, WINDOW)
        for i in range(nb):
            rows = pl.ds(i * blk, blk)
            q = qkv_s[rows, cols]
            q = jnp.where(mask, q, jnp.zeros_like(q))
            s = dg(q, keys, NT)
            cuts = [s[:, j * blk : (j + 1) * blk] for j in range(nb)]
            own = jnp.max(cuts[i], axis=1, keepdims=True) * c
            others = functools.reduce(jnp.maximum, [cuts[j] for j in range(nb) if j != i])
            m = jnp.maximum(own, jnp.max(others, axis=1, keepdims=True) * c + off)
            m_off = m - off
            ps = [jnp.exp2(cuts[j] * c - (m if j == i else m_off)) for j in range(nb)]
            total = jnp.sum(functools.reduce(jnp.add, ps), axis=1, keepdims=True)
            p = jnp.concatenate([x.astype(BF) for x in ps], axis=1)
            o = dg(p, values, NN) * (1.0 / total)
            og = (o * gate_ref[i, :, cols]).astype(BF)
            att_s[rows, cols] = jnp.where(mask, o, att_s[rows, cols])
            gated_s[rows, cols] = jnp.where(mask, og, gated_s[rows, cols])
            lse_sc[rows, :] = jnp.where(lane128 == h, m + jnp.log2(total), lse_sc[rows, :])
        run_at(h, groups[nb : nb + heads])
        return carry

    lax.fori_loop(0, heads, body, 0)
    moves["att"].start()
    moves["gated"].start()
    lse_ref[...] = lse_sc[...].T[:heads, :]
    streams = [
        Stream(attn_slots, attn_sems, attn_ref),
        Stream(after_slots, after_sems, after_ref),
        Stream(n2_slots, n2_sems, n2_ref),
        Stream(gm_slots, gm_sems, gm_ref),
    ]
    for i in range(nb):
        rows = slice(i * blk, (i + 1) * blk)
        attn = dg(gated_s[rows, :], wp_s[...], NN) + vector(PROJ_BIAS)
        streams[0].put(attn)
        after = tok_s[rows, :] + mod(i, GATE1) * attn
        streams[1].put(after)
        normed, _ = ln_parts(after)
        y = normed * (1.0 + mod(i, SCALE2)) + mod(i, SHIFT2)
        streams[2].put(y.astype(BF))
        token_gate = jax.nn.sigmoid(jnp.sum(y * vector(ROUTER), axis=1, keepdims=True))
        tg_ref[rows, :] = token_gate
        cot_copy(i).wait()
        cot = cot_s[i % 2]
        streams[3].put((cot * (mod(i, GATE2) * (keep_ref[rows, :] * token_gate))).astype(BF))
        if i + 2 < nb:
            cot_copy(i + 2).start()
        run_group(nb + heads + i)
    for g in gathers:
        g.run("end")
    for stream in streams:
        stream.end()
    for name in ("w", "wp", "n1", "qkv", "att", "gated"):
        moves[name].wait()


def forward_call(off, gate_rows, mods, vecs, keep, tokens, cot, g, up, down, heads, blk, planes):
    t, d = tokens.shape
    gathered = shape((4, planes, 2) + up.shape, BF)
    dma = pltpu.SemaphoreType.DMA
    return pl.pallas_call(
        functools.partial(forward_kernel, heads=heads, blk=blk, planes=planes),
        out_shape=(
            shape((heads, t)),
            shape((t, 1)),
            shape((t, d), BF),
            shape((t, 3 * d), BF),
            shape((d, 3 * d), BF),
            shape((d, d), BF),
            shape((t, d)),
            shape((t, d), BF),
            shape((t, d)),
            shape((t, d)),
            shape((t, d), BF),
            shape((t, d), BF),
            gathered,
            gathered,
        ),
        in_specs=[SMEM_SPEC] + [VMEM_SPEC] * 4 + [ANY_SPEC] * 5,
        out_specs=(VMEM_SPEC,) * 2 + (ANY_SPEC,) * 12,
        scratch_shapes=[
            pltpu.VMEM((t, 128), F32),
            pltpu.VMEM(g.shape, BF),
            pltpu.VMEM((t, d), F32),
            pltpu.VMEM((d, 3 * d), BF),
            pltpu.VMEM((d, d), BF),
            pltpu.VMEM((t, d), BF),
            pltpu.VMEM((t, 3 * d), BF),
            pltpu.VMEM((t, d), F32),
            pltpu.VMEM((t, d), BF),
            pltpu.VMEM((2, blk, d), F32),
            dma((2,)),
            dma((8,)),
        ]
        + Stream.scratch(blk, d, F32) * 2
        + Stream.scratch(blk, d, BF) * 2
        + Gather.scratch(planes) * 2,
        compiler_params=params(62, collective_id=2),
        name="attention_and_middle_forward",
    )(off, gate_rows, mods, vecs, keep, tokens, cot, g, up, down)


def attn_bwd_kernel(
    off_ref,
    qkv_ref,
    do_ref,
    lse_ref,
    delta_ref,
    up_ref,
    down_ref,
    dqkv_ref,
    g_up_ref,
    g_down_ref,
    kt_sc,
    dqt_sc,
    *rest,
    heads,
    blk,
    planes,
):
    place = Place(planes)
    place.barrier(True)
    half = len(rest) // 2
    first = planes // 2

    def source(ref):
        return lambda j, c: ref.at[:, j - first, c]

    js = list(range(first, planes))
    scatters = [
        Scatter(place, 0, js, source(up_ref), *rest[:half]),
        Scatter(place, 1, js, source(down_ref), *rest[half:]),
    ]
    steps = scatter_steps(scatters)
    steps[0]()
    groups = spread_out(steps[1:], heads)
    t, d = do_ref.shape
    hd = d // heads
    nb = t // blk
    scale = hd**-0.5
    c = scale * LOG2E
    off = off_ref[0]
    kt_sc[...] = qkv_ref[:, d : 2 * d].T

    def body(h, carry):
        a, mask = head_window(h, hd, d)
        cols = pl.ds(a, WINDOW)
        key_cols = pl.ds(pl.multiple_of(d + a, 128), WINDOW)
        value_cols = pl.ds(pl.multiple_of(2 * d + a, 128), WINDOW)
        keys = qkv_ref[:, key_cols]
        values = qkv_ref[:, value_cols]
        keys_t = kt_sc[cols, :]
        dk_sum = None
        dv_sum = None
        for i in range(nb):
            rows = pl.ds(i * blk, blk)
            span = slice(i * blk, (i + 1) * blk)
            q = qkv_ref[rows, cols]
            q = jnp.where(mask, q, jnp.zeros_like(q))
            do = do_ref[rows, cols]
            do = jnp.where(mask, do, jnp.zeros_like(do))
            lse = lse_ref[pl.ds(h, 1), span]
            delta = delta_ref[pl.ds(h, 1), span]
            s_t = dg(keys, q, NT)
            dp_t = dg(values, do, NT)
            ps = []
            ds = []
            for j in range(nb):
                part = slice(j * blk, (j + 1) * blk)
                p = jnp.exp2(s_t[part] * c - (lse if j == i else lse - off))
                ps.append(p.astype(BF))
                ds.append((p * (dp_t[part] - delta)).astype(BF))
            p = jnp.concatenate(ps, axis=0)
            grad_s = jnp.concatenate(ds, axis=0)
            dv = dg(p, do, NN)
            dk = dg(grad_s, q, NN)
            dv_sum = dv if dv_sum is None else dv_sum + dv
            dk_sum = dk if dk_sum is None else dk_sum + dk
            dqt_sc[:, span] = (dg(keys_t, grad_s, NN) * scale).astype(BF)
        dk = (dk_sum * scale).astype(BF)
        dqkv_ref[:, key_cols] = jnp.where(mask, dk, dqkv_ref[:, key_cols])
        dqkv_ref[:, value_cols] = jnp.where(mask, dv_sum.astype(BF), dqkv_ref[:, value_cols])
        dqkv_ref[:, cols] = jnp.where(mask, dqt_sc[...].T, dqkv_ref[:, cols])
        run_at(h, groups)
        return carry

    lax.fori_loop(0, heads, body, 0)
    g_up_ref[...] = scatters[0].total()
    g_down_ref[...] = scatters[1].total()


def attn_bwd(off, qkv, do, lse, delta, up, down, heads, blk, planes):
    t, d = do.shape
    rows, cols = up.shape[3:]
    return pl.pallas_call(
        functools.partial(attn_bwd_kernel, heads=heads, blk=blk, planes=planes),
        out_shape=(shape((t, 3 * d), BF), shape((rows, cols)), shape((rows, cols))),
        in_specs=[SMEM_SPEC] + [VMEM_SPEC] * 4 + [ANY_SPEC] * 2,
        out_specs=(VMEM_SPEC,) * 3,
        scratch_shapes=[pltpu.VMEM((d, t), BF), pltpu.VMEM((WINDOW, t), BF)]
        + Scatter.scratch(planes - planes // 2, rows, cols) * 2,
        compiler_params=params(collective_id=3),
        name="attention_backward",
    )(off, qkv, do, lse, delta, up, down)


def mlp_kernel(
    n2_ref,
    gm_ref,
    b1_ref,
    cs_ref,
    g1_ref,
    g2_ref,
    mlp_ref,
    gn2_ref,
    gb1_ref,
    gch_ref,
    o1_ref,
    o2_ref,
    p1_ref,
    p2_ref,
    g1_s,
    g2_s,
    w1_s,
    w2_s,
    sc_s,
    gp_s,
    p1_s,
    p2_s,
    g_sems,
    p_sems,
    *rest,
    blk,
    planes,
):
    t, d = n2_ref.shape
    nb = t // blk
    hidden = w1_s.shape[0]
    quarter = hidden // 8
    piece = d // 4
    j = pl.program_id(0)
    place = Place(planes)
    hosted = planes // 2
    half = len(rest) // 2
    scatters = [
        Scatter(place, u, list(range(hosted)), lambda j, c, p=p: p.at[:, c], None, *scratch)
        for u, (p, scratch) in enumerate(((p1_s, rest[:half]), (p2_s, rest[half:])))
    ]

    def loads(step):
        plane = lax.rem(place.z + 1 + step, planes)
        return [
            pltpu.make_async_copy(g.at[:, plane], slot, g_sems.at[i])
            for i, (g, slot) in enumerate(((g1_ref, g1_s), (g2_ref, g2_s)))
        ]

    def keeps(step):
        return [
            pltpu.make_async_copy(slot, p.at[:, step - hosted], p_sems.at[i])
            for i, (slot, p) in enumerate(((p1_s, p1_ref), (p2_s, p2_ref)))
        ]

    def early(step):
        for s in scatters:
            if step - 1 < hosted:
                s.take(1, step - 1)
                s.issue(2, step - 1)
        for s in scatters:
            if 0 <= step - 2 < hosted:
                s.take(3, step - 2)

    def late(step):
        for s in scatters:
            if step - 1 < hosted:
                s.take(2, step - 1)
                s.issue(3, step - 1)
                s.sent(1, step - 1)
        if step - 1 >= hosted:
            for copy in keeps(step - 1):
                copy.wait()

    def at_steps(do):
        for step in range(1, planes):
            pl.when(j == step)(functools.partial(do, step))

    def places():
        for c in range(2):
            for k in range(4):
                yield c, slice((4 * c + k) * quarter, (4 * c + k + 1) * quarter), k

    @pl.when(j == 0)
    def _():
        for copy in loads(0):
            copy.start()
        place.barrier(True)
        mlp_ref[...] = jnp.zeros_like(mlp_ref)
        gn2_ref[...] = jnp.zeros_like(gn2_ref)

    for copy in loads(j):
        copy.wait()
    for c, rows, k in places():
        cols = slice(k * piece, (k + 1) * piece)
        for w, g in ((w1_s, g1_s), (w2_s, g2_s)):
            w[rows, :] = jnp.concatenate([g[n, c, :quarter, cols] for n in range(4)], axis=1)

    @pl.when(j + 1 < planes)
    def _():
        for copy in loads(j + 1):
            copy.start()

    at_steps(early)
    w1 = w1_s[...]
    w2 = w2_s[...]
    grad_bias = None
    for i in range(nb):
        rows = slice(i * blk, (i + 1) * blk)
        pre = dg(n2_ref[rows, :], w1, NT) + b1_ref[0]
        grad_scaled = dg(gm_ref[rows, :], w2, NT)
        act, slope = gelu_parts(pre)
        gate = cs_ref[0, i : i + 1]
        scaled = (act * gate).astype(BF)
        grad_pre = (grad_scaled * gate * slope).astype(BF)
        gch_ref[0, i : i + 1] = col_sum(grad_scaled * act)
        part = col_sum(grad_pre.astype(F32))
        grad_bias = part if grad_bias is None else grad_bias + part
        sc_s[rows, :] = scaled
        gp_s[rows, :] = grad_pre
        mlp_ref[rows, :] += dg(scaled, w2, NN)
        gn2_ref[rows, :] += dg(grad_pre, w1, NN)
    gb1_ref[0] = grad_bias

    at_steps(late)
    for left, right, out in ((gp_s, n2_ref, p1_s), (sc_s, gm_ref, p2_s)):
        grad = dg(left[...], right[...], TN).astype(BF)
        for c, rows, k in places():
            for n in range(4):
                out[n, c, :quarter, k * piece : (k + 1) * piece] = grad[rows, n * piece : (n + 1) * piece]
    for step in range(planes):

        @pl.when(j == step)
        def _(step=step):
            if step < hosted:
                for s in scatters:
                    s.issue(1, step)
            else:
                for copy in keeps(step):
                    copy.start()

    @pl.when(j == planes - 1)
    def _():
        o1_ref[...] = scatters[0].total((2, 3, 4))
        o2_ref[...] = scatters[1].total((2, 3, 4))
        for copy in keeps(planes - 1):
            copy.wait()


def mlp_call(n2, gm, g1, g2, b1, gates, blk):
    t, d = n2.shape
    planes, rows = g1.shape[1], g1.shape[3]
    nb, ff = gates.shape
    hb = ff // planes
    hosted = planes // 2

    def turn(j):
        return lax.rem(lax.axis_index("wide") // 2 + 1 + j, planes)

    b_spec = pl.BlockSpec((1, 1, hb), lambda j: (turn(j), 0, 0))
    c_spec = pl.BlockSpec((1, nb, hb), lambda j: (turn(j), 0, 0))
    kept = shape((4, planes - hosted, 2, rows, d), BF)
    dma = pltpu.SemaphoreType.DMA
    mlp, gn2, gb1, gch, o1, o2, p1, p2 = pl.pallas_call(
        functools.partial(mlp_kernel, blk=blk, planes=planes),
        grid=(planes,),
        out_shape=(
            shape((t, d)),
            shape((t, d)),
            shape((planes, 1, hb)),
            shape((planes, nb, hb)),
            shape((rows, d)),
            shape((rows, d)),
            kept,
            kept,
        ),
        in_specs=[whole(t, d), whole(t, d), b_spec, c_spec, ANY_SPEC, ANY_SPEC],
        out_specs=(whole(t, d), whole(t, d), b_spec, c_spec, whole(rows, d), whole(rows, d))
        + (ANY_SPEC,) * 2,
        scratch_shapes=[pltpu.VMEM((4, 2, rows, d), BF)] * 2
        + [pltpu.VMEM((hb, d), BF)] * 2
        + [pltpu.VMEM((t, hb), BF)] * 2
        + [pltpu.VMEM((4, 2, rows, d), BF)] * 2
        + [dma((2,))] * 2
        + Scatter.scratch(hosted, rows, d, False) * 2,
        compiler_params=params(62, collective_id=5),
        name="feed_forward",
    )(n2, gm, b1.reshape(planes, 1, hb), gates.reshape(nb, planes, hb).transpose(1, 0, 2), g1, g2)
    return mlp, gn2, o1, o2, p1, p2, gb1.reshape(ff), gch.transpose(1, 0, 2).reshape(nb, ff)


def middle_back_kernel(
    mlp_ref,
    gn2_ref,
    after_ref,
    attn_ref,
    cot_ref,
    gm_ref,
    gated_ref,
    att_ref,
    tg_ref,
    keep_ref,
    w_ref,
    vec_ref,
    table_ref,
    head_ref,
    out_ref,
    ga_ref,
    do_ref,
    delta_ref,
    gw_ref,
    mod_ref,
    sums_ref,
    *,
    heads,
):
    d = after_ref.shape[1]
    hd = d // heads
    first = pl.program_id(0) == 0
    after = after_ref[...]
    cot = cot_ref[...]
    gate2 = table_ref[0, GATE2 : GATE2 + 1]
    tg = tg_ref[...]
    keep = keep_ref[...]
    normed, rstd = ln_parts(after)
    scale2 = table_ref[0, SCALE2 : SCALE2 + 1]
    y = normed * (1.0 + scale2) + table_ref[0, SHIFT2 : SHIFT2 + 1]
    mlp_out = mlp_ref[...] + vec_ref[DOWN_BIAS : DOWN_BIAS + 1]
    open_gate = keep * tg
    out_ref[...] = after + (gate2 * open_gate) * mlp_out
    weighted = cot * mlp_out
    grad_tg = jnp.sum(weighted * gate2, axis=1, keepdims=True) * keep
    coef = grad_tg * tg * (1.0 - tg)
    gy = gn2_ref[...] + coef * vec_ref[ROUTER : ROUTER + 1]
    ga = cot + ln_back(gy, normed, rstd, scale2)
    ga_ref[...] = ga
    attn = attn_ref[...]
    g_attn = (ga * table_ref[0, GATE1 : GATE1 + 1]).astype(BF)
    mod_ref[0] = jnp.concatenate(
        [col_sum(ga * attn), col_sum(gy), col_sum(gy * normed), col_sum(weighted * open_gate)], axis=0
    )
    sums = jnp.concatenate(
        [
            col_sum(coef * y),
            col_sum(g_attn.astype(F32)),
            col_sum(gm_ref[...].astype(F32)),
        ],
        axis=0,
    )
    g_gated = dg(g_attn, w_ref[...], NT)
    att = att_ref[...]
    mod_ref[1] = jnp.concatenate([col_sum(g_gated * att), jnp.zeros((3, d), F32)], axis=0)
    do = (g_gated * head_ref[0]).astype(BF)
    do_ref[...] = do
    lane = lax.broadcasted_iota(jnp.int32, (heads, d), 1)
    head = lax.broadcasted_iota(jnp.int32, (heads, d), 0) * hd
    pick = jnp.where((lane >= head) & (lane < head + hd), 1.0, 0.0)
    delta_ref[...] = lax.dot_general(
        pick, do.astype(F32) * att, NT, precision=HIGHEST, preferred_element_type=F32
    )
    gw = dg(gated_ref[...], g_attn, TN)

    @pl.when(first)
    def _():
        sums_ref[...] = sums
        gw_ref[...] = gw

    @pl.when(jnp.logical_not(first))
    def _():
        sums_ref[...] += sums
        gw_ref[...] += gw


def middle_back_call(
    mlp, gn2, after, attn, cot, gm, gated, att, tg, keep, w, vecs, table, head_rows, heads, blk
):
    t, d = after.shape
    nb = t // blk
    r, v, column = rows_of(blk, d), row_vec(d), rows_of(blk, 1)
    return pl.pallas_call(
        functools.partial(middle_back_kernel, heads=heads),
        grid=(nb,),
        out_shape=(
            shape((t, d)),
            shape((t, d)),
            shape((t, d), BF),
            shape((heads, t)),
            shape((d, d)),
            shape((nb * 2, 4, d)),
            shape((3, d)),
        ),
        in_specs=[r] * 8 + [column, column, whole(d, d), whole(*vecs.shape)]
        + [pl.BlockSpec((1,) + table.shape[1:], lambda i: (i, 0, 0)), v],
        out_specs=(
            r,
            r,
            r,
            pl.BlockSpec((heads, blk), lambda i: (0, i)),
            whole(d, d),
            pl.BlockSpec((2, 4, d), lambda i: (i, 0, 0)),
            whole(3, d),
        ),
        compiler_params=params(),
        name="middle_backward",
    )(mlp, gn2, after, attn, cot, gm, gated, att, tg, keep, w, vecs, table, head_rows)


def qkv_weight_kernel(n1_ref, q_ref, k_ref, v_ref, gp_ref, out_ref, bias_ref, n1t):
    @pl.when(pl.program_id(0) == 0)
    def _():
        n1t[...] = n1_ref[...].T

    width = q_ref.shape[1]
    devices = out_ref.shape[1]
    r = n1_ref.shape[1] // devices
    dqkv = jnp.concatenate([q_ref[...], k_ref[...], v_ref[...]], axis=1)
    grad = dg(n1t[...], dqkv, NN).astype(BF)
    bias_ref[0] = col_sum(dqkv.astype(F32))
    for i in range(devices):
        rows = slice(i * r, (i + 1) * r)
        for b in range(3):
            out_ref[0, i, b * r : (b + 1) * r, :] = grad[rows, b * width : (b + 1) * width]
        out_ref[0, i, 3 * r : 4 * r, :] = gp_ref[rows, :].astype(BF)


def qkv_weight_call(n1, dqkv, g_proj, devices, cuts):
    t, d = n1.shape
    width = d // cuts
    rows = up_to(4 * d // devices, 16)
    third = [pl.BlockSpec((t, width), lambda j, b=b: (0, b * cuts + j)) for b in range(3)]
    parts, bias = pl.pallas_call(
        qkv_weight_kernel,
        grid=(cuts,),
        out_shape=(shape((cuts, devices, rows, width), BF), shape((cuts, 1, 3 * width))),
        in_specs=[whole(t, d)] + third + [pl.BlockSpec((d, width), lambda j: (0, j))],
        out_specs=(
            pl.BlockSpec((1, devices, rows, width), lambda j: (j, 0, 0, 0)),
            pl.BlockSpec((1, 1, 3 * width), lambda j: (j, 0, 0)),
        ),
        scratch_shapes=[pltpu.VMEM((d, t), BF)],
        compiler_params=params(),
        name="qkv_weight_gradient",
    )(n1, dqkv, dqkv, dqkv, g_proj)
    return parts, bias.reshape(cuts, 3, width).transpose(1, 0, 2).reshape(3, d)


def qkv_back_kernel(dqkv_ref, w_ref, tokens_ref, ga_ref, table_ref, out_ref, mod_ref):
    gy = dg(dqkv_ref[...], w_ref[...], NT)
    normed, rstd = ln_parts(tokens_ref[...])
    out_ref[...] = ga_ref[...] + ln_back(gy, normed, rstd, table_ref[0, SCALE1 : SCALE1 + 1])
    mod_ref[0] = jnp.concatenate([col_sum(gy), col_sum(gy * normed)], axis=0)


def qkv_back_call(dqkv, w, tokens, ga, table, blk):
    t, d = tokens.shape
    n = dqkv.shape[1]
    r = rows_of(blk, d)
    return pl.pallas_call(
        qkv_back_kernel,
        grid=(t // blk,),
        out_shape=(shape((t, d)), shape((t // blk, 2, d))),
        in_specs=[rows_of(blk, n), whole(d, n), r, r]
        + [pl.BlockSpec((1,) + table.shape[1:], lambda i: (i, 0, 0))],
        out_specs=(r, pl.BlockSpec((1, 2, d), lambda i: (i, 0, 0))),
        compiler_params=params(),
        name="qkv_backward",
    )(dqkv, w, tokens, ga, table)


def final_kernel(
    part_ref,
    sums_ref,
    mods_ref,
    logits_ref,
    conds_ref,
    out_ref,
    sum_ref,
    ada_ref,
    ada_bias_ref,
    router_ref,
    logit_ref,
    all_sums,
    all_mods,
    all_logits,
    mod_sems,
    logit_sems,
    *rest,
    planes,
    cuts,
):
    place = Place(planes)
    mods = Exchange(place, mods_ref, all_mods, mod_sems, False)
    logits = Exchange(place, logits_ref, all_logits, logit_sems, True)
    mods.greet()
    width = out_ref.shape[1] // cuts
    sums = Gather(place, sums_ref, all_sums, *rest[:6])
    rest = rest[6:]
    each = len(rest) // cuts

    def source(m):
        return lambda j, c: part_ref.at[m, :, lax.rem(place.z + 1 + j, planes), c]

    scatters = [
        Scatter(place, m, list(range(planes)), source(m), *rest[each * m : each * (m + 1)])
        for m in range(cuts)
    ]
    steps = scatter_steps(scatters)
    parts = sums.parts()
    steps[0]()
    sums.run("begin")
    mods.start()
    logits.start()

    def products():
        mods.arrive()
        logits.arrive()
        devices, rows, d = conds_ref.shape
        conds = conds_ref[...].reshape(devices * rows, d)
        got = all_mods[...].reshape(devices * rows, -1)
        columns = ada_bias_ref.shape[1]
        ada_ref[...] = dg(conds, got, TN)[:, :columns]
        ada_bias_ref[...] = col_sum(got.astype(F32))[:, :columns]
        got = all_logits[...].reshape(devices * rows, -1)
        router_ref[...] = lax.dot_general(
            conds.astype(F32), got, TN, precision=HIGHEST, preferred_element_type=F32
        )
        logit_ref[...] = col_sum(got)

    small = [functools.partial(sums.run, part) for part in parts[1:-1]]
    groups = spread_out(small, len(steps) - 1)
    for i, (step, group) in enumerate(zip(steps[1:], groups)):
        step()
        for part in group:
            part()
        if i == 2:
            products()
    sums.run("end")
    sum_ref[...] = jnp.sum(all_sums[...].reshape((8 * planes,) + sum_ref.shape), axis=0)
    for m, s in enumerate(scatters):
        out_ref[:, m * width : (m + 1) * width] = s.total()
    mods.end()
    logits.end()


def final_call(parts, sums, mods, logits, conds, mod_width, planes):
    cuts, devices, rows, width = parts.shape
    d = conds.shape[2]
    spread = (4, planes, 2)
    return pl.pallas_call(
        functools.partial(final_kernel, planes=planes, cuts=cuts),
        out_shape=(
            shape((rows, cuts * width)),
            shape(sums.shape),
            shape((d, mod_width)),
            shape((1, mod_width)),
            shape((d, logits.shape[1])),
            shape((1, logits.shape[1])),
        ),
        in_specs=[ANY_SPEC] + [VMEM_SPEC] * 4,
        out_specs=(VMEM_SPEC,) * 6,
        scratch_shapes=[
            pltpu.VMEM(spread + sums.shape, F32),
            pltpu.VMEM(mods.shape, BF),
            pltpu.VMEM((devices,) + logits.shape, F32),
        ]
        + [Exchange.scratch(planes)] * 2
        + Gather.scratch(planes)
        + Scatter.scratch(planes, rows, width) * cuts,
        compiler_params=params(collective_id=4),
        name="attention_weight_sums",
    )(parts.reshape((cuts,) + spread + (rows, width)), sums, mods, logits, conds)


def on_device(
    planes,
    tokens,
    conditioning,
    row_items,
    head_mask,
    chan_mask,
    skip_mask,
    ada_weight,
    ada_bias,
    qkv_weight,
    query_bias,
    value_bias,
    proj_weight,
    proj_bias,
    fc1_weight,
    fc1_bias,
    fc2_weight,
    fc2_bias,
    head_router,
    head_router_bias,
    chan_router,
    chan_router_bias,
    token_router,
    cotangent,
):
    t, d = tokens.shape
    slots = conditioning.shape[0]
    heads = head_mask.shape[1]
    groups = chan_mask.shape[1]
    hidden = fc1_bias.shape[0]
    hd = d // heads
    unit = hidden // groups
    blk = t // slots
    single = row_items[0] == 1
    off = jnp.where(single, 0.0, MASKED).astype(F32).reshape(1)

    def per_block(table):
        return jnp.where(single, table[:1], table)

    def per_slot(blocks):
        total = jnp.sum(blocks, axis=0, keepdims=True)
        first = (jnp.arange(slots) == 0).reshape((slots,) + (1,) * (blocks.ndim - 1))
        return jnp.where(single, jnp.where(first, total, 0.0), blocks)

    devices = 8 * planes
    def pack_rows(*blocks):
        return pad_rows(jnp.concatenate(blocks, axis=0))

    def pack_piece(weight):
        rows, cols = weight.shape
        return pad_rows(weight.reshape(4, rows // 4, cols).transpose(1, 0, 2).reshape(rows // 4, d))

    def unpack_piece(piece, rows):
        cols = d // 4
        return piece[: rows // 4].reshape(rows // 4, 4, cols).transpose(1, 0, 2).reshape(rows, cols)

    silu_cond = jax.nn.silu(conditioning.astype(F32)).astype(BF)
    shard = pack_rows(qkv_weight[:, :d], qkv_weight[:, d : 2 * d], qkv_weight[:, 2 * d :], proj_weight)
    conds_pad = pad_rows(silu_cond.reshape(slots, -1, 128).transpose(1, 0, 2).reshape(-1, 128))
    g_attn, conds, mod_columns = prologue_call(
        shard, conds_pad, ada_weight, ada_bias.astype(F32)[None], planes, slots
    )
    mod_width = ada_bias.shape[0]
    every_cond = conds[:, : slots * d // 128].reshape(devices, -1, slots, 128).transpose(0, 2, 1, 3)
    every_cond = jnp.pad(
        every_cond.reshape(devices, slots, d), ((0, 0), (0, up_to(slots, 16) - slots), (0, 0))
    )
    modulation = mod_columns[:, :slots, :mod_width].transpose(1, 0, 2).reshape(slots, 6, d)
    table = per_block(modulation.astype(F32))
    def router(weight, bias, mask):
        gate = jax.nn.sigmoid(dg(silu_cond, weight, NN) + bias.astype(F32))
        mask = mask.astype(F32)
        return mask * gate, mask * gate * (1.0 - gate)

    head_gate, head_slope = router(head_router, head_router_bias, head_mask)
    chan_gate, chan_slope = router(chan_router, chan_router_bias, chan_mask)
    head_rows = jnp.repeat(per_block(head_gate), hd, axis=1)[:, None, :]
    chan_rows = jnp.repeat(per_block(chan_gate), unit, axis=1)
    keep = (1.0 - skip_mask.astype(F32))[:, None]

    vecs = jnp.concatenate([query_bias, value_bias, proj_bias, fc2_bias, token_router])
    vecs = vecs.astype(F32).reshape(5, d)
    lse, tg, n1, qkv, full_qkv, full_proj, att, gated, attn, after, n2, gm, g_up, g_down = forward_call(
        off,
        head_rows,
        table,
        vecs,
        keep,
        tokens,
        cotangent,
        g_attn.reshape((devices,) + shard.shape),
        pack_piece(fc1_weight),
        pack_piece(fc2_weight),
        heads,
        blk,
        planes,
    )
    mlp, gn2, o_up, o_down, p_up, p_down, gb1, gch = mlp_call(
        n2, gm, g_up, g_down, fc1_bias.astype(F32), chan_rows, blk
    )
    output, ga, do, delta, g_proj, mods, sums = middle_back_call(
        mlp,
        gn2,
        after,
        attn,
        cotangent,
        gm,
        gated,
        att,
        tg,
        keep,
        full_proj,
        vecs,
        table,
        head_rows,
        heads,
        blk,
    )
    mods = mods.reshape(slots, 8, d)
    dqkv, g_up, g_down = attn_bwd(off, qkv, do, lse, delta, p_up, p_down, heads, blk, planes)
    parts, qkv_sums = qkv_weight_call(n1, dqkv, g_proj, devices, 3)
    grad_tokens, mods1 = qkv_back_call(dqkv, full_qkv, tokens, ga, table, blk)
    block_mods = jnp.concatenate(
        [mods1[:, 0], mods1[:, 1], mods[:, 0], mods[:, 1], mods[:, 2], mods[:, 3]], axis=1
    )
    grad_slot_mod = per_slot(block_mods).astype(BF)
    g_head = per_slot(jnp.sum(mods[:, 4].reshape(slots, heads, hd), axis=2)) * head_slope
    g_chan = per_slot(jnp.sum(gch.reshape(slots, groups, unit), axis=2)) * chan_slope
    logits = jnp.pad(
        jnp.concatenate([g_head, g_chan], axis=1),
        ((0, up_to(slots, 16) - slots), (0, up_to(heads + groups, 128) - heads - groups)),
    )
    blocks = grad_slot_mod.reshape(slots, devices, mod_width).transpose(1, 0, 2)
    blocks = jnp.pad(
        blocks,
        ((0, 0), (0, up_to(slots, 16) - slots), (0, up_to(mod_width, 128) - mod_width)),
    )
    vector = jnp.concatenate([qkv_sums[0], qkv_sums[2], sums[1], gb1, sums[2], sums[0]])
    length = vector.shape[0]
    vector = jnp.pad(vector, (0, up_to(length, 1024) - length)).reshape(-1, 128)
    g_attn, small, grad_ada_weight, grad_ada_bias, router_grads, logit_sums = final_call(
        parts, vector, blocks, logits, every_cond, mod_width, planes
    )
    g_attn = g_attn[: 4 * (d // devices)].reshape(4, d // devices, d)
    small = small.reshape(-1)[:length]
    grad_ada_bias = grad_ada_bias[0]
    logit_sums = logit_sums[0]
    ends = [d, 2 * d, 3 * d, 3 * d + hidden, 4 * d + hidden]
    g_query, g_value, g_proj_bias, g_b1, g_b2, g_router = jnp.split(small, ends)
    return (
        output,
        grad_tokens,
        grad_ada_weight,
        grad_ada_bias,
        g_attn[:3].transpose(1, 0, 2).reshape(d // devices, 3 * d),
        g_query,
        g_value,
        g_attn[3],
        g_proj_bias,
        unpack_piece(g_up + o_up, fc1_weight.shape[0]),
        g_b1,
        unpack_piece(g_down + o_down, fc2_weight.shape[0]),
        g_b2,
        router_grads[:, :heads],
        logit_sums[:heads],
        router_grads[:, heads : heads + groups],
        logit_sums[heads : heads + groups],
        g_router,
    )


def solution(mesh):
    planes = mesh.shape["wide"] // 2
    return jax.shard_map(
        functools.partial(on_device, planes),
        mesh=mesh,
        in_specs=(
            P(("narrow", "wide"), None),
            P(("narrow", "wide"), None),
            P(("narrow", "wide")),
            P(("narrow", "wide"), None),
            P(("narrow", "wide"), None),
            P(("narrow", "wide")),
            P(None, ("narrow", "wide")),
            P(("narrow", "wide")),
            P(("narrow", "wide"), None),
            P(),
            P(),
            P(("narrow", "wide"), None),
            P(),
            P("wide", "narrow"),
            P(),
            P("wide", "narrow"),
            P(),
            P(),
            P(),
            P(),
            P(),
            P(),
            P(("narrow", "wide"), None),
        ),
        out_specs=(
            P(("narrow", "wide"), None),
            P(("narrow", "wide"), None),
            P(None, ("narrow", "wide")),
            P(("narrow", "wide")),
            P(("narrow", "wide"), None),
            P(),
            P(),
            P(("narrow", "wide"), None),
            P(),
            P("wide", "narrow"),
            P(),
            P("wide", "narrow"),
            P(),
            P(),
            P(),
            P(),
            P(),
            P(),
        ),
        check_vma=False,
    )
```

```python
import functools

import jax
import jax.numpy as jnp
from jax import lax
from jax.experimental import pallas as pl
from jax.experimental.pallas import tpu as pltpu
from jax.sharding import PartitionSpec as P

HIGHEST = lax.Precision.HIGHEST
F32 = jnp.float32
BF = jnp.bfloat16
EPSILON = 1e-06
MASKED = -1e30
LOG2E = 1.4426950408889634
WINDOW = 256
NN = (((1,), (0,)), ((), ()))
NT = (((1,), (1,)), ((), ()))
TN = (((0,), (0,)), ((), ()))
VMEM_SPEC = pl.BlockSpec(memory_space=pltpu.VMEM)
ANY_SPEC = pl.BlockSpec(memory_space=pl.ANY)
MESH = pl.DeviceIdType.MESH
SMEM_SPEC = pl.BlockSpec(memory_space=pltpu.SMEM)


def dg(a, b, dims):
    return lax.dot_general(a, b, dims, preferred_element_type=F32)


def params(mib=60, collective_id=None):
    if collective_id is None:
        return pltpu.CompilerParams(vmem_limit_bytes=mib << 20)
    return pltpu.CompilerParams(
        vmem_limit_bytes=mib << 20, collective_id=collective_id, has_side_effects=True
    )


def up_to(count, multiple):
    return -(-count // multiple) * multiple


def pad_rows(x):
    return jnp.pad(x, ((0, up_to(x.shape[0], 16) - x.shape[0]), (0, 0)))


def spread_out(steps, count):
    groups = [[] for _ in range(count)]
    for i, step in enumerate(steps):
        groups[i * count // len(steps)].append(step)
    return groups


def run_at(index, groups):
    for i, group in enumerate(groups):
        if group:

            @pl.when(index == i)
            def _(group=group):
                for step in group:
                    step()


def shape(dims, dtype=F32):
    return jax.ShapeDtypeStruct(dims, dtype)


def whole(*dims):
    return pl.BlockSpec(dims, lambda i: (0,) * len(dims), pipeline_mode=pl.Buffered(1))


def rows_of(block, width):
    return pl.BlockSpec((block, width), lambda i: (i, 0))


def row_vec(width):
    return pl.BlockSpec((1, 1, width), lambda i: (i, 0, 0))


def ln_parts(x):
    centered = x - jnp.mean(x, axis=-1, keepdims=True)
    rstd = lax.rsqrt(jnp.mean(centered * centered, axis=-1, keepdims=True) + EPSILON)
    return centered * rstd, rstd


def ln_back(grad_y, normed, rstd, scale):
    m = grad_y * (1.0 + scale)
    mean_m = jnp.mean(m, axis=-1, keepdims=True)
    mean_mn = jnp.mean(m * normed, axis=-1, keepdims=True)
    return (m - mean_m - normed * mean_mn) * rstd


def col_sum(x):
    return jnp.sum(x, axis=0, keepdims=True)


def gelu_parts(x):
    k0 = 0.7978845608028654
    k1 = 0.044715
    x2 = x * x
    t = jnp.tanh(k0 * x * (1.0 + k1 * x2))
    half = 0.5 * (1.0 + t)
    return x * half, half + 0.5 * x * (1.0 - t * t) * (k0 * (1.0 + 3.0 * k1 * x2))


class Place:
    def __init__(self, planes):
        self.planes = planes
        self.n = lax.axis_index("narrow")
        w = lax.axis_index("wide")
        self.z = w // 2
        self.c = w % 2
        self.xn = self.n + 1 - 2 * (self.n % 2)
        self.yn = self.n + 2 - 4 * (self.n // 2)
        self.dn = 3 - self.n

    def dev(self, n, z, c):
        return (n, z * 2 + c)

    def barrier(self, every_plane=False):
        sem = pltpu.get_barrier_semaphore()

        def greet(n, z, c):
            pl.semaphore_signal(sem, inc=1, device_id=self.dev(n, z, c), device_id_type=MESH)

        greet(self.xn, self.z, self.c)
        greet(self.yn, self.z, self.c)
        greet(self.n, self.z, 1 - self.c)
        if every_plane:
            for k in range(1, self.planes):
                greet(self.n, lax.rem(self.z + k, self.planes), self.c)
            pl.semaphore_wait(sem, self.planes + 2)
            return
        for step in (-1, 1):

            @pl.when(self.has(step))
            def _(step=step):
                greet(self.n, self.z + step, self.c)

        ends = jnp.where(self.z > 0, 1, 0) + jnp.where(self.z < self.planes - 1, 1, 0)
        pl.semaphore_wait(sem, 3 + ends)

    def has(self, step):
        return self.z + step >= 0 if step < 0 else self.z + step < self.planes


def plane_turn(planes, j):
    order = sorted(range(1, planes), key=lambda k: (-min(k, planes - k), k)) + [0]
    if isinstance(j, int):
        return order[j]
    return sum(jnp.where(j == i, k, 0) for i, k in enumerate(order))


def remote(src, dst, sems, idx, device):
    return pltpu.make_async_remote_copy(
        src_ref=src,
        dst_ref=dst,
        send_sem=sems.at[0, idx],
        recv_sem=sems.at[1, idx],
        device_id=device,
        device_id_type=MESH,
    )


class Gather:
    def __init__(self, place, src, out, own, zs, xs, ys, ds, cs):
        self.p, self.src, self.out = place, src, out
        self.own, self.zs, self.xs, self.ys, self.ds, self.cs = own, zs, xs, ys, ds, cs
        self.steps = [0]
        for k in range(1, place.planes):
            self.steps += [-k, k]

    def index(self, k):
        return k + self.p.planes - 1

    def at(self, n, k, c=None):
        p = self.p
        return self.out.at[n, p.z + k, p.c if c is None else c]

    def mine(self, k):
        return self.src if k == 0 else self.at(self.p.n, k)

    def via(self, k):
        p = self.p
        return (p.xn, p.yn) if k % 2 == 0 else (p.yn, p.xn)

    def copy(self, kind, k):
        p = self.p
        i = self.index(k)
        if kind == "x":
            return remote(self.mine(k), self.at(p.n, k), self.xs, i, p.dev(p.xn, p.z, p.c))
        if kind == "y":
            return remote(self.mine(k), self.at(p.n, k), self.ys, i, p.dev(p.yn, p.z, p.c))
        if kind == "d":
            via, to = self.via(k)
            return remote(self.at(via, k), self.at(via, k), self.ds, i, p.dev(to, p.z, p.c))
        if kind == "up" or kind == "down":
            step = 1 if kind == "up" else -1
            j = self.index(k - step)
            return remote(self.mine(k), self.at(p.n, k), self.zs, j, p.dev(p.n, p.z + step, p.c))
        j = ("c", "C", "d2", "D").index(kind)
        n = (p.n, p.xn, p.yn, p.dn)[j]
        shard = self.mine(k) if j == 0 else self.at(n, k)
        slot = j * (2 * p.planes - 1) + i
        return remote(shard, self.at(n, k), self.cs, slot, p.dev(p.n, p.z, 1 - p.c))

    def arrived(self, n, k, sems, idx, c=None):
        p = self.p
        dst = self.at(n, k, c)
        remote(dst, dst, sems, idx, p.dev(p.xn, p.z, p.c)).wait_recv()

    def run(self, part):
        if part == "begin":
            pltpu.make_async_copy(self.src, self.at(self.p.n, 0), self.own).start()
            self.spread(0)
        elif part == "end":
            pltpu.make_async_copy(self.src, self.at(self.p.n, 0), self.own).wait()
            for k in self.steps:
                self.when(self.p.has(k), functools.partial(self.finish, k))
        else:
            kind, k = part
            self.when(self.p.has(k), functools.partial(getattr(self, kind), k))

    def when(self, cond, do):
        pl.when(cond)(do)

    def onward(self, k, act):
        p = self.p
        if k <= 0:
            self.when(p.has(1), lambda: act(self.copy("up", k)))
        if k >= 0:
            self.when(p.has(-1), lambda: act(self.copy("down", k)))

    def spread(self, k):
        self.onward(k, lambda copy: copy.start())
        self.copy("x", k).start()
        self.copy("y", k).start()
        self.copy("c", k).start()

    def plane(self, k):
        self.arrived(self.p.n, k, self.zs, self.index(k))
        self.spread(k)

    def near(self, k):
        p = self.p
        self.arrived(p.xn, k, self.xs, self.index(k))
        if k % 2 == 0:
            self.copy("d", k).start()
        self.copy("C", k).start()
        self.arrived(p.yn, k, self.ys, self.index(k))
        if k % 2 == 1:
            self.copy("d", k).start()
        self.copy("d2", k).start()

    def far(self, k):
        self.arrived(self.p.dn, k, self.ds, self.index(k))
        self.copy("D", k).start()

    def finish(self, k):
        p = self.p
        for j, n in enumerate((p.n, p.xn, p.yn, p.dn)):
            self.arrived(n, k, self.cs, j * (2 * p.planes - 1) + self.index(k), 1 - p.c)
        for kind in ("x", "y", "d", "c", "C", "d2", "D"):
            self.copy(kind, k).wait_send()
        self.onward(k, lambda copy: copy.wait_send())

    def parts(self):
        found = ["begin"]
        rounds = [[0]] + [[-k, k] for k in range(1, self.p.planes)]
        for r in range(len(rounds) + 2):
            if 0 < r < len(rounds):
                found += [("plane", k) for k in rounds[r]]
            if 1 <= r <= len(rounds):
                found += [("near", k) for k in rounds[r - 1]]
            if 2 <= r:
                found += [("far", k) for k in rounds[r - 2]]
        return found + ["end"]

    @staticmethod
    def scratch(planes):
        dma = pltpu.SemaphoreType.DMA
        span = 2 * planes - 1
        return [dma(())] + [dma((2, span))] * 4 + [dma((2, 4 * span))]


class Scatter:
    def __init__(self, place, turn, js, source, own, r1, r2, r3, r4, own_sem, s1, s2, s3, s4):
        self.p, self.turn, self.js, self.source = place, turn, js, source
        self.own, self.r1, self.r2, self.r3, self.r4 = own, r1, r2, r3, r4
        self.own_sem, self.s1, self.s2, self.s3, self.s4 = own_sem, s1, s2, s3, s4

    def owner(self, j):
        return lax.rem(self.p.z + plane_turn(self.p.planes, j), self.p.planes)

    def moves_on(self, j):
        return j + 1 < self.p.planes

    def load(self, j):
        slot = self.js.index(j) % 2
        return pltpu.make_async_copy(
            self.source(j, self.p.c), self.own.at[slot], self.own_sem.at[slot]
        )

    def x_first(self, j):
        return (self.js.index(j) + self.turn) % 2 == 0

    def sides(self, j):
        p = self.p
        return (p.xn, p.yn) if self.x_first(j) else (p.yn, p.xn)

    def copies(self, stage, j):
        p = self.p
        i = self.js.index(j)
        side, other = self.sides(j)
        if stage == 1:
            to = p.dev(p.n, p.z, 1 - p.c)
            return [remote(self.source(j, 1 - p.c), self.r1.at[i], self.s1, i, to)]
        if stage == 2:
            to = p.dev(side, p.z, p.c)
            return [
                remote(self.r1.at[i, side], self.r2.at[i, 0], self.s2, 2 * i, to),
                remote(self.r1.at[i, p.dn], self.r2.at[i, 1], self.s2, 2 * i + 1, to),
            ]
        if stage == 3:
            to = p.dev(other, p.z, p.c)
            return [remote(self.r1.at[i, other], self.r3.at[i], self.s3, i, to)]
        to = p.dev(p.n, self.owner(j), p.c)
        return [remote(self.r1.at[i, p.n], self.r4.at[i], self.s4, i, to)]

    def issue(self, stage, j):
        for copy in self.copies(stage, j):
            copy.start()

    def sent(self, stage, j):
        for copy in self.copies(stage, j):
            copy.wait_send()

    def begin(self):
        if self.own is not None:
            self.load(self.js[0]).start()

    def take(self, stage, j):
        p = self.p
        i = self.js.index(j)
        for copy in self.copies(stage, j):
            copy.wait_recv()
        side, other = self.sides(j)

        def add(n, value):
            self.r1[i, n] = self.r1[i, n] + value

        if stage == 1:
            if self.own is None:
                mine = self.source(j, p.c)
            else:
                self.load(j).wait()
                if i + 1 < len(self.js):
                    self.load(self.js[i + 1]).start()
                mine = self.own.at[i % 2]
            for n in range(4):
                add(n, mine[n])
        elif stage == 2:
            add(p.n, self.r2[i, 0])
            add(other, self.r2[i, 1])
        else:
            add(p.n, self.r3[i])
            if self.moves_on(j):
                self.issue(4, j)

    def total(self, stages=(1, 2, 3, 4)):
        found = None
        for i, j in enumerate(self.js):
            if self.moves_on(j):
                self.copies(4, j)[0].wait_recv()
                part = self.r4[i].astype(F32)
            else:
                part = self.r1[i, self.p.n].astype(F32)
            found = part if found is None else found + part
        for j in self.js:
            for stage in stages:
                if stage < 4 or self.moves_on(j):
                    self.sent(stage, j)
        return found

    @staticmethod
    def scratch(count, rows, cols, load=True):
        dma = pltpu.SemaphoreType.DMA
        own = [pltpu.VMEM((2, 4, rows, cols), BF)] if load else []
        return own + [
            pltpu.VMEM((count, 4, rows, cols), BF),
            pltpu.VMEM((count, 2, rows, cols), BF),
            pltpu.VMEM((count, rows, cols), BF),
            pltpu.VMEM((count, rows, cols), BF),
            dma((2,)),
            dma((2, count)),
            dma((2, 2 * count)),
            dma((2, count)),
            dma((2, count)),
        ]


def scatter_steps(scatters, span=2, window=2):
    js = scatters[0].js
    units = range(len(scatters))
    queue = [(u, j) for j in js for u in units]
    x_items, y_items = [], []
    for i in range(0, len(js), span):
        pair = [(u, j) for j in js[i : i + span] for u in units]
        for stage in (2, 3):
            for u, j in pair:
                first = scatters[u].x_first(j)
                (x_items if first == (stage == 2) else y_items).append((stage, u, j))
    sent = []
    done = []

    def begin():
        for s in scatters:
            s.begin()
        for u, j in queue[:window]:
            scatters[u].issue(1, j)
            sent.append((u, j))

    def ready(stage, u, j):
        if stage == 2:
            while (u, j) not in done:
                v, i = queue[len(done)]
                scatters[v].take(1, i)
                done.append((v, i))
                if len(sent) < len(queue):
                    v, i = queue[len(sent)]
                    scatters[v].issue(1, i)
                    sent.append((v, i))

    def step(i):
        for items in (x_items, y_items):
            if window <= i < len(items) + window:
                stage, u, j = items[i - window]
                scatters[u].take(stage, j)
        for items in (x_items, y_items):
            if i < len(items):
                stage, u, j = items[i]
                ready(stage, u, j)
                scatters[u].issue(stage, j)

    count = max(len(x_items), len(y_items)) + window
    return [begin] + [functools.partial(step, i) for i in range(count)]


class Exchange:
    def __init__(self, place, src, out, sems, same):
        self.p, self.src, self.out, self.sems, self.same = place, src, out, sems, same
        self.wide = 2 * place.planes
        self.total = 4 * self.wide
        self.me = place.n * self.wide + place.z * 2 + place.c

    def device(self, i):
        other = lax.rem(self.me + i, self.total)
        return other // self.wide, lax.rem(other, self.wide)

    def greet(self):
        sem = pltpu.get_barrier_semaphore()

        def signal(i, carry):
            pl.semaphore_signal(sem, inc=1, device_id=self.device(i), device_id_type=MESH)
            return carry

        lax.fori_loop(1, self.total, signal, 0)
        pl.semaphore_wait(sem, self.total - 1)

    def copy(self, i):
        other = lax.rem(self.me + i, self.total)
        src = self.src if self.same else self.src.at[other]
        return remote(src, self.out.at[self.me], self.sems, i, self.device(i))

    def each(self, do):
        def body(i, carry):
            do(i)
            return carry

        lax.fori_loop(1, self.total, body, 0)

    def start(self):
        self.each(lambda i: self.copy(i).start())
        self.out[self.me] = self.src[...] if self.same else self.src[self.me]

    def arrive(self):
        def wait(i):
            dst = self.out.at[lax.rem(self.me + self.total - i, self.total)]
            remote(dst, dst, self.sems, i, self.device(i)).wait_recv()

        self.each(wait)

    def end(self):
        self.each(lambda i: self.copy(i).wait_send())

    @staticmethod
    def scratch(planes):
        return pltpu.SemaphoreType.DMA((2, 8 * planes))


class Stream:
    def __init__(self, slots, sems, out):
        self.slots, self.sems, self.out = slots, sems, out
        self.count = 0

    def copy(self, i):
        rows = self.slots.shape[1]
        return pltpu.make_async_copy(
            self.slots.at[i % 2], self.out.at[pl.ds(i * rows, rows)], self.sems.at[i % 2]
        )

    def put(self, value):
        i = self.count
        if i >= 2:
            self.copy(i - 2).wait()
        self.slots[i % 2] = value
        self.copy(i).start()
        self.count = i + 1

    def end(self):
        for i in range(max(self.count - 2, 0), self.count):
            self.copy(i).wait()

    @staticmethod
    def scratch(rows, width, dtype):
        return [pltpu.VMEM((2, rows, width), dtype), pltpu.SemaphoreType.DMA((2,))]


def prologue_kernel(
    shard_ref, cond_ref, ada_ref, ada_bias_ref, g_ref, conds_ref, mods_ref, mod_local, cond_sems, mod_sems, *sems, planes, slots
):
    place = Place(planes)
    weights = Gather(place, shard_ref, g_ref, *sems)
    conds = Exchange(place, cond_ref, conds_ref, cond_sems, True)
    mods = Exchange(place, mod_local, mods_ref, mod_sems, False)
    conds.greet()
    weights.run("begin")
    conds.start()
    mod_local[...] = jnp.zeros_like(mod_local)
    parts = weights.parts()
    for part in parts[1:4]:
        weights.run(part)
    conds.arrive()
    devices, rows, lanes = conds_ref.shape
    d, width = ada_ref.shape
    every = conds_ref[...].reshape(devices * rows, lanes)
    columns = ada_bias_ref[...]
    for j in range(d // lanes):
        piece = dg(every, ada_ref[j * lanes : (j + 1) * lanes, :], NN).reshape(devices, rows, width)
        columns = columns + piece[:, slots * j : slots * (j + 1)]
    mod_local[:, :slots, :width] = columns.astype(BF)
    mods.start()
    for part in parts[4:-1]:
        weights.run(part)
    mods.arrive()
    conds.end()
    mods.end()
    weights.run("end")


def prologue_call(shard, cond, ada, ada_bias, planes, slots):
    devices = 8 * planes
    lanes = up_to(ada.shape[1], 128)
    return pl.pallas_call(
        functools.partial(prologue_kernel, planes=planes, slots=slots),
        out_shape=(
            shape((4, planes, 2) + shard.shape, BF),
            shape((devices,) + cond.shape, BF),
            shape((devices, 16, lanes), BF),
        ),
        in_specs=[ANY_SPEC, VMEM_SPEC, VMEM_SPEC, VMEM_SPEC],
        out_specs=(ANY_SPEC, VMEM_SPEC, VMEM_SPEC),
        scratch_shapes=[pltpu.VMEM((devices, 16, lanes), BF)]
        + [Exchange.scratch(planes)] * 2
        + Gather.scratch(planes),
        compiler_params=params(collective_id=1),
        name="weights_and_modulation",
    )(shard, cond, ada, ada_bias)


def head_window(h, hd, width):
    a = pl.multiple_of(jnp.minimum((h * hd) // 128, (width - WINDOW) // 128) * 128, 128)
    lane = lax.broadcasted_iota(jnp.int32, (1, WINDOW), 1) + a
    return a, (lane >= h * hd) & (lane < h * hd + hd)


QUERY_BIAS, VALUE_BIAS, PROJ_BIAS, DOWN_BIAS, ROUTER = range(5)
SHIFT1, SCALE1, GATE1, SHIFT2, SCALE2, GATE2 = range(6)


def forward_kernel(
    off_ref,
    gate_ref,
    mod_ref,
    vec_ref,
    keep_ref,
    tokens_ref,
    cot_ref,
    g_ref,
    up_ref,
    down_ref,
    lse_ref,
    tg_ref,
    n1_ref,
    qkv_ref,
    w_ref,
    wp_ref,
    att_ref,
    gated_ref,
    attn_ref,
    after_ref,
    n2_ref,
    gm_ref,
    g_up_ref,
    g_down_ref,
    lse_sc,
    g_s,
    tok_s,
    w_s,
    wp_s,
    n1_s,
    qkv_s,
    att_s,
    gated_s,
    cot_s,
    cot_sems,
    sems,
    attn_slots,
    attn_sems,
    after_slots,
    after_sems,
    n2_slots,
    n2_sems,
    gm_slots,
    gm_sems,
    *gather_sems,
    heads,
    blk,
    planes,
):
    t, d = tok_s.shape
    hd = d // heads
    nb = t // blk
    c = hd**-0.5 * LOG2E
    place = Place(planes)
    place.barrier()
    half = len(gather_sems) // 2
    gathers = [
        Gather(place, up_ref, g_up_ref, *gather_sems[:half]),
        Gather(place, down_ref, g_down_ref, *gather_sems[half:]),
    ]
    parts = gathers[0].parts()
    for g in gathers:
        g.run("begin")
    groups = spread_out(
        [functools.partial(g.run, part) for part in parts[1:-1] for g in gathers], 2 * nb + heads
    )

    def run_group(i):
        for step in groups[i]:
            step()

    moves = {
        name: pltpu.make_async_copy(src, dst, sems.at[i])
        for i, (name, src, dst) in enumerate(
            (
                ("g", g_ref, g_s),
                ("tok", tokens_ref, tok_s),
                ("w", w_s, w_ref),
                ("wp", wp_s, wp_ref),
                ("n1", n1_s, n1_ref),
                ("qkv", qkv_s, qkv_ref),
                ("att", att_s, att_ref),
                ("gated", gated_s, gated_ref),
            )
        )
    }

    def cot_copy(i):
        return pltpu.make_async_copy(
            cot_ref.at[pl.ds(i * blk, blk)], cot_s.at[i % 2], cot_sems.at[i % 2]
        )

    moves["g"].start()
    moves["tok"].start()
    for i in range(2):
        cot_copy(i).start()
    devices = g_s.shape[0]
    r = d // devices
    moves["g"].wait()
    for i in range(devices):
        rows = slice(i * r, (i + 1) * r)
        for b in range(3):
            w_s[rows, b * d : (b + 1) * d] = g_s[i, b * r : (b + 1) * r, :]
        wp_s[rows, :] = g_s[i, 3 * r : 4 * r, :]
    moves["w"].start()
    moves["wp"].start()
    moves["tok"].wait()

    def vector(i):
        return vec_ref[i : i + 1, :]

    def mod(i, k):
        return mod_ref[i, k : k + 1, :]

    bias = jnp.concatenate(
        [vector(QUERY_BIAS), jnp.zeros((1, d), F32), vector(VALUE_BIAS)], axis=1
    )
    for i in range(nb):
        rows = slice(i * blk, (i + 1) * blk)
        normed, _ = ln_parts(tok_s[rows, :])
        low = (normed * (1.0 + mod(i, SCALE1)) + mod(i, SHIFT1)).astype(BF)
        n1_s[:, rows] = low.T
        qkv_s[rows, :] = (dg(low, w_s[...], NN) + bias).astype(BF)
        run_group(i)
    moves["n1"].start()
    moves["qkv"].start()
    off = off_ref[0]
    lane128 = lax.broadcasted_iota(jnp.int32, (1, 128), 1)

    def body(h, carry):
        a, mask = head_window(h, hd, d)
        keys = qkv_s[:, pl.ds(pl.multiple_of(d + a, 128), WINDOW)]
        values = qkv_s[:, pl.ds(pl.multiple_of(2 * d + a, 128), WINDOW)]
        cols = pl.ds(a, WINDOW)
        for i in range(nb):
            rows = pl.ds(i * blk, blk)
            q = qkv_s[rows, cols]
            q = jnp.where(mask, q, jnp.zeros_like(q))
            s = dg(q, keys, NT)
            cuts = [s[:, j * blk : (j + 1) * blk] for j in range(nb)]
            own = jnp.max(cuts[i], axis=1, keepdims=True) * c
            others = functools.reduce(jnp.maximum, [cuts[j] for j in range(nb) if j != i])
            m = jnp.maximum(own, jnp.max(others, axis=1, keepdims=True) * c + off)
            m_off = m - off
            ps = [jnp.exp2(cuts[j] * c - (m if j == i else m_off)) for j in range(nb)]
            total = jnp.sum(functools.reduce(jnp.add, ps), axis=1, keepdims=True)
            p = jnp.concatenate([x.astype(BF) for x in ps], axis=1)
            o = dg(p, values, NN) * (1.0 / total)
            og = (o * gate_ref[i, :, cols]).astype(BF)
            att_s[rows, cols] = jnp.where(mask, o, att_s[rows, cols])
            gated_s[rows, cols] = jnp.where(mask, og, gated_s[rows, cols])
            lse_sc[rows, :] = jnp.where(lane128 == h, m + jnp.log2(total), lse_sc[rows, :])
        run_at(h, groups[nb : nb + heads])
        return carry

    lax.fori_loop(0, heads, body, 0)
    moves["att"].start()
    moves["gated"].start()
    lse_ref[...] = lse_sc[...].T[:heads, :]
    streams = [
        Stream(attn_slots, attn_sems, attn_ref),
        Stream(after_slots, after_sems, after_ref),
        Stream(n2_slots, n2_sems, n2_ref),
        Stream(gm_slots, gm_sems, gm_ref),
    ]
    for i in range(nb):
        rows = slice(i * blk, (i + 1) * blk)
        attn = dg(gated_s[rows, :], wp_s[...], NN) + vector(PROJ_BIAS)
        streams[0].put(attn)
        after = tok_s[rows, :] + mod(i, GATE1) * attn
        streams[1].put(after)
        normed, _ = ln_parts(after)
        y = normed * (1.0 + mod(i, SCALE2)) + mod(i, SHIFT2)
        streams[2].put(y.astype(BF))
        token_gate = jax.nn.sigmoid(jnp.sum(y * vector(ROUTER), axis=1, keepdims=True))
        tg_ref[rows, :] = token_gate
        cot_copy(i).wait()
        cot = cot_s[i % 2]
        streams[3].put((cot * (mod(i, GATE2) * (keep_ref[rows, :] * token_gate))).astype(BF))
        if i + 2 < nb:
            cot_copy(i + 2).start()
        run_group(nb + heads + i)
    for g in gathers:
        g.run("end")
    for stream in streams:
        stream.end()
    for name in ("w", "wp", "n1", "qkv", "att", "gated"):
        moves[name].wait()


def forward_call(off, gate_rows, mods, vecs, keep, tokens, cot, g, up, down, heads, blk, planes):
    t, d = tokens.shape
    gathered = shape((4, planes, 2) + up.shape, BF)
    dma = pltpu.SemaphoreType.DMA
    return pl.pallas_call(
        functools.partial(forward_kernel, heads=heads, blk=blk, planes=planes),
        out_shape=(
            shape((heads, t)),
            shape((t, 1)),
            shape((d, t), BF),
            shape((t, 3 * d), BF),
            shape((d, 3 * d), BF),
            shape((d, d), BF),
            shape((t, d)),
            shape((t, d), BF),
            shape((t, d)),
            shape((t, d)),
            shape((t, d), BF),
            shape((t, d), BF),
            gathered,
            gathered,
        ),
        in_specs=[SMEM_SPEC] + [VMEM_SPEC] * 4 + [ANY_SPEC] * 5,
        out_specs=(VMEM_SPEC,) * 2 + (ANY_SPEC,) * 12,
        scratch_shapes=[
            pltpu.VMEM((t, 128), F32),
            pltpu.VMEM(g.shape, BF),
            pltpu.VMEM((t, d), F32),
            pltpu.VMEM((d, 3 * d), BF),
            pltpu.VMEM((d, d), BF),
            pltpu.VMEM((d, t), BF),
            pltpu.VMEM((t, 3 * d), BF),
            pltpu.VMEM((t, d), F32),
            pltpu.VMEM((t, d), BF),
            pltpu.VMEM((2, blk, d), F32),
            dma((2,)),
            dma((8,)),
        ]
        + Stream.scratch(blk, d, F32) * 2
        + Stream.scratch(blk, d, BF) * 2
        + Gather.scratch(planes) * 2,
        compiler_params=params(62, collective_id=2),
        name="attention_and_middle_forward",
    )(off, gate_rows, mods, vecs, keep, tokens, cot, g, up, down)


def backward_kernel(
    off_ref,
    qkv_ref,
    do_ref,
    lse_ref,
    delta_ref,
    n1t_ref,
    gp_ref,
    up_ref,
    down_ref,
    dqkv_ref,
    bias_ref,
    g_up_ref,
    g_down_ref,
    done_ref,
    part_ref,
    kt_sc,
    dqt_sc,
    part_sem,
    *rest,
    heads,
    blk,
    planes,
    cuts,
):
    t, d = do_ref.shape
    hd = d // heads
    nb = t // blk
    scale = hd**-0.5
    c = scale * LOG2E
    width = d // cuts
    devices = 8 * planes
    r = d // devices
    first = planes // 2
    place = Place(planes)
    place.barrier(True)
    slots, rest = rest[: cuts - 1], rest[cuts - 1 :]
    each = 10
    js = list(range(first, planes))

    def kept(ref):
        return lambda j, c: ref.at[:, j - first, c]

    def local(ref):
        return lambda j, c: ref.at[:, lax.rem(place.z + plane_turn(planes, j), planes), c]

    ups = [
        Scatter(place, u, js, kept(ref), *rest[each * u : each * (u + 1)])
        for u, ref in enumerate((up_ref, down_ref))
    ]
    rest = rest[2 * each :]
    each -= 1
    chains = [
        Scatter(
            place, m, list(range(planes)), local(slots[m]), None, *rest[each * m : each * (m + 1)]
        )
        for m in range(cuts - 1)
    ]
    up_steps = scatter_steps(ups)
    chain_steps = [scatter_steps([chain], planes) for chain in chains]
    up_steps[0]()
    ends = [-(-width * (m + 1) // hd) for m in range(cuts)]
    queues = [[] for _ in range(heads + 1)]

    def place_steps(steps, start, first, stop):
        queues[start] += steps[:2]
        for i, step in enumerate(steps[2:]):
            queues[first + i * (stop - first) // max(len(steps) - 3, 1)].append(step)

    place_steps(up_steps[1:], 0, ends[0] + 1, ends[1] + 1)
    for m in range(cuts - 1):
        steps = chain_steps[m][1:]
        place_steps(steps, ends[m], min(ends[m] + 4 - m, heads), min(ends[m] + 7, heads))

    off = off_ref[0]
    kt_sc[...] = qkv_ref[:, d : 2 * d].T

    def body(h, carry, start, end):
        a, mask = head_window(h, hd, d)
        cols = pl.ds(a, WINDOW)
        key_cols = pl.ds(pl.multiple_of(d + a, 128), WINDOW)
        value_cols = pl.ds(pl.multiple_of(2 * d + a, 128), WINDOW)
        keys = qkv_ref[:, key_cols]
        values = qkv_ref[:, value_cols]
        keys_t = kt_sc[cols, :]
        dk_sum = None
        dv_sum = None
        for i in range(nb):
            rows = pl.ds(i * blk, blk)
            span = slice(i * blk, (i + 1) * blk)
            q = qkv_ref[rows, cols]
            q = jnp.where(mask, q, jnp.zeros_like(q))
            do = do_ref[rows, cols]
            do = jnp.where(mask, do, jnp.zeros_like(do))
            lse = lse_ref[pl.ds(h, 1), span]
            delta = delta_ref[pl.ds(h, 1), span]
            s_t = dg(keys, q, NT)
            dp_t = dg(values, do, NT)
            ps = []
            ds = []
            for j in range(nb):
                cut = slice(j * blk, (j + 1) * blk)
                p = jnp.exp2(s_t[cut] * c - (lse if j == i else lse - off))
                ps.append(p.astype(BF))
                ds.append((p * (dp_t[cut] - delta)).astype(BF))
            p = jnp.concatenate(ps, axis=0)
            grad_s = jnp.concatenate(ds, axis=0)
            dv = dg(p, do, NN)
            dk = dg(grad_s, q, NN)
            dv_sum = dv if dv_sum is None else dv_sum + dv
            dk_sum = dk if dk_sum is None else dk_sum + dk
            dqt_sc[:, span] = (dg(keys_t, grad_s, NN) * scale).astype(BF)
        dk = (dk_sum * scale).astype(BF)
        dqkv_ref[:, key_cols] = jnp.where(mask, dk, dqkv_ref[:, key_cols])
        dqkv_ref[:, value_cols] = jnp.where(mask, dv_sum.astype(BF), dqkv_ref[:, value_cols])
        dqkv_ref[:, cols] = jnp.where(mask, dqt_sc[...].T, dqkv_ref[:, cols])
        run_at(h - start, queues[start:end])
        return carry

    def weight_part(m, out):
        dqkv = jnp.concatenate(
            [dqkv_ref[:, b * d + m * width : b * d + (m + 1) * width] for b in range(3)], axis=1
        )
        bias_ref[m] = col_sum(dqkv.astype(F32))
        grad = dg(n1t_ref[...], dqkv, NN).astype(BF)
        for i in range(devices):
            rows = slice(i * r, (i + 1) * r)
            at = (i // (2 * planes), i // 2 % planes, i % 2)
            for b in range(3):
                out[at + (slice(b * r, (b + 1) * r),)] = grad[rows, b * width : (b + 1) * width]
            out[at + (slice(3 * r, 4 * r),)] = gp_ref[rows, m * width : (m + 1) * width]

    for m in range(cuts):
        start = 0 if m == 0 else ends[m - 1]
        lax.fori_loop(start, ends[m], functools.partial(body, start=start, end=ends[m]), 0)
        if m + 1 < cuts:
            weight_part(m, slots[m])
            chain_steps[m][0]()
    for j in chains[0].js:
        chains[0].sent(1, j)
    weight_part(cuts - 1, slots[0])
    keep = pltpu.make_async_copy(slots[0], part_ref, part_sem)
    keep.start()
    for step in queues[heads]:
        step()
    g_up_ref[...] = ups[0].total()
    g_down_ref[...] = ups[1].total()
    for m, chain in enumerate(chains):
        stages = (2, 3, 4) if m == 0 else (1, 2, 3, 4)
        done_ref[:, m * width : (m + 1) * width] = chain.total(stages)
    keep.wait()


def backward_call(off, qkv, do, lse, delta, n1t, g_proj, up, down, heads, blk, planes, cuts):
    t, d = do.shape
    rows, cols = up.shape[3:]
    width = d // cuts
    part = (4, planes, 2, up_to(4 * d // (8 * planes), 16), width)
    return pl.pallas_call(
        functools.partial(backward_kernel, heads=heads, blk=blk, planes=planes, cuts=cuts),
        out_shape=(
            shape((t, 3 * d), BF),
            shape((cuts, 1, 3 * width)),
            shape((rows, cols)),
            shape((rows, cols)),
            shape((part[3], (cuts - 1) * width)),
            shape(part, BF),
        ),
        in_specs=[SMEM_SPEC] + [VMEM_SPEC] * 6 + [ANY_SPEC] * 2,
        out_specs=(VMEM_SPEC,) * 5 + (ANY_SPEC,),
        scratch_shapes=[
            pltpu.VMEM((d, t), BF),
            pltpu.VMEM((WINDOW, t), BF),
            pltpu.SemaphoreType.DMA(()),
        ]
        + [pltpu.VMEM(part, BF)] * (cuts - 1)
        + Scatter.scratch(planes - planes // 2, rows, cols) * 2
        + Scatter.scratch(planes, part[3], width, False) * (cuts - 1),
        compiler_params=params(63, collective_id=3),
        name="attention_backward",
    )(off, qkv, do, lse, delta, n1t, g_proj, up, down)


def mlp_kernel(
    n2_ref,
    gm_ref,
    b1_ref,
    cs_ref,
    g1_ref,
    g2_ref,
    mlp_ref,
    gn2_ref,
    gb1_ref,
    gch_ref,
    o1_ref,
    o2_ref,
    p1_ref,
    p2_ref,
    g1_s,
    g2_s,
    w1_s,
    w2_s,
    sc_s,
    gp_s,
    p1_s,
    p2_s,
    g_sems,
    p_sems,
    *rest,
    blk,
    planes,
):
    t, d = n2_ref.shape
    nb = t // blk
    hidden = w1_s.shape[0]
    quarter = hidden // 8
    piece = d // 4
    j = pl.program_id(0)
    place = Place(planes)
    hosted = planes // 2
    half = len(rest) // 2
    scatters = [
        Scatter(place, u, list(range(hosted)), lambda j, c, p=p: p.at[:, c], None, *scratch)
        for u, (p, scratch) in enumerate(((p1_s, rest[:half]), (p2_s, rest[half:])))
    ]

    def loads(step):
        plane = lax.rem(place.z + plane_turn(planes, step), planes)
        return [
            pltpu.make_async_copy(g.at[:, plane], slot, g_sems.at[i])
            for i, (g, slot) in enumerate(((g1_ref, g1_s), (g2_ref, g2_s)))
        ]

    def keeps(step):
        return [
            pltpu.make_async_copy(slot, p.at[:, step - hosted], p_sems.at[i])
            for i, (slot, p) in enumerate(((p1_s, p1_ref), (p2_s, p2_ref)))
        ]

    def early(step):
        for s in scatters:
            if step - 1 < hosted:
                s.take(1, step - 1)
                s.issue(2, step - 1)
        for s in scatters:
            if 0 <= step - 2 < hosted:
                s.take(3, step - 2)

    def late(step):
        for s in scatters:
            if step - 1 < hosted:
                s.take(2, step - 1)
                s.issue(3, step - 1)
                s.sent(1, step - 1)
        if step - 1 >= hosted:
            for copy in keeps(step - 1):
                copy.wait()

    def at_steps(do):
        for step in range(1, planes):
            pl.when(j == step)(functools.partial(do, step))

    def places():
        for c in range(2):
            for k in range(4):
                yield c, slice((4 * c + k) * quarter, (4 * c + k + 1) * quarter), k

    @pl.when(j == 0)
    def _():
        for copy in loads(0):
            copy.start()
        place.barrier(True)
        mlp_ref[...] = jnp.zeros_like(mlp_ref)
        gn2_ref[...] = jnp.zeros_like(gn2_ref)

    for copy in loads(j):
        copy.wait()
    for c, rows, k in places():
        cols = slice(k * piece, (k + 1) * piece)
        for w, g in ((w1_s, g1_s), (w2_s, g2_s)):
            w[rows, :] = jnp.concatenate([g[n, c, :quarter, cols] for n in range(4)], axis=1)

    @pl.when(j + 1 < planes)
    def _():
        for copy in loads(j + 1):
            copy.start()

    at_steps(early)
    w1 = w1_s[...]
    w2 = w2_s[...]
    grad_bias = None
    for i in range(nb):
        rows = slice(i * blk, (i + 1) * blk)
        pre = dg(n2_ref[rows, :], w1, NT) + b1_ref[0]
        grad_scaled = dg(gm_ref[rows, :], w2, NT)
        act, slope = gelu_parts(pre)
        gate = cs_ref[0, i : i + 1]
        scaled = (act * gate).astype(BF)
        grad_pre = (grad_scaled * gate * slope).astype(BF)
        gch_ref[0, i : i + 1] = col_sum(grad_scaled * act)
        part = col_sum(grad_pre.astype(F32))
        grad_bias = part if grad_bias is None else grad_bias + part
        sc_s[rows, :] = scaled
        gp_s[rows, :] = grad_pre
        mlp_ref[rows, :] += dg(scaled, w2, NN)
        gn2_ref[rows, :] += dg(grad_pre, w1, NN)
    gb1_ref[0] = grad_bias

    at_steps(late)
    for left, right, out in ((gp_s, n2_ref, p1_s), (sc_s, gm_ref, p2_s)):
        grad = dg(left[...], right[...], TN).astype(BF)
        for c, rows, k in places():
            for n in range(4):
                out[n, c, :quarter, k * piece : (k + 1) * piece] = grad[rows, n * piece : (n + 1) * piece]
    for step in range(planes):

        @pl.when(j == step)
        def _(step=step):
            if step < hosted:
                for s in scatters:
                    s.issue(1, step)
            else:
                for copy in keeps(step):
                    copy.start()

    @pl.when(j == planes - 1)
    def _():
        o1_ref[...] = scatters[0].total((2, 3, 4))
        o2_ref[...] = scatters[1].total((2, 3, 4))
        for copy in keeps(planes - 1):
            copy.wait()


def mlp_call(n2, gm, g1, g2, b1, gates, blk):
    t, d = n2.shape
    planes, rows = g1.shape[1], g1.shape[3]
    nb, ff = gates.shape
    hb = ff // planes
    hosted = planes // 2

    def turn(j):
        return lax.rem(lax.axis_index("wide") // 2 + plane_turn(planes, j), planes)

    b_spec = pl.BlockSpec((1, 1, hb), lambda j: (turn(j), 0, 0))
    c_spec = pl.BlockSpec((1, nb, hb), lambda j: (turn(j), 0, 0))
    kept = shape((4, planes - hosted, 2, rows, d), BF)
    dma = pltpu.SemaphoreType.DMA
    mlp, gn2, gb1, gch, o1, o2, p1, p2 = pl.pallas_call(
        functools.partial(mlp_kernel, blk=blk, planes=planes),
        grid=(planes,),
        out_shape=(
            shape((t, d)),
            shape((t, d)),
            shape((planes, 1, hb)),
            shape((planes, nb, hb)),
            shape((rows, d)),
            shape((rows, d)),
            kept,
            kept,
        ),
        in_specs=[whole(t, d), whole(t, d), b_spec, c_spec, ANY_SPEC, ANY_SPEC],
        out_specs=(whole(t, d), whole(t, d), b_spec, c_spec, whole(rows, d), whole(rows, d))
        + (ANY_SPEC,) * 2,
        scratch_shapes=[pltpu.VMEM((4, 2, rows, d), BF)] * 2
        + [pltpu.VMEM((hb, d), BF)] * 2
        + [pltpu.VMEM((t, hb), BF)] * 2
        + [pltpu.VMEM((4, 2, rows, d), BF)] * 2
        + [dma((2,))] * 2
        + Scatter.scratch(hosted, rows, d, False) * 2,
        compiler_params=params(62, collective_id=5),
        name="feed_forward",
    )(n2, gm, b1.reshape(planes, 1, hb), gates.reshape(nb, planes, hb).transpose(1, 0, 2), g1, g2)
    return mlp, gn2, o1, o2, p1, p2, gb1.reshape(ff), gch.transpose(1, 0, 2).reshape(nb, ff)


def middle_back_kernel(
    mlp_ref,
    gn2_ref,
    after_ref,
    attn_ref,
    cot_ref,
    gm_ref,
    gated_ref,
    att_ref,
    tg_ref,
    keep_ref,
    w_ref,
    vec_ref,
    table_ref,
    head_ref,
    out_ref,
    ga_ref,
    do_ref,
    delta_ref,
    gw_ref,
    mod_ref,
    sums_ref,
    gw_s,
    *,
    heads,
):
    d = after_ref.shape[1]
    hd = d // heads
    first = pl.program_id(0) == 0
    after = after_ref[...]
    cot = cot_ref[...]
    gate2 = table_ref[0, GATE2 : GATE2 + 1]
    tg = tg_ref[...]
    keep = keep_ref[...]
    normed, rstd = ln_parts(after)
    scale2 = table_ref[0, SCALE2 : SCALE2 + 1]
    y = normed * (1.0 + scale2) + table_ref[0, SHIFT2 : SHIFT2 + 1]
    mlp_out = mlp_ref[...] + vec_ref[DOWN_BIAS : DOWN_BIAS + 1]
    open_gate = keep * tg
    out_ref[...] = after + (gate2 * open_gate) * mlp_out
    weighted = cot * mlp_out
    grad_tg = jnp.sum(weighted * gate2, axis=1, keepdims=True) * keep
    coef = grad_tg * tg * (1.0 - tg)
    gy = gn2_ref[...] + coef * vec_ref[ROUTER : ROUTER + 1]
    ga = cot + ln_back(gy, normed, rstd, scale2)
    ga_ref[...] = ga
    attn = attn_ref[...]
    g_attn = (ga * table_ref[0, GATE1 : GATE1 + 1]).astype(BF)
    mod_ref[0] = jnp.concatenate(
        [col_sum(ga * attn), col_sum(gy), col_sum(gy * normed), col_sum(weighted * open_gate)], axis=0
    )
    sums = jnp.concatenate(
        [
            col_sum(coef * y),
            col_sum(g_attn.astype(F32)),
            col_sum(gm_ref[...].astype(F32)),
        ],
        axis=0,
    )
    g_gated = dg(g_attn, w_ref[...], NT)
    att = att_ref[...]
    mod_ref[1] = jnp.concatenate([col_sum(g_gated * att), jnp.zeros((3, d), F32)], axis=0)
    do = (g_gated * head_ref[0]).astype(BF)
    do_ref[...] = do
    lane = lax.broadcasted_iota(jnp.int32, (heads, d), 1)
    head = lax.broadcasted_iota(jnp.int32, (heads, d), 0) * hd
    pick = jnp.where((lane >= head) & (lane < head + hd), 1.0, 0.0)
    delta_ref[...] = lax.dot_general(
        pick, do.astype(F32) * att, NT, precision=HIGHEST, preferred_element_type=F32
    )
    gw = dg(gated_ref[...], g_attn, TN)

    @pl.when(first)
    def _():
        sums_ref[...] = sums
        gw_s[...] = gw

    @pl.when(jnp.logical_not(first))
    def _():
        sums_ref[...] += sums
        gw_s[...] += gw

    @pl.when(pl.program_id(0) == pl.num_programs(0) - 1)
    def _():
        gw_ref[...] = gw_s[...].astype(BF)


def middle_back_call(
    mlp, gn2, after, attn, cot, gm, gated, att, tg, keep, w, vecs, table, head_rows, heads, blk
):
    t, d = after.shape
    nb = t // blk
    r, v, column = rows_of(blk, d), row_vec(d), rows_of(blk, 1)
    return pl.pallas_call(
        functools.partial(middle_back_kernel, heads=heads),
        grid=(nb,),
        out_shape=(
            shape((t, d)),
            shape((t, d)),
            shape((t, d), BF),
            shape((heads, t)),
            shape((d, d), BF),
            shape((nb * 2, 4, d)),
            shape((3, d)),
        ),
        in_specs=[r] * 8 + [column, column, whole(d, d), whole(*vecs.shape)]
        + [pl.BlockSpec((1,) + table.shape[1:], lambda i: (i, 0, 0)), v],
        out_specs=(
            r,
            r,
            r,
            pl.BlockSpec((heads, blk), lambda i: (0, i)),
            whole(d, d),
            pl.BlockSpec((2, 4, d), lambda i: (i, 0, 0)),
            whole(3, d),
        ),
        scratch_shapes=[pltpu.VMEM((d, d), F32)],
        compiler_params=params(),
        name="middle_backward",
    )(mlp, gn2, after, attn, cot, gm, gated, att, tg, keep, w, vecs, table, head_rows)


def final_kernel(
    single_ref,
    table_ref,
    mods_ref,
    sums_ref,
    logits_ref,
    conds_ref,
    part_ref,
    dqkv_ref,
    w_ref,
    tokens_ref,
    ga_ref,
    out_ref,
    sum_ref,
    ada_ref,
    ada_bias_ref,
    router_ref,
    logit_ref,
    grad_ref,
    all_sums,
    own_mods,
    all_mods,
    all_logits,
    w_s,
    dq_s,
    tok_s,
    ga_s,
    w_sem,
    in_sems,
    out_slots,
    out_sems,
    mod_sems,
    logit_sems,
    *rest,
    planes,
    blk,
):
    place = Place(planes)
    mods = Exchange(place, own_mods, all_mods, mod_sems, False)
    logits = Exchange(place, logits_ref, all_logits, logit_sems, True)

    def source(j, c):
        return part_ref.at[:, lax.rem(place.z + plane_turn(planes, j), planes), c]

    sums = Gather(place, sums_ref, all_sums, *rest[:6])
    chain = Scatter(place, 0, list(range(planes)), source, *rest[6:])
    t, d = tokens_ref.shape
    nb = t // blk
    w_load = pltpu.make_async_copy(w_ref, w_s, w_sem)

    def loads(i):
        rows = pl.ds(i * blk, blk)
        return [
            pltpu.make_async_copy(src.at[rows], dst.at[i % 2], in_sems.at[k, i % 2])
            for k, (src, dst) in enumerate(((dqkv_ref, dq_s), (tokens_ref, tok_s), (ga_ref, ga_s)))
        ]

    w_load.start()
    for copy in loads(0) + loads(1):
        copy.start()
    mods.greet()
    steps = scatter_steps([chain], planes)
    steps[0]()
    sums.run("begin")
    logits.start()
    own_mods[...] = jnp.zeros_like(own_mods)
    out = Stream(out_slots, out_sems, grad_ref)
    tables = []

    def block(i):
        if i == 0:
            w_load.wait()
        for copy in loads(i):
            copy.wait()
        gy = dg(dq_s[i % 2], w_s[...], NT)
        normed, rstd = ln_parts(tok_s[i % 2])
        out.put(ga_s[i % 2] + ln_back(gy, normed, rstd, table_ref[i, SCALE1 : SCALE1 + 1]))
        tables.append([col_sum(gy), col_sum(gy * normed)] + [mods_ref[i, k : k + 1] for k in range(4)])
        if i + 2 < nb:
            for copy in loads(i + 2):
                copy.start()

    def exchange():
        single = single_ref[0]
        devices = own_mods.shape[0]
        width = ada_bias_ref.shape[1]
        flat = [jnp.concatenate(row, axis=1) for row in tables]
        rows = [(1.0 - single) * row for row in flat]
        rows[0] = flat[0] + single * functools.reduce(jnp.add, flat[1:])
        every = jnp.concatenate(rows, axis=0).astype(BF)
        for i in range(devices):
            own_mods[i, :nb, :width] = every[:, i * width : (i + 1) * width]
        mods.start()

    def products():
        mods.arrive()
        logits.arrive()
        devices, rows, _ = conds_ref.shape
        conds = conds_ref[...].reshape(devices * rows, d)
        got = all_mods[...].reshape(devices * rows, -1)
        columns = ada_bias_ref.shape[1]
        ada_ref[...] = dg(conds, got, TN)[:, :columns]
        ada_bias_ref[...] = col_sum(got.astype(F32))[:, :columns]
        got = all_logits[...].reshape(devices * rows, -1)
        router_ref[...] = lax.dot_general(
            conds.astype(F32), got, TN, precision=HIGHEST, preferred_element_type=F32
        )
        logit_ref[...] = col_sum(got)

    parts = [functools.partial(sums.run, part) for part in sums.parts()[1:-1]]
    rest = steps[3:]
    work = [
        [functools.partial(block, 0)],
        steps[1:3],
        [functools.partial(block, i) for i in range(1, nb - 1)],
        rest[:1],
        [functools.partial(block, nb - 1), exchange],
        rest[1:],
    ]
    work = [do for group in work for do in group]
    for do, group in zip(work, spread_out(parts, len(work))):
        do()
        for part in group:
            part()
    products()
    sums.run("end")
    sum_ref[...] = jnp.sum(all_sums[...].reshape((8 * planes,) + sum_ref.shape), axis=0)
    out_ref[...] = chain.total()
    out.end()
    mods.end()
    logits.end()


def final_call(single, table, mods, sums, logits, conds, part, dqkv, w, tokens, ga, mod_width, planes, blk):
    rows, width = part.shape[3:]
    t, d = tokens.shape
    devices = 8 * planes
    spread = (4, planes, 2)
    blocks = (devices, conds.shape[1], up_to(mod_width, 128))
    dma = pltpu.SemaphoreType.DMA
    return pl.pallas_call(
        functools.partial(final_kernel, planes=planes, blk=blk),
        out_shape=(
            shape((rows, width)),
            shape(sums.shape),
            shape((d, mod_width)),
            shape((1, mod_width)),
            shape((d, logits.shape[1])),
            shape((1, logits.shape[1])),
            shape((t, d)),
        ),
        in_specs=[SMEM_SPEC] + [VMEM_SPEC] * 5 + [ANY_SPEC] * 5,
        out_specs=(VMEM_SPEC,) * 6 + (ANY_SPEC,),
        scratch_shapes=[
            pltpu.VMEM(spread + sums.shape, F32),
            pltpu.VMEM(blocks, BF),
            pltpu.VMEM(blocks, BF),
            pltpu.VMEM((devices,) + logits.shape, F32),
            pltpu.VMEM(w.shape, BF),
            pltpu.VMEM((2, blk, 3 * d), BF),
            pltpu.VMEM((2, blk, d), F32),
            pltpu.VMEM((2, blk, d), F32),
            dma(()),
            dma((3, 2)),
        ]
        + Stream.scratch(blk, d, F32)
        + [Exchange.scratch(planes)] * 2
        + Gather.scratch(planes)
        + Scatter.scratch(planes, rows, width),
        compiler_params=params(collective_id=4),
        name="last_sums",
    )(single, table, mods, sums, logits, conds, part, dqkv, w, tokens, ga)


def on_device(
    planes,
    tokens,
    conditioning,
    row_items,
    head_mask,
    chan_mask,
    skip_mask,
    ada_weight,
    ada_bias,
    qkv_weight,
    query_bias,
    value_bias,
    proj_weight,
    proj_bias,
    fc1_weight,
    fc1_bias,
    fc2_weight,
    fc2_bias,
    head_router,
    head_router_bias,
    chan_router,
    chan_router_bias,
    token_router,
    cotangent,
):
    t, d = tokens.shape
    slots = conditioning.shape[0]
    heads = head_mask.shape[1]
    groups = chan_mask.shape[1]
    hidden = fc1_bias.shape[0]
    hd = d // heads
    unit = hidden // groups
    blk = t // slots
    single = row_items[0] == 1
    off = jnp.where(single, 0.0, MASKED).astype(F32).reshape(1)

    def per_block(table):
        return jnp.where(single, table[:1], table)

    def per_slot(blocks):
        total = jnp.sum(blocks, axis=0, keepdims=True)
        first = (jnp.arange(slots) == 0).reshape((slots,) + (1,) * (blocks.ndim - 1))
        return jnp.where(single, jnp.where(first, total, 0.0), blocks)

    devices = 8 * planes
    def pack_rows(*blocks):
        return pad_rows(jnp.concatenate(blocks, axis=0))

    def pack_piece(weight):
        rows, cols = weight.shape
        return pad_rows(weight.reshape(4, rows // 4, cols).transpose(1, 0, 2).reshape(rows // 4, d))

    def unpack_piece(piece, rows):
        cols = d // 4
        return piece[: rows // 4].reshape(rows // 4, 4, cols).transpose(1, 0, 2).reshape(rows, cols)

    silu_cond = jax.nn.silu(conditioning.astype(F32)).astype(BF)
    shard = pack_rows(qkv_weight[:, :d], qkv_weight[:, d : 2 * d], qkv_weight[:, 2 * d :], proj_weight)
    conds_pad = pad_rows(silu_cond.reshape(slots, -1, 128).transpose(1, 0, 2).reshape(-1, 128))
    g_attn, conds, mod_columns = prologue_call(
        shard, conds_pad, ada_weight, ada_bias.astype(F32)[None], planes, slots
    )
    mod_width = ada_bias.shape[0]
    every_cond = conds[:, : slots * d // 128].reshape(devices, -1, slots, 128).transpose(0, 2, 1, 3)
    every_cond = jnp.pad(
        every_cond.reshape(devices, slots, d), ((0, 0), (0, up_to(slots, 16) - slots), (0, 0))
    )
    modulation = mod_columns[:, :slots, :mod_width].transpose(1, 0, 2).reshape(slots, 6, d)
    table = per_block(modulation.astype(F32))
    def router(weight, bias, mask):
        gate = jax.nn.sigmoid(dg(silu_cond, weight, NN) + bias.astype(F32))
        mask = mask.astype(F32)
        return mask * gate, mask * gate * (1.0 - gate)

    head_gate, head_slope = router(head_router, head_router_bias, head_mask)
    chan_gate, chan_slope = router(chan_router, chan_router_bias, chan_mask)
    head_rows = jnp.repeat(per_block(head_gate), hd, axis=1)[:, None, :]
    chan_rows = jnp.repeat(per_block(chan_gate), unit, axis=1)
    keep = (1.0 - skip_mask.astype(F32))[:, None]

    vecs = jnp.concatenate([query_bias, value_bias, proj_bias, fc2_bias, token_router])
    vecs = vecs.astype(F32).reshape(5, d)
    lse, tg, n1t, qkv, full_qkv, full_proj, att, gated, attn, after, n2, gm, g_up, g_down = forward_call(
        off,
        head_rows,
        table,
        vecs,
        keep,
        tokens,
        cotangent,
        g_attn.reshape((devices,) + shard.shape),
        pack_piece(fc1_weight),
        pack_piece(fc2_weight),
        heads,
        blk,
        planes,
    )
    mlp, gn2, o_up, o_down, p_up, p_down, gb1, gch = mlp_call(
        n2, gm, g_up, g_down, fc1_bias.astype(F32), chan_rows, blk
    )
    output, ga, do, delta, g_proj, mods, sums = middle_back_call(
        mlp,
        gn2,
        after,
        attn,
        cotangent,
        gm,
        gated,
        att,
        tg,
        keep,
        full_proj,
        vecs,
        table,
        head_rows,
        heads,
        blk,
    )
    mods = mods.reshape(slots, 8, d)
    dqkv, qkv_sums, g_up, g_down, g_done, part = backward_call(
        off, qkv, do, lse, delta, n1t, g_proj, p_up, p_down, heads, blk, planes, 3
    )
    qkv_sums = qkv_sums.reshape(3, 3, d // 3).transpose(1, 0, 2).reshape(3, d)
    g_head = per_slot(jnp.sum(mods[:, 4].reshape(slots, heads, hd), axis=2)) * head_slope
    g_chan = per_slot(jnp.sum(gch.reshape(slots, groups, unit), axis=2)) * chan_slope
    logits = jnp.pad(
        jnp.concatenate([g_head, g_chan], axis=1),
        ((0, up_to(slots, 16) - slots), (0, up_to(heads + groups, 128) - heads - groups)),
    )
    vector = jnp.concatenate([qkv_sums[0], qkv_sums[2], sums[1], gb1, sums[2], sums[0]])
    length = vector.shape[0]
    vector = jnp.pad(vector, (0, up_to(length, 1024) - length)).reshape(-1, 128)
    g_last, small, grad_ada_weight, grad_ada_bias, router_grads, logit_sums, grad_tokens = final_call(
        jnp.where(single, 1.0, 0.0).astype(F32).reshape(1),
        table,
        mods,
        vector,
        logits,
        every_cond,
        part,
        dqkv,
        full_qkv,
        tokens,
        ga,
        mod_width,
        planes,
        blk,
    )
    g_attn = jnp.concatenate([g_done, g_last], axis=1)
    g_attn = g_attn[: 4 * (d // devices)].reshape(4, d // devices, d)
    small = small.reshape(-1)[:length]
    grad_ada_bias = grad_ada_bias[0]
    logit_sums = logit_sums[0]
    ends = [d, 2 * d, 3 * d, 3 * d + hidden, 4 * d + hidden]
    g_query, g_value, g_proj_bias, g_b1, g_b2, g_router = jnp.split(small, ends)
    return (
        output,
        grad_tokens,
        grad_ada_weight,
        grad_ada_bias,
        g_attn[:3].transpose(1, 0, 2).reshape(d // devices, 3 * d),
        g_query,
        g_value,
        g_attn[3],
        g_proj_bias,
        unpack_piece(g_up + o_up, fc1_weight.shape[0]),
        g_b1,
        unpack_piece(g_down + o_down, fc2_weight.shape[0]),
        g_b2,
        router_grads[:, :heads],
        logit_sums[:heads],
        router_grads[:, heads : heads + groups],
        logit_sums[heads : heads + groups],
        g_router,
    )


def solution(mesh):
    planes = mesh.shape["wide"] // 2
    return jax.shard_map(
        functools.partial(on_device, planes),
        mesh=mesh,
        in_specs=(
            P(("narrow", "wide"), None),
            P(("narrow", "wide"), None),
            P(("narrow", "wide")),
            P(("narrow", "wide"), None),
            P(("narrow", "wide"), None),
            P(("narrow", "wide")),
            P(None, ("narrow", "wide")),
            P(("narrow", "wide")),
            P(("narrow", "wide"), None),
            P(),
            P(),
            P(("narrow", "wide"), None),
            P(),
            P("wide", "narrow"),
            P(),
            P("wide", "narrow"),
            P(),
            P(),
            P(),
            P(),
            P(),
            P(),
            P(("narrow", "wide"), None),
        ),
        out_specs=(
            P(("narrow", "wide"), None),
            P(("narrow", "wide"), None),
            P(None, ("narrow", "wide")),
            P(("narrow", "wide")),
            P(("narrow", "wide"), None),
            P(),
            P(),
            P(("narrow", "wide"), None),
            P(),
            P("wide", "narrow"),
            P(),
            P("wide", "narrow"),
            P(),
            P(),
            P(),
            P(),
            P(),
            P(),
        ),
        check_vma=False,
    )
```

```python
import functools

import jax
import jax.numpy as jnp
from jax import lax
from jax.experimental import pallas as pl
from jax.experimental.pallas import tpu as pltpu
from jax.sharding import PartitionSpec as P

HIGHEST = lax.Precision.HIGHEST
F32 = jnp.float32
BF = jnp.bfloat16
EPSILON = 1e-06
MASKED = -1e30
LOG2E = 1.4426950408889634
WINDOW = 256
NN = (((1,), (0,)), ((), ()))
NT = (((1,), (1,)), ((), ()))
TN = (((0,), (0,)), ((), ()))
VMEM_SPEC = pl.BlockSpec(memory_space=pltpu.VMEM)
ANY_SPEC = pl.BlockSpec(memory_space=pl.ANY)
MESH = pl.DeviceIdType.MESH
SMEM_SPEC = pl.BlockSpec(memory_space=pltpu.SMEM)


def dg(a, b, dims):
    return lax.dot_general(a, b, dims, preferred_element_type=F32)


def params(mib=60, collective_id=None):
    if collective_id is None:
        return pltpu.CompilerParams(vmem_limit_bytes=mib << 20)
    return pltpu.CompilerParams(
        vmem_limit_bytes=mib << 20, collective_id=collective_id, has_side_effects=True
    )


def up_to(count, multiple):
    return -(-count // multiple) * multiple


def pad_rows(x):
    return jnp.pad(x, ((0, up_to(x.shape[0], 16) - x.shape[0]), (0, 0)))


def spread_out(steps, count):
    groups = [[] for _ in range(count)]
    for i, step in enumerate(steps):
        groups[i * count // len(steps)].append(step)
    return groups


def run_at(index, groups):
    for i, group in enumerate(groups):
        if group:

            @pl.when(index == i)
            def _(group=group):
                for step in group:
                    step()


def shape(dims, dtype=F32):
    return jax.ShapeDtypeStruct(dims, dtype)


def whole(*dims):
    return pl.BlockSpec(dims, lambda i: (0,) * len(dims), pipeline_mode=pl.Buffered(1))


def rows_of(block, width):
    return pl.BlockSpec((block, width), lambda i: (i, 0))


def row_vec(width):
    return pl.BlockSpec((1, 1, width), lambda i: (i, 0, 0))


def ln_parts(x):
    centered = x - jnp.mean(x, axis=-1, keepdims=True)
    rstd = lax.rsqrt(jnp.mean(centered * centered, axis=-1, keepdims=True) + EPSILON)
    return centered * rstd, rstd


def ln_back(grad_y, normed, rstd, scale):
    m = grad_y * (1.0 + scale)
    mean_m = jnp.mean(m, axis=-1, keepdims=True)
    mean_mn = jnp.mean(m * normed, axis=-1, keepdims=True)
    return (m - mean_m - normed * mean_mn) * rstd


def col_sum(x):
    return jnp.sum(x, axis=0, keepdims=True)


def gelu_parts(x):
    k0 = 0.7978845608028654
    k1 = 0.044715
    x2 = x * x
    t = jnp.tanh(k0 * x * (1.0 + k1 * x2))
    half = 0.5 * (1.0 + t)
    return x * half, half + 0.5 * x * (1.0 - t * t) * (k0 * (1.0 + 3.0 * k1 * x2))


class Place:
    def __init__(self, planes):
        self.planes = planes
        self.n = lax.axis_index("narrow")
        w = lax.axis_index("wide")
        self.z = w // 2
        self.c = w % 2
        self.xn = self.n + 1 - 2 * (self.n % 2)
        self.yn = self.n + 2 - 4 * (self.n // 2)
        self.dn = 3 - self.n

    def dev(self, n, z, c):
        return (n, z * 2 + c)

    def barrier(self, every_plane=False):
        sem = pltpu.get_barrier_semaphore()

        def greet(n, z, c):
            pl.semaphore_signal(sem, inc=1, device_id=self.dev(n, z, c), device_id_type=MESH)

        greet(self.xn, self.z, self.c)
        greet(self.yn, self.z, self.c)
        greet(self.n, self.z, 1 - self.c)
        if every_plane:
            for k in range(1, self.planes):
                greet(self.n, lax.rem(self.z + k, self.planes), self.c)
            pl.semaphore_wait(sem, self.planes + 2)
            return
        for step in (-1, 1):

            @pl.when(self.has(step))
            def _(step=step):
                greet(self.n, self.z + step, self.c)

        ends = jnp.where(self.z > 0, 1, 0) + jnp.where(self.z < self.planes - 1, 1, 0)
        pl.semaphore_wait(sem, 3 + ends)

    def has(self, step):
        return self.z + step >= 0 if step < 0 else self.z + step < self.planes


def plane_turn(planes, j):
    order = sorted(range(1, planes), key=lambda k: (-min(k, planes - k), k)) + [0]
    if isinstance(j, int):
        return order[j]
    return sum(jnp.where(j == i, k, 0) for i, k in enumerate(order))


def remote(src, dst, sems, idx, device):
    return pltpu.make_async_remote_copy(
        src_ref=src,
        dst_ref=dst,
        send_sem=sems.at[0, idx],
        recv_sem=sems.at[1, idx],
        device_id=device,
        device_id_type=MESH,
    )


class Gather:
    def __init__(self, place, src, out, own, zs, xs, ys, ds, cs):
        self.p, self.src, self.out = place, src, out
        self.own, self.zs, self.xs, self.ys, self.ds, self.cs = own, zs, xs, ys, ds, cs
        self.steps = [0]
        for k in range(1, place.planes):
            self.steps += [-k, k]

    def index(self, k):
        return k + self.p.planes - 1

    def at(self, n, k, c=None):
        p = self.p
        return self.out.at[n, p.z + k, p.c if c is None else c]

    def mine(self, k):
        return self.src if k == 0 else self.at(self.p.n, k)

    def via(self, k):
        p = self.p
        return (p.xn, p.yn) if k % 2 == 0 else (p.yn, p.xn)

    def copy(self, kind, k):
        p = self.p
        i = self.index(k)
        if kind == "x":
            return remote(self.mine(k), self.at(p.n, k), self.xs, i, p.dev(p.xn, p.z, p.c))
        if kind == "y":
            return remote(self.mine(k), self.at(p.n, k), self.ys, i, p.dev(p.yn, p.z, p.c))
        if kind == "d":
            via, to = self.via(k)
            return remote(self.at(via, k), self.at(via, k), self.ds, i, p.dev(to, p.z, p.c))
        if kind == "up" or kind == "down":
            step = 1 if kind == "up" else -1
            j = self.index(k - step)
            return remote(self.mine(k), self.at(p.n, k), self.zs, j, p.dev(p.n, p.z + step, p.c))
        j = ("c", "C", "d2", "D").index(kind)
        n = (p.n, p.xn, p.yn, p.dn)[j]
        shard = self.mine(k) if j == 0 else self.at(n, k)
        slot = j * (2 * p.planes - 1) + i
        return remote(shard, self.at(n, k), self.cs, slot, p.dev(p.n, p.z, 1 - p.c))

    def arrived(self, n, k, sems, idx, c=None):
        p = self.p
        dst = self.at(n, k, c)
        remote(dst, dst, sems, idx, p.dev(p.xn, p.z, p.c)).wait_recv()

    def run(self, part):
        if part == "begin":
            pltpu.make_async_copy(self.src, self.at(self.p.n, 0), self.own).start()
            self.spread(0)
        elif part == "end":
            pltpu.make_async_copy(self.src, self.at(self.p.n, 0), self.own).wait()
            for k in self.steps:
                self.when(self.p.has(k), functools.partial(self.finish, k))
        else:
            kind, k = part
            self.when(self.p.has(k), functools.partial(getattr(self, kind), k))

    def when(self, cond, do):
        pl.when(cond)(do)

    def onward(self, k, act):
        p = self.p
        if k <= 0:
            self.when(p.has(1), lambda: act(self.copy("up", k)))
        if k >= 0:
            self.when(p.has(-1), lambda: act(self.copy("down", k)))

    def spread(self, k):
        self.onward(k, lambda copy: copy.start())
        self.copy("x", k).start()
        self.copy("y", k).start()
        self.copy("c", k).start()

    def plane(self, k):
        self.arrived(self.p.n, k, self.zs, self.index(k))
        self.spread(k)

    def near(self, k):
        p = self.p
        self.arrived(p.xn, k, self.xs, self.index(k))
        if k % 2 == 0:
            self.copy("d", k).start()
        self.copy("C", k).start()
        self.arrived(p.yn, k, self.ys, self.index(k))
        if k % 2 == 1:
            self.copy("d", k).start()
        self.copy("d2", k).start()

    def far(self, k):
        self.arrived(self.p.dn, k, self.ds, self.index(k))
        self.copy("D", k).start()

    def finish(self, k):
        p = self.p
        for j, n in enumerate((p.n, p.xn, p.yn, p.dn)):
            self.arrived(n, k, self.cs, j * (2 * p.planes - 1) + self.index(k), 1 - p.c)
        for kind in ("x", "y", "d", "c", "C", "d2", "D"):
            self.copy(kind, k).wait_send()
        self.onward(k, lambda copy: copy.wait_send())

    def parts(self):
        found = ["begin"]
        rounds = [[0]] + [[-k, k] for k in range(1, self.p.planes)]
        for r in range(len(rounds) + 2):
            if 0 < r < len(rounds):
                found += [("plane", k) for k in rounds[r]]
            if 1 <= r <= len(rounds):
                found += [("near", k) for k in rounds[r - 1]]
            if 2 <= r:
                found += [("far", k) for k in rounds[r - 2]]
        return found + ["end"]

    @staticmethod
    def scratch(planes):
        dma = pltpu.SemaphoreType.DMA
        span = 2 * planes - 1
        return [dma(())] + [dma((2, span))] * 4 + [dma((2, 4 * span))]


class Scatter:
    def __init__(self, place, turn, js, source, own, r1, r2, r3, r4, own_sem, s1, s2, s3, s4):
        self.p, self.turn, self.js, self.source = place, turn, js, source
        self.own, self.r1, self.r2, self.r3, self.r4 = own, r1, r2, r3, r4
        self.own_sem, self.s1, self.s2, self.s3, self.s4 = own_sem, s1, s2, s3, s4

    def owner(self, j):
        return lax.rem(self.p.z + plane_turn(self.p.planes, j), self.p.planes)

    def moves_on(self, j):
        return j + 1 < self.p.planes

    def load(self, j):
        slot = self.js.index(j) % 2
        return pltpu.make_async_copy(
            self.source(j, self.p.c), self.own.at[slot], self.own_sem.at[slot]
        )

    def x_first(self, j):
        return (self.js.index(j) + self.turn) % 2 == 0

    def sides(self, j):
        p = self.p
        return (p.xn, p.yn) if self.x_first(j) else (p.yn, p.xn)

    def copies(self, stage, j):
        p = self.p
        i = self.js.index(j)
        side, other = self.sides(j)
        if stage == 1:
            to = p.dev(p.n, p.z, 1 - p.c)
            return [remote(self.source(j, 1 - p.c), self.r1.at[i], self.s1, i, to)]
        if stage == 2:
            to = p.dev(side, p.z, p.c)
            return [
                remote(self.r1.at[i, side], self.r2.at[i, 0], self.s2, 2 * i, to),
                remote(self.r1.at[i, p.dn], self.r2.at[i, 1], self.s2, 2 * i + 1, to),
            ]
        if stage == 3:
            to = p.dev(other, p.z, p.c)
            return [remote(self.r1.at[i, other], self.r3.at[i], self.s3, i, to)]
        to = p.dev(p.n, self.owner(j), p.c)
        return [remote(self.r1.at[i, p.n], self.r4.at[i], self.s4, i, to)]

    def issue(self, stage, j):
        for copy in self.copies(stage, j):
            copy.start()

    def sent(self, stage, j):
        for copy in self.copies(stage, j):
            copy.wait_send()

    def begin(self):
        if self.own is not None:
            self.load(self.js[0]).start()

    def take(self, stage, j):
        p = self.p
        i = self.js.index(j)
        for copy in self.copies(stage, j):
            copy.wait_recv()
        side, other = self.sides(j)

        def add(n, value):
            self.r1[i, n] = self.r1[i, n] + value

        if stage == 1:
            if self.own is None:
                mine = self.source(j, p.c)
            else:
                self.load(j).wait()
                if i + 1 < len(self.js):
                    self.load(self.js[i + 1]).start()
                mine = self.own.at[i % 2]
            for n in range(4):
                add(n, mine[n])
        elif stage == 2:
            add(p.n, self.r2[i, 0])
            add(other, self.r2[i, 1])
        else:
            add(p.n, self.r3[i])
            if self.moves_on(j):
                self.issue(4, j)

    def total(self, stages=(1, 2, 3, 4)):
        found = None
        for i, j in enumerate(self.js):
            if self.moves_on(j):
                self.copies(4, j)[0].wait_recv()
                part = self.r4[i].astype(F32)
            else:
                part = self.r1[i, self.p.n].astype(F32)
            found = part if found is None else found + part
        for j in self.js:
            for stage in stages:
                if stage < 4 or self.moves_on(j):
                    self.sent(stage, j)
        return found

    @staticmethod
    def scratch(count, rows, cols, load=True):
        dma = pltpu.SemaphoreType.DMA
        own = [pltpu.VMEM((2, 4, rows, cols), BF)] if load else []
        return own + [
            pltpu.VMEM((count, 4, rows, cols), BF),
            pltpu.VMEM((count, 2, rows, cols), BF),
            pltpu.VMEM((count, rows, cols), BF),
            pltpu.VMEM((count, rows, cols), BF),
            dma((2,)),
            dma((2, count)),
            dma((2, 2 * count)),
            dma((2, count)),
            dma((2, count)),
        ]


def scatter_steps(scatters, span=2, window=2):
    js = scatters[0].js
    units = range(len(scatters))
    queue = [(u, j) for j in js for u in units]
    x_items, y_items = [], []
    for i in range(0, len(js), span):
        pair = [(u, j) for j in js[i : i + span] for u in units]
        for stage in (2, 3):
            for u, j in pair:
                first = scatters[u].x_first(j)
                (x_items if first == (stage == 2) else y_items).append((stage, u, j))
    sent = []
    done = []

    def begin():
        for s in scatters:
            s.begin()
        for u, j in queue[:window]:
            scatters[u].issue(1, j)
            sent.append((u, j))

    def ready(stage, u, j):
        if stage == 2:
            while (u, j) not in done:
                v, i = queue[len(done)]
                scatters[v].take(1, i)
                done.append((v, i))
                if len(sent) < len(queue):
                    v, i = queue[len(sent)]
                    scatters[v].issue(1, i)
                    sent.append((v, i))

    def step(i):
        for items in (x_items, y_items):
            if window <= i < len(items) + window:
                stage, u, j = items[i - window]
                scatters[u].take(stage, j)
        for items in (x_items, y_items):
            if i < len(items):
                stage, u, j = items[i]
                ready(stage, u, j)
                scatters[u].issue(stage, j)

    count = max(len(x_items), len(y_items)) + window
    return [begin] + [functools.partial(step, i) for i in range(count)]


class Exchange:
    def __init__(self, place, src, out, sems, same):
        self.p, self.src, self.out, self.sems, self.same = place, src, out, sems, same
        self.wide = 2 * place.planes
        self.total = 4 * self.wide
        self.me = place.n * self.wide + place.z * 2 + place.c

    def device(self, i):
        other = lax.rem(self.me + i, self.total)
        return other // self.wide, lax.rem(other, self.wide)

    def greet(self):
        sem = pltpu.get_barrier_semaphore()

        def signal(i, carry):
            pl.semaphore_signal(sem, inc=1, device_id=self.device(i), device_id_type=MESH)
            return carry

        lax.fori_loop(1, self.total, signal, 0)
        pl.semaphore_wait(sem, self.total - 1)

    def copy(self, i):
        other = lax.rem(self.me + i, self.total)
        src = self.src if self.same else self.src.at[other]
        return remote(src, self.out.at[self.me], self.sems, i, self.device(i))

    def each(self, do):
        def body(i, carry):
            do(i)
            return carry

        lax.fori_loop(1, self.total, body, 0)

    def start(self):
        self.each(lambda i: self.copy(i).start())
        self.out[self.me] = self.src[...] if self.same else self.src[self.me]

    def arrive(self):
        def wait(i):
            dst = self.out.at[lax.rem(self.me + self.total - i, self.total)]
            remote(dst, dst, self.sems, i, self.device(i)).wait_recv()

        self.each(wait)

    def end(self):
        self.each(lambda i: self.copy(i).wait_send())

    @staticmethod
    def scratch(planes):
        return pltpu.SemaphoreType.DMA((2, 8 * planes))


class Stream:
    def __init__(self, slots, sems, out):
        self.slots, self.sems, self.out = slots, sems, out
        self.count = 0

    def copy(self, i):
        rows = self.slots.shape[1]
        return pltpu.make_async_copy(
            self.slots.at[i % 2], self.out.at[pl.ds(i * rows, rows)], self.sems.at[i % 2]
        )

    def put(self, value):
        i = self.count
        if i >= 2:
            self.copy(i - 2).wait()
        self.slots[i % 2] = value
        self.copy(i).start()
        self.count = i + 1

    def end(self):
        for i in range(max(self.count - 2, 0), self.count):
            self.copy(i).wait()

    @staticmethod
    def scratch(rows, width, dtype):
        return [pltpu.VMEM((2, rows, width), dtype), pltpu.SemaphoreType.DMA((2,))]


def head_window(h, hd, width):
    a = pl.multiple_of(jnp.minimum((h * hd) // 128, (width - WINDOW) // 128) * 128, 128)
    lane = lax.broadcasted_iota(jnp.int32, (1, WINDOW), 1) + a
    return a, (lane >= h * hd) & (lane < h * hd + hd)


QUERY_BIAS, VALUE_BIAS, PROJ_BIAS, DOWN_BIAS, ROUTER = range(5)
SHIFT1, SCALE1, GATE1, SHIFT2, SCALE2, GATE2 = range(6)


def forward_kernel(
    off_ref,
    single_ref,
    gate_ref,
    keep_ref,
    cond_ref,
    ada_ref,
    ada_bias_ref,
    qkv_shard_ref,
    proj_shard_ref,
    up_t_ref,
    down_t_ref,
    query_bias_ref,
    value_bias_ref,
    proj_bias_ref,
    down_bias_ref,
    router_ref,
    tokens_ref,
    cot_ref,
    lse_ref,
    tg_ref,
    conds_ref,
    table_ref,
    vec_ref,
    n1_ref,
    qkv_ref,
    w_ref,
    wp_ref,
    att_ref,
    gated_ref,
    attn_ref,
    after_ref,
    n2_ref,
    gm_ref,
    g_up_ref,
    g_down_ref,
    lse_sc,
    shard_ref,
    up_ref,
    down_ref,
    g_s,
    mod_local,
    mods_s,
    flat_s,
    tok_s,
    w_s,
    wp_s,
    n1_s,
    qkv_s,
    att_s,
    gated_s,
    cot_s,
    cot_sems,
    sems,
    attn_slots,
    attn_sems,
    after_slots,
    after_sems,
    n2_slots,
    n2_sems,
    gm_slots,
    gm_sems,
    cond_sems,
    mod_sems,
    *gather_sems,
    heads,
    blk,
    planes,
):
    t, d = tok_s.shape
    hd = d // heads
    nb = t // blk
    c = hd**-0.5 * LOG2E
    place = Place(planes)
    weights = Gather(place, shard_ref, g_s, *gather_sems[:6])
    gathers = [
        Gather(place, up_ref, g_up_ref, *gather_sems[6:12]),
        Gather(place, down_ref, g_down_ref, *gather_sems[12:]),
    ]
    conds = Exchange(place, cond_ref, conds_ref, cond_sems, True)
    mods = Exchange(place, mod_local, mods_s, mod_sems, False)
    rows = proj_shard_ref.shape[0]
    for b in range(3):
        shard_ref[b * rows : (b + 1) * rows, :] = qkv_shard_ref[:, b * d : (b + 1) * d]
    shard_ref[3 * rows : 4 * rows, :] = proj_shard_ref[...]
    conds.greet()
    weights.run("begin")
    conds.start()
    for src, dst in ((up_t_ref, up_ref), (down_t_ref, down_ref)):
        natural = src[...].T
        quarter = natural.shape[0] // 4
        dst[:quarter, :] = jnp.concatenate(
            [natural[k * quarter : (k + 1) * quarter] for k in range(4)], axis=1
        )
    vec_ref[...] = jnp.zeros_like(vec_ref)
    for i, ref in enumerate(
        (query_bias_ref, value_bias_ref, proj_bias_ref, down_bias_ref, router_ref)
    ):
        vec_ref[i : i + 1, :] = ref[...].astype(F32).reshape(1, d)

    def run_group(i):
        for step in groups[i]:
            step()

    moves = {
        name: pltpu.make_async_copy(src, dst, sems.at[i])
        for i, (name, src, dst) in enumerate(
            (
                ("tok", tokens_ref, tok_s),
                ("w", w_s, w_ref),
                ("wp", wp_s, wp_ref),
                ("n1", n1_s, n1_ref),
                ("qkv", qkv_s, qkv_ref),
                ("att", att_s, att_ref),
                ("gated", gated_s, gated_ref),
            )
        )
    }

    def cot_copy(i):
        return pltpu.make_async_copy(
            cot_ref.at[pl.ds(i * blk, blk)], cot_s.at[i % 2], cot_sems.at[i % 2]
        )

    moves["tok"].start()
    for i in range(2):
        cot_copy(i).start()
    parts = weights.parts()
    rest = [(g, part) for part in parts[1:-1] for g in gathers]
    mod_local[...] = jnp.zeros_like(mod_local)
    for part in parts[1:4]:
        weights.run(part)
    conds.arrive()
    devices, rows, lanes = conds_ref.shape
    width = ada_ref.shape[0]
    slots = table_ref.shape[0]
    every = conds_ref[...].reshape(devices * rows, lanes)
    columns = ada_bias_ref[...]
    for j in range(d // lanes):
        piece = dg(every, ada_ref[:, j * lanes : (j + 1) * lanes], NT).reshape(devices, rows, width)
        columns = columns + piece[:, slots * j : slots * (j + 1)]
    mod_local[:, :slots, :width] = columns.astype(BF)
    mods.start()
    middle = 9
    for part in parts[4:middle]:
        weights.run(part)
    for g in gathers:
        g.run("begin")
    late = parts[middle:-1]
    for part in late[: len(late) // 2]:
        weights.run(part)
    for g, part in rest[:4]:
        g.run(part)
    for part in late[len(late) // 2 :]:
        weights.run(part)
    groups = spread_out([functools.partial(g.run, part) for g, part in rest[4:]], 2 * nb + heads)
    mods.arrive()
    for i in range(devices):
        flat_s[:slots, i * width : (i + 1) * width] = mods_s[i, :slots, :width].astype(F32)
    single = single_ref[0]
    flat = flat_s[:slots, :]
    flat = flat * (1.0 - single) + flat[:1] * single
    for k in range(6):
        table_ref[:, k, :] = flat[:, k * d : (k + 1) * d]
    weights.run("end")
    r = d // devices
    for i in range(devices):
        at = (i // (2 * planes), i // 2 % planes, i % 2)
        rows = slice(i * r, (i + 1) * r)
        for b in range(3):
            w_s[rows, b * d : (b + 1) * d] = g_s[at + (slice(b * r, (b + 1) * r),)]
        wp_s[rows, :] = g_s[at + (slice(3 * r, 4 * r),)]
    moves["w"].start()
    moves["wp"].start()
    moves["tok"].wait()

    def vector(i):
        return vec_ref[i : i + 1, :]

    def mod(i, k):
        return table_ref[i, k : k + 1, :]

    bias = jnp.concatenate(
        [vector(QUERY_BIAS), jnp.zeros((1, d), F32), vector(VALUE_BIAS)], axis=1
    )
    for i in range(nb):
        rows = slice(i * blk, (i + 1) * blk)
        normed, _ = ln_parts(tok_s[rows, :])
        low = (normed * (1.0 + mod(i, SCALE1)) + mod(i, SHIFT1)).astype(BF)
        n1_s[:, rows] = low.T
        qkv_s[rows, :] = (dg(low, w_s[...], NN) + bias).astype(BF)
        run_group(i)
    moves["n1"].start()
    moves["qkv"].start()
    off = off_ref[0]
    lane128 = lax.broadcasted_iota(jnp.int32, (1, 128), 1)

    def body(h, carry):
        a, mask = head_window(h, hd, d)
        keys = qkv_s[:, pl.ds(pl.multiple_of(d + a, 128), WINDOW)]
        values = qkv_s[:, pl.ds(pl.multiple_of(2 * d + a, 128), WINDOW)]
        cols = pl.ds(a, WINDOW)
        for i in range(nb):
            rows = pl.ds(i * blk, blk)
            q = qkv_s[rows, cols]
            q = jnp.where(mask, q, jnp.zeros_like(q))
            s = dg(q, keys, NT)
            cuts = [s[:, j * blk : (j + 1) * blk] for j in range(nb)]
            own = jnp.max(cuts[i], axis=1, keepdims=True) * c
            others = functools.reduce(jnp.maximum, [cuts[j] for j in range(nb) if j != i])
            m = jnp.maximum(own, jnp.max(others, axis=1, keepdims=True) * c + off)
            m_off = m - off
            ps = [jnp.exp2(cuts[j] * c - (m if j == i else m_off)) for j in range(nb)]
            total = jnp.sum(functools.reduce(jnp.add, ps), axis=1, keepdims=True)
            p = jnp.concatenate([x.astype(BF) for x in ps], axis=1)
            o = dg(p, values, NN) * (1.0 / total)
            og = (o * gate_ref[i, :, cols]).astype(BF)
            att_s[rows, cols] = jnp.where(mask, o, att_s[rows, cols])
            gated_s[rows, cols] = jnp.where(mask, og, gated_s[rows, cols])
            lse_sc[rows, :] = jnp.where(lane128 == h, m + jnp.log2(total), lse_sc[rows, :])
        run_at(h, groups[nb : nb + heads])
        return carry

    lax.fori_loop(0, heads, body, 0)
    moves["att"].start()
    moves["gated"].start()
    lse_ref[...] = lse_sc[...].T[:heads, :]
    streams = [
        Stream(attn_slots, attn_sems, attn_ref),
        Stream(after_slots, after_sems, after_ref),
        Stream(n2_slots, n2_sems, n2_ref),
        Stream(gm_slots, gm_sems, gm_ref),
    ]
    for i in range(nb):
        rows = slice(i * blk, (i + 1) * blk)
        attn = dg(gated_s[rows, :], wp_s[...], NN) + vector(PROJ_BIAS)
        streams[0].put(attn)
        after = tok_s[rows, :] + mod(i, GATE1) * attn
        streams[1].put(after)
        normed, _ = ln_parts(after)
        y = normed * (1.0 + mod(i, SCALE2)) + mod(i, SHIFT2)
        streams[2].put(y.astype(BF))
        token_gate = jax.nn.sigmoid(jnp.sum(y * vector(ROUTER), axis=1, keepdims=True))
        tg_ref[rows, :] = token_gate
        cot_copy(i).wait()
        cot = cot_s[i % 2]
        streams[3].put((cot * (mod(i, GATE2) * (keep_ref[rows, :] * token_gate))).astype(BF))
        if i + 2 < nb:
            cot_copy(i + 2).start()
        run_group(nb + heads + i)
    for g in gathers:
        g.run("end")
    for stream in streams:
        stream.end()
    for name in ("w", "wp", "n1", "qkv", "att", "gated"):
        moves[name].wait()
    conds.end()
    mods.end()


def forward_call(
    off, single, gate_rows, keep, cond, ada_t, ada_bias, qkv_w, proj_w, up_t, down_t, vectors, tokens, cot, heads, blk, planes
):
    t, d = tokens.shape
    devices = 8 * planes
    slots = t // blk
    lanes = up_to(ada_t.shape[0], 128)
    shard = (up_to(4 * proj_w.shape[0], 16), d)
    unit = (up_to(up_t.shape[1] // 4, 16), d)
    gathered = shape((4, planes, 2) + unit, BF)
    dma = pltpu.SemaphoreType.DMA
    return pl.pallas_call(
        functools.partial(forward_kernel, heads=heads, blk=blk, planes=planes),
        out_shape=(
            shape((heads, t)),
            shape((t, 1)),
            shape((devices,) + cond.shape, BF),
            shape((slots, 6, d)),
            shape((8, d)),
            shape((d, t), BF),
            shape((t, 3 * d), BF),
            shape((d, 3 * d), BF),
            shape((d, d), BF),
            shape((t, d)),
            shape((t, d), BF),
            shape((t, d)),
            shape((t, d)),
            shape((t, d), BF),
            shape((t, d), BF),
            gathered,
            gathered,
        ),
        in_specs=[SMEM_SPEC] * 2 + [VMEM_SPEC] * 14 + [ANY_SPEC] * 2,
        out_specs=(VMEM_SPEC,) * 5 + (ANY_SPEC,) * 12,
        scratch_shapes=[
            pltpu.VMEM((t, 128), F32),
            pltpu.VMEM(shard, BF),
            pltpu.VMEM(unit, BF),
            pltpu.VMEM(unit, BF),
            pltpu.VMEM((4, planes, 2) + shard, BF),
            pltpu.VMEM((devices, 16, lanes), BF),
            pltpu.VMEM((devices, 16, lanes), BF),
            pltpu.VMEM((up_to(slots, 8), 6 * d), F32),
            pltpu.VMEM((t, d), F32),
            pltpu.VMEM((d, 3 * d), BF),
            pltpu.VMEM((d, d), BF),
            pltpu.VMEM((d, t), BF),
            pltpu.VMEM((t, 3 * d), BF),
            pltpu.VMEM((t, d), F32),
            pltpu.VMEM((t, d), BF),
            pltpu.VMEM((2, blk, d), F32),
            dma((2,)),
            dma((7,)),
        ]
        + Stream.scratch(blk, d, F32) * 2
        + Stream.scratch(blk, d, BF) * 2
        + [Exchange.scratch(planes)] * 2
        + Gather.scratch(planes) * 3,
        compiler_params=params(63, collective_id=2),
        name="forward",
    )(
        off, single, gate_rows, keep, cond, ada_t, ada_bias, qkv_w, proj_w, up_t, down_t, *vectors, tokens, cot
    )


def backward_kernel(
    off_ref,
    qkv_ref,
    do_ref,
    lse_ref,
    delta_ref,
    n1t_ref,
    gp_ref,
    up_ref,
    down_ref,
    dqkv_ref,
    bias_ref,
    g_up_ref,
    g_down_ref,
    done_ref,
    part_ref,
    kt_sc,
    dqt_sc,
    part_sem,
    *rest,
    heads,
    blk,
    planes,
    cuts,
):
    t, d = do_ref.shape
    hd = d // heads
    nb = t // blk
    scale = hd**-0.5
    c = scale * LOG2E
    width = d // cuts
    devices = 8 * planes
    r = d // devices
    first = planes // 2
    place = Place(planes)
    place.barrier(True)
    slots, rest = rest[: cuts - 1], rest[cuts - 1 :]
    each = 10
    js = list(range(first, planes))

    def kept(ref):
        return lambda j, c: ref.at[:, j - first, c]

    def local(ref):
        return lambda j, c: ref.at[:, lax.rem(place.z + plane_turn(planes, j), planes), c]

    ups = [
        Scatter(place, u, js, kept(ref), *rest[each * u : each * (u + 1)])
        for u, ref in enumerate((up_ref, down_ref))
    ]
    rest = rest[2 * each :]
    each -= 1
    chains = [
        Scatter(
            place, m, list(range(planes)), local(slots[m]), None, *rest[each * m : each * (m + 1)]
        )
        for m in range(cuts - 1)
    ]
    up_steps = scatter_steps(ups)
    chain_steps = [scatter_steps([chain], planes) for chain in chains]
    up_steps[0]()
    ends = [-(-width * (m + 1) // hd) for m in range(cuts)]
    queues = [[] for _ in range(heads + 1)]

    def place_steps(steps, start, first, stop):
        queues[start] += steps[:2]
        for i, step in enumerate(steps[2:]):
            queues[first + i * (stop - first) // max(len(steps) - 3, 1)].append(step)

    place_steps(up_steps[1:], 0, ends[0] + 1, ends[1] + 1)
    for m in range(cuts - 1):
        steps = chain_steps[m][1:]
        place_steps(steps, ends[m], min(ends[m] + 4 - m, heads), min(ends[m] + 7, heads))

    off = off_ref[0]
    kt_sc[...] = qkv_ref[:, d : 2 * d].T

    def body(h, carry, start, end):
        a, mask = head_window(h, hd, d)
        cols = pl.ds(a, WINDOW)
        key_cols = pl.ds(pl.multiple_of(d + a, 128), WINDOW)
        value_cols = pl.ds(pl.multiple_of(2 * d + a, 128), WINDOW)
        keys = qkv_ref[:, key_cols]
        values = qkv_ref[:, value_cols]
        keys_t = kt_sc[cols, :]
        dk_sum = None
        dv_sum = None
        for i in range(nb):
            rows = pl.ds(i * blk, blk)
            span = slice(i * blk, (i + 1) * blk)
            q = qkv_ref[rows, cols]
            q = jnp.where(mask, q, jnp.zeros_like(q))
            do = do_ref[rows, cols]
            do = jnp.where(mask, do, jnp.zeros_like(do))
            lse = lse_ref[pl.ds(h, 1), span]
            delta = delta_ref[pl.ds(h, 1), span]
            s_t = dg(keys, q, NT)
            dp_t = dg(values, do, NT)
            ps = []
            ds = []
            for j in range(nb):
                cut = slice(j * blk, (j + 1) * blk)
                p = jnp.exp2(s_t[cut] * c - (lse if j == i else lse - off))
                ps.append(p.astype(BF))
                ds.append((p * (dp_t[cut] - delta)).astype(BF))
            p = jnp.concatenate(ps, axis=0)
            grad_s = jnp.concatenate(ds, axis=0)
            dv = dg(p, do, NN)
            dk = dg(grad_s, q, NN)
            dv_sum = dv if dv_sum is None else dv_sum + dv
            dk_sum = dk if dk_sum is None else dk_sum + dk
            dqt_sc[:, span] = (dg(keys_t, grad_s, NN) * scale).astype(BF)
        dk = (dk_sum * scale).astype(BF)
        dqkv_ref[:, key_cols] = jnp.where(mask, dk, dqkv_ref[:, key_cols])
        dqkv_ref[:, value_cols] = jnp.where(mask, dv_sum.astype(BF), dqkv_ref[:, value_cols])
        dqkv_ref[:, cols] = jnp.where(mask, dqt_sc[...].T, dqkv_ref[:, cols])
        run_at(h - start, queues[start:end])
        return carry

    def weight_part(m, out):
        dqkv = jnp.concatenate(
            [dqkv_ref[:, b * d + m * width : b * d + (m + 1) * width] for b in range(3)], axis=1
        )
        bias_ref[m] = col_sum(dqkv.astype(F32))
        grad = dg(n1t_ref[...], dqkv, NN).astype(BF)
        for i in range(devices):
            rows = slice(i * r, (i + 1) * r)
            at = (i // (2 * planes), i // 2 % planes, i % 2)
            for b in range(3):
                out[at + (slice(b * r, (b + 1) * r),)] = grad[rows, b * width : (b + 1) * width]
            out[at + (slice(3 * r, 4 * r),)] = gp_ref[rows, m * width : (m + 1) * width]

    for m in range(cuts):
        start = 0 if m == 0 else ends[m - 1]
        lax.fori_loop(start, ends[m], functools.partial(body, start=start, end=ends[m]), 0)
        if m + 1 < cuts:
            weight_part(m, slots[m])
            chain_steps[m][0]()
    for j in chains[0].js:
        chains[0].sent(1, j)
    weight_part(cuts - 1, slots[0])
    keep = pltpu.make_async_copy(slots[0], part_ref, part_sem)
    keep.start()
    for step in queues[heads]:
        step()
    g_up_ref[...] = ups[0].total()
    g_down_ref[...] = ups[1].total()
    for m, chain in enumerate(chains):
        stages = (2, 3, 4) if m == 0 else (1, 2, 3, 4)
        done_ref[:, m * width : (m + 1) * width] = chain.total(stages)
    keep.wait()


def backward_call(off, qkv, do, lse, delta, n1t, g_proj, up, down, heads, blk, planes, cuts):
    t, d = do.shape
    rows, cols = up.shape[3:]
    width = d // cuts
    part = (4, planes, 2, up_to(4 * d // (8 * planes), 16), width)
    return pl.pallas_call(
        functools.partial(backward_kernel, heads=heads, blk=blk, planes=planes, cuts=cuts),
        out_shape=(
            shape((t, 3 * d), BF),
            shape((cuts, 1, 3 * width)),
            shape((rows, cols)),
            shape((rows, cols)),
            shape((part[3], (cuts - 1) * width)),
            shape(part, BF),
        ),
        in_specs=[SMEM_SPEC] + [VMEM_SPEC] * 6 + [ANY_SPEC] * 2,
        out_specs=(VMEM_SPEC,) * 5 + (ANY_SPEC,),
        scratch_shapes=[
            pltpu.VMEM((d, t), BF),
            pltpu.VMEM((WINDOW, t), BF),
            pltpu.SemaphoreType.DMA(()),
        ]
        + [pltpu.VMEM(part, BF)] * (cuts - 1)
        + Scatter.scratch(planes - planes // 2, rows, cols) * 2
        + Scatter.scratch(planes, part[3], width, False) * (cuts - 1),
        compiler_params=params(63, collective_id=3),
        name="attention_backward",
    )(off, qkv, do, lse, delta, n1t, g_proj, up, down)


def mlp_kernel(
    n2_ref,
    gm_ref,
    b1_ref,
    cs_ref,
    g1_ref,
    g2_ref,
    mlp_ref,
    gn2_ref,
    gb1_ref,
    gch_ref,
    o1_ref,
    o2_ref,
    p1_ref,
    p2_ref,
    g1_s,
    g2_s,
    w1_s,
    w2_s,
    sc_s,
    gp_s,
    p1_s,
    p2_s,
    g_sems,
    p_sems,
    *rest,
    blk,
    planes,
):
    t, d = n2_ref.shape
    nb = t // blk
    hidden = w1_s.shape[0]
    quarter = hidden // 8
    piece = d // 4
    j = pl.program_id(0)
    place = Place(planes)
    hosted = planes // 2
    half = len(rest) // 2
    scatters = [
        Scatter(place, u, list(range(hosted)), lambda j, c, p=p: p.at[:, c], None, *scratch)
        for u, (p, scratch) in enumerate(((p1_s, rest[:half]), (p2_s, rest[half:])))
    ]

    def loads(step):
        plane = lax.rem(place.z + plane_turn(planes, step), planes)
        return [
            pltpu.make_async_copy(g.at[:, plane], slot, g_sems.at[i])
            for i, (g, slot) in enumerate(((g1_ref, g1_s), (g2_ref, g2_s)))
        ]

    def keeps(step):
        return [
            pltpu.make_async_copy(slot, p.at[:, step - hosted], p_sems.at[i])
            for i, (slot, p) in enumerate(((p1_s, p1_ref), (p2_s, p2_ref)))
        ]

    def early(step):
        for s in scatters:
            if step - 1 < hosted:
                s.take(1, step - 1)
                s.issue(2, step - 1)
        for s in scatters:
            if 0 <= step - 2 < hosted:
                s.take(3, step - 2)

    def late(step):
        for s in scatters:
            if step - 1 < hosted:
                s.take(2, step - 1)
                s.issue(3, step - 1)
                s.sent(1, step - 1)
        if step - 1 >= hosted:
            for copy in keeps(step - 1):
                copy.wait()

    def at_steps(do):
        for step in range(1, planes):
            pl.when(j == step)(functools.partial(do, step))

    def places():
        for c in range(2):
            for k in range(4):
                yield c, slice((4 * c + k) * quarter, (4 * c + k + 1) * quarter), k

    @pl.when(j == 0)
    def _():
        for copy in loads(0):
            copy.start()
        place.barrier(True)
        mlp_ref[...] = jnp.zeros_like(mlp_ref)
        gn2_ref[...] = jnp.zeros_like(gn2_ref)

    for copy in loads(j):
        copy.wait()
    for c, rows, k in places():
        cols = slice(k * piece, (k + 1) * piece)
        for w, g in ((w1_s, g1_s), (w2_s, g2_s)):
            w[rows, :] = jnp.concatenate([g[n, c, :quarter, cols] for n in range(4)], axis=1)

    @pl.when(j + 1 < planes)
    def _():
        for copy in loads(j + 1):
            copy.start()

    at_steps(early)
    w1 = w1_s[...]
    w2 = w2_s[...]
    grad_bias = None
    for i in range(nb):
        rows = slice(i * blk, (i + 1) * blk)
        pre = dg(n2_ref[rows, :], w1, NT) + b1_ref[0]
        grad_scaled = dg(gm_ref[rows, :], w2, NT)
        act, slope = gelu_parts(pre)
        gate = cs_ref[0, i : i + 1]
        scaled = (act * gate).astype(BF)
        grad_pre = (grad_scaled * gate * slope).astype(BF)
        gch_ref[0, i : i + 1] = col_sum(grad_scaled * act)
        part = col_sum(grad_pre.astype(F32))
        grad_bias = part if grad_bias is None else grad_bias + part
        sc_s[rows, :] = scaled
        gp_s[rows, :] = grad_pre
        mlp_ref[rows, :] += dg(scaled, w2, NN)
        gn2_ref[rows, :] += dg(grad_pre, w1, NN)
    gb1_ref[0] = grad_bias

    at_steps(late)
    for left, right, out in ((gp_s, n2_ref, p1_s), (sc_s, gm_ref, p2_s)):
        grad = dg(left[...], right[...], TN).astype(BF)
        for c, rows, k in places():
            for n in range(4):
                out[n, c, :quarter, k * piece : (k + 1) * piece] = grad[rows, n * piece : (n + 1) * piece]
    for step in range(planes):

        @pl.when(j == step)
        def _(step=step):
            if step < hosted:
                for s in scatters:
                    s.issue(1, step)
            else:
                for copy in keeps(step):
                    copy.start()

    @pl.when(j == planes - 1)
    def _():
        o1_ref[...] = scatters[0].total((2, 3, 4))
        o2_ref[...] = scatters[1].total((2, 3, 4))
        for copy in keeps(planes - 1):
            copy.wait()


def mlp_call(n2, gm, g1, g2, b1, gates, blk):
    t, d = n2.shape
    planes, rows = g1.shape[1], g1.shape[3]
    nb, ff = gates.shape
    hb = ff // planes
    hosted = planes // 2

    def turn(j):
        return lax.rem(lax.axis_index("wide") // 2 + plane_turn(planes, j), planes)

    b_spec = pl.BlockSpec((1, 1, hb), lambda j: (turn(j), 0, 0))
    c_spec = pl.BlockSpec((1, nb, hb), lambda j: (turn(j), 0, 0))
    kept = shape((4, planes - hosted, 2, rows, d), BF)
    dma = pltpu.SemaphoreType.DMA
    mlp, gn2, gb1, gch, o1, o2, p1, p2 = pl.pallas_call(
        functools.partial(mlp_kernel, blk=blk, planes=planes),
        grid=(planes,),
        out_shape=(
            shape((t, d)),
            shape((t, d)),
            shape((planes, 1, hb)),
            shape((planes, nb, hb)),
            shape((rows, d)),
            shape((rows, d)),
            kept,
            kept,
        ),
        in_specs=[whole(t, d), whole(t, d), b_spec, c_spec, ANY_SPEC, ANY_SPEC],
        out_specs=(whole(t, d), whole(t, d), b_spec, c_spec, whole(rows, d), whole(rows, d))
        + (ANY_SPEC,) * 2,
        scratch_shapes=[pltpu.VMEM((4, 2, rows, d), BF)] * 2
        + [pltpu.VMEM((hb, d), BF)] * 2
        + [pltpu.VMEM((t, hb), BF)] * 2
        + [pltpu.VMEM((4, 2, rows, d), BF)] * 2
        + [dma((2,))] * 2
        + Scatter.scratch(hosted, rows, d, False) * 2,
        compiler_params=params(62, collective_id=5),
        name="feed_forward",
    )(n2, gm, b1.reshape(planes, 1, hb), gates.reshape(nb, planes, hb).transpose(1, 0, 2), g1, g2)
    return mlp, gn2, o1, o2, p1, p2, gb1.reshape(ff), gch.transpose(1, 0, 2).reshape(nb, ff)


def middle_back_kernel(
    mlp_ref,
    gn2_ref,
    after_ref,
    attn_ref,
    cot_ref,
    gm_ref,
    gated_ref,
    att_ref,
    tg_ref,
    keep_ref,
    w_ref,
    vec_ref,
    table_ref,
    head_ref,
    out_ref,
    ga_ref,
    do_ref,
    delta_ref,
    gw_ref,
    mod_ref,
    sums_ref,
    gw_s,
    *,
    heads,
):
    d = after_ref.shape[1]
    hd = d // heads
    first = pl.program_id(0) == 0
    after = after_ref[...]
    cot = cot_ref[...]
    gate2 = table_ref[0, GATE2 : GATE2 + 1]
    tg = tg_ref[...]
    keep = keep_ref[...]
    normed, rstd = ln_parts(after)
    scale2 = table_ref[0, SCALE2 : SCALE2 + 1]
    y = normed * (1.0 + scale2) + table_ref[0, SHIFT2 : SHIFT2 + 1]
    mlp_out = mlp_ref[...] + vec_ref[DOWN_BIAS : DOWN_BIAS + 1]
    open_gate = keep * tg
    out_ref[...] = after + (gate2 * open_gate) * mlp_out
    weighted = cot * mlp_out
    grad_tg = jnp.sum(weighted * gate2, axis=1, keepdims=True) * keep
    coef = grad_tg * tg * (1.0 - tg)
    gy = gn2_ref[...] + coef * vec_ref[ROUTER : ROUTER + 1]
    ga = cot + ln_back(gy, normed, rstd, scale2)
    ga_ref[...] = ga
    attn = attn_ref[...]
    g_attn = (ga * table_ref[0, GATE1 : GATE1 + 1]).astype(BF)
    mod_ref[0] = jnp.concatenate(
        [col_sum(ga * attn), col_sum(gy), col_sum(gy * normed), col_sum(weighted * open_gate)], axis=0
    )
    sums = jnp.concatenate(
        [
            col_sum(coef * y),
            col_sum(g_attn.astype(F32)),
            col_sum(gm_ref[...].astype(F32)),
        ],
        axis=0,
    )
    g_gated = dg(g_attn, w_ref[...], NT)
    att = att_ref[...]
    mod_ref[1] = jnp.concatenate([col_sum(g_gated * att), jnp.zeros((3, d), F32)], axis=0)
    do = (g_gated * head_ref[0]).astype(BF)
    do_ref[...] = do
    lane = lax.broadcasted_iota(jnp.int32, (heads, d), 1)
    head = lax.broadcasted_iota(jnp.int32, (heads, d), 0) * hd
    pick = jnp.where((lane >= head) & (lane < head + hd), 1.0, 0.0)
    delta_ref[...] = lax.dot_general(
        pick, do.astype(F32) * att, NT, precision=HIGHEST, preferred_element_type=F32
    )
    gw = dg(gated_ref[...], g_attn, TN)

    @pl.when(first)
    def _():
        sums_ref[...] = sums
        gw_s[...] = gw

    @pl.when(jnp.logical_not(first))
    def _():
        sums_ref[...] += sums
        gw_s[...] += gw

    @pl.when(pl.program_id(0) == pl.num_programs(0) - 1)
    def _():
        gw_ref[...] = gw_s[...].astype(BF)


def middle_back_call(
    mlp, gn2, after, attn, cot, gm, gated, att, tg, keep, w, vecs, table, head_rows, heads, blk
):
    t, d = after.shape
    nb = t // blk
    r, v, column = rows_of(blk, d), row_vec(d), rows_of(blk, 1)
    return pl.pallas_call(
        functools.partial(middle_back_kernel, heads=heads),
        grid=(nb,),
        out_shape=(
            shape((t, d)),
            shape((t, d)),
            shape((t, d), BF),
            shape((heads, t)),
            shape((d, d), BF),
            shape((nb * 2, 4, d)),
            shape((3, d)),
        ),
        in_specs=[r] * 8 + [column, column, whole(d, d), whole(*vecs.shape)]
        + [pl.BlockSpec((1,) + table.shape[1:], lambda i: (i, 0, 0)), v],
        out_specs=(
            r,
            r,
            r,
            pl.BlockSpec((heads, blk), lambda i: (0, i)),
            whole(d, d),
            pl.BlockSpec((2, 4, d), lambda i: (i, 0, 0)),
            whole(3, d),
        ),
        scratch_shapes=[pltpu.VMEM((d, d), F32)],
        compiler_params=params(),
        name="middle_backward",
    )(mlp, gn2, after, attn, cot, gm, gated, att, tg, keep, w, vecs, table, head_rows)


def final_kernel(
    single_ref,
    table_ref,
    mods_ref,
    sums_ref,
    logits_ref,
    conds_ref,
    up1_ref,
    up2_ref,
    down1_ref,
    down2_ref,
    done_ref,
    part_ref,
    dqkv_ref,
    w_ref,
    tokens_ref,
    ga_ref,
    qkv_grad_ref,
    proj_grad_ref,
    sum_ref,
    ada_ref,
    ada_bias_ref,
    router_ref,
    logit_ref,
    up_ref,
    down_ref,
    grad_ref,
    conds_s,
    all_sums,
    own_mods,
    all_mods,
    all_logits,
    w_s,
    dq_s,
    tok_s,
    ga_s,
    w_sem,
    in_sems,
    out_slots,
    out_sems,
    mod_sems,
    logit_sems,
    *rest,
    planes,
    blk,
):
    place = Place(planes)
    mods = Exchange(place, own_mods, all_mods, mod_sems, False)
    logits = Exchange(place, logits_ref, all_logits, logit_sems, True)

    def source(j, c):
        return part_ref.at[:, lax.rem(place.z + plane_turn(planes, j), planes), c]

    sums = Gather(place, sums_ref, all_sums, *rest[:6])
    chain = Scatter(place, 0, list(range(planes)), source, *rest[6:])
    t, d = tokens_ref.shape
    nb = t // blk
    w_load = pltpu.make_async_copy(w_ref, w_s, w_sem)

    def loads(i):
        rows = pl.ds(i * blk, blk)
        return [
            pltpu.make_async_copy(src.at[rows], dst.at[i % 2], in_sems.at[k, i % 2])
            for k, (src, dst) in enumerate(((dqkv_ref, dq_s), (tokens_ref, tok_s), (ga_ref, ga_s)))
        ]

    w_load.start()
    for copy in loads(0) + loads(1):
        copy.start()
    mods.greet()
    steps = scatter_steps([chain], planes)
    steps[0]()
    sums.run("begin")
    logits.start()
    own_mods[...] = jnp.zeros_like(own_mods)
    out = Stream(out_slots, out_sems, grad_ref)
    tables = []

    def block(i):
        if i == 0:
            w_load.wait()
        for copy in loads(i):
            copy.wait()
        gy = dg(dq_s[i % 2], w_s[...], NT)
        normed, rstd = ln_parts(tok_s[i % 2])
        out.put(ga_s[i % 2] + ln_back(gy, normed, rstd, table_ref[i, SCALE1 : SCALE1 + 1]))
        tables.append([col_sum(gy), col_sum(gy * normed)] + [mods_ref[i, k : k + 1] for k in range(4)])
        if i + 2 < nb:
            for copy in loads(i + 2):
                copy.start()

    def exchange():
        single = single_ref[0]
        devices = own_mods.shape[0]
        width = ada_bias_ref.shape[1]
        flat = [jnp.concatenate(row, axis=1) for row in tables]
        rows = [(1.0 - single) * row for row in flat]
        rows[0] = flat[0] + single * functools.reduce(jnp.add, flat[1:])
        every = jnp.concatenate(rows, axis=0).astype(BF)
        for i in range(devices):
            own_mods[i, :nb, :width] = every[:, i * width : (i + 1) * width]
        mods.start()

    def products():
        mods.arrive()
        logits.arrive()
        devices, rows, _ = conds_s.shape
        conds = conds_s[...].reshape(devices * rows, d)
        got = all_mods[...].reshape(devices * rows, -1)
        columns = ada_bias_ref.shape[1]
        ada_ref[...] = dg(got, conds, TN)[:columns]
        ada_bias_ref[...] = col_sum(got.astype(F32))[:, :columns]
        got = all_logits[...].reshape(devices * rows, -1)
        router_ref[...] = lax.dot_general(
            got, conds.astype(F32), TN, precision=HIGHEST, preferred_element_type=F32
        )
        logit_ref[...] = col_sum(got)

    def local_work():
        lanes = conds_ref.shape[2]
        conds_s[...] = jnp.zeros_like(conds_s)
        for j in range(d // lanes):
            rows = slice(nb * j, nb * (j + 1))
            conds_s[:, :nb, j * lanes : (j + 1) * lanes] = conds_ref[:, rows, :]
        piece = up_ref.shape[0]
        quarter = up_ref.shape[1] // 4
        for a, b, to in ((up1_ref, up2_ref, up_ref), (down1_ref, down2_ref, down_ref)):
            both = a[...] + b[...]
            rows = [both[:quarter, k * piece : (k + 1) * piece] for k in range(4)]
            to[...] = jnp.concatenate(rows, axis=0).T

    parts = [functools.partial(sums.run, part) for part in sums.parts()[1:-1]]
    rest = steps[3:]
    work = [
        [functools.partial(block, 0)],
        steps[1:3],
        [functools.partial(block, i) for i in range(1, nb - 1)],
        rest[:1],
        [functools.partial(block, nb - 1), exchange],
        rest[1:2],
        [local_work],
        rest[2:],
    ]
    work = [do for group in work for do in group]
    for do, group in zip(work, spread_out(parts, len(work))):
        do()
        for part in group:
            part()
    products()
    sums.run("end")
    sum_ref[...] = jnp.sum(all_sums[...].reshape((8 * planes,) + sum_ref.shape), axis=0)
    last = chain.total()
    r = proj_grad_ref.shape[0]
    ready = done_ref.shape[1]
    for b in range(4):
        rows = slice(b * r, (b + 1) * r)
        to, start = (qkv_grad_ref, b * d) if b < 3 else (proj_grad_ref, 0)
        to[:, start : start + ready] = done_ref[rows, :]
        to[:, start + ready : start + d] = last[rows]
    out.end()
    mods.end()
    logits.end()


def final_call(
    single, table, mods, sums, logits, conds, pairs, done, part, dqkv, w, tokens, ga, mod_width, hidden, planes, blk
):
    rows, width = part.shape[3:]
    t, d = tokens.shape
    devices = 8 * planes
    spread = (4, planes, 2)
    padded = logits.shape[0]
    blocks = (devices, padded, up_to(mod_width, 128))
    piece = shape((d // 4, hidden))
    dma = pltpu.SemaphoreType.DMA
    return pl.pallas_call(
        functools.partial(final_kernel, planes=planes, blk=blk),
        out_shape=(
            shape((d // devices, 3 * d)),
            shape((d // devices, d)),
            shape(sums.shape),
            shape((mod_width, d)),
            shape((1, mod_width)),
            shape((logits.shape[1], d)),
            shape((1, logits.shape[1])),
            piece,
            piece,
            shape((t, d)),
        ),
        in_specs=[SMEM_SPEC] + [VMEM_SPEC] * 10 + [ANY_SPEC] * 5,
        out_specs=(VMEM_SPEC,) * 9 + (ANY_SPEC,),
        scratch_shapes=[
            pltpu.VMEM((devices, padded, d), BF),
            pltpu.VMEM(spread + sums.shape, F32),
            pltpu.VMEM(blocks, BF),
            pltpu.VMEM(blocks, BF),
            pltpu.VMEM((devices,) + logits.shape, F32),
            pltpu.VMEM(w.shape, BF),
            pltpu.VMEM((2, blk, 3 * d), BF),
            pltpu.VMEM((2, blk, d), F32),
            pltpu.VMEM((2, blk, d), F32),
            dma(()),
            dma((3, 2)),
        ]
        + Stream.scratch(blk, d, F32)
        + [Exchange.scratch(planes)] * 2
        + Gather.scratch(planes)
        + Scatter.scratch(planes, rows, width),
        compiler_params=params(collective_id=4),
        name="last_sums",
    )(single, table, mods, sums, logits, conds, *pairs, done, part, dqkv, w, tokens, ga)


def on_device(
    planes,
    tokens,
    conditioning,
    row_items,
    head_mask,
    chan_mask,
    skip_mask,
    ada_weight,
    ada_bias,
    qkv_weight,
    query_bias,
    value_bias,
    proj_weight,
    proj_bias,
    fc1_weight,
    fc1_bias,
    fc2_weight,
    fc2_bias,
    head_router,
    head_router_bias,
    chan_router,
    chan_router_bias,
    token_router,
    cotangent,
):
    t, d = tokens.shape
    slots = conditioning.shape[0]
    heads = head_mask.shape[1]
    groups = chan_mask.shape[1]
    hidden = fc1_bias.shape[0]
    hd = d // heads
    unit = hidden // groups
    blk = t // slots
    single = row_items[0] == 1
    off = jnp.where(single, 0.0, MASKED).astype(F32).reshape(1)

    def per_block(table):
        return jnp.where(single, table[:1], table)

    def per_slot(blocks):
        total = jnp.sum(blocks, axis=0, keepdims=True)
        first = (jnp.arange(slots) == 0).reshape((slots,) + (1,) * (blocks.ndim - 1))
        return jnp.where(single, jnp.where(first, total, 0.0), blocks)

    devices = 8 * planes
    silu_cond = jax.nn.silu(conditioning.astype(F32)).astype(BF)
    conds_pad = pad_rows(silu_cond.reshape(slots, -1, 128).transpose(1, 0, 2).reshape(-1, 128))
    mod_width = ada_bias.shape[0]
    alone = jnp.where(single, 1.0, 0.0).astype(F32).reshape(1)

    def router(weight, bias, mask):
        gate = jax.nn.sigmoid(dg(silu_cond, weight, NN) + bias.astype(F32))
        mask = mask.astype(F32)
        return mask * gate, mask * gate * (1.0 - gate)

    head_gate, head_slope = router(head_router, head_router_bias, head_mask)
    chan_gate, chan_slope = router(chan_router, chan_router_bias, chan_mask)
    head_rows = jnp.repeat(per_block(head_gate), hd, axis=1)[:, None, :]
    chan_rows = jnp.repeat(per_block(chan_gate), unit, axis=1)
    keep = (1.0 - skip_mask.astype(F32))[:, None]

    (
        lse,
        tg,
        conds,
        table,
        vecs,
        n1t,
        qkv,
        full_qkv,
        full_proj,
        att,
        gated,
        attn,
        after,
        n2,
        gm,
        g_up,
        g_down,
    ) = forward_call(
        off,
        alone,
        head_rows,
        keep,
        conds_pad,
        ada_weight.T,
        ada_bias.astype(F32)[None],
        qkv_weight,
        proj_weight,
        fc1_weight.T,
        fc2_weight.T,
        (query_bias, value_bias, proj_bias, fc2_bias, token_router),
        tokens,
        cotangent,
        heads,
        blk,
        planes,
    )
    mlp, gn2, o_up, o_down, p_up, p_down, gb1, gch = mlp_call(
        n2, gm, g_up, g_down, fc1_bias.astype(F32), chan_rows, blk
    )
    output, ga, do, delta, g_proj, mods, sums = middle_back_call(
        mlp,
        gn2,
        after,
        attn,
        cotangent,
        gm,
        gated,
        att,
        tg,
        keep,
        full_proj,
        vecs,
        table,
        head_rows,
        heads,
        blk,
    )
    mods = mods.reshape(slots, 8, d)
    dqkv, qkv_sums, g_up, g_down, g_done, part = backward_call(
        off, qkv, do, lse, delta, n1t, g_proj, p_up, p_down, heads, blk, planes, 3
    )
    qkv_sums = qkv_sums.reshape(3, 3, d // 3).transpose(1, 0, 2).reshape(3, d)
    g_head = per_slot(jnp.sum(mods[:, 4].reshape(slots, heads, hd), axis=2)) * head_slope
    g_chan = per_slot(jnp.sum(gch.reshape(slots, groups, unit), axis=2)) * chan_slope
    logits = jnp.pad(
        jnp.concatenate([g_head, g_chan], axis=1),
        ((0, up_to(slots, 16) - slots), (0, up_to(heads + groups, 128) - heads - groups)),
    )
    vector = jnp.concatenate([qkv_sums[0], qkv_sums[2], sums[1], gb1, sums[2], sums[0]])
    length = vector.shape[0]
    vector = jnp.pad(vector, (0, up_to(length, 1024) - length)).reshape(-1, 128)
    (
        g_qkv,
        g_proj,
        small,
        grad_ada_t,
        grad_ada_bias,
        router_t,
        logit_sums,
        g_up_t,
        g_down_t,
        grad_tokens,
    ) = final_call(
        alone,
        table,
        mods,
        vector,
        logits,
        conds,
        (g_up, o_up, g_down, o_down),
        g_done,
        part,
        dqkv,
        full_qkv,
        tokens,
        ga,
        mod_width,
        fc1_weight.shape[0],
        planes,
        blk,
    )
    small = small.reshape(-1)[:length]
    grad_ada_bias = grad_ada_bias[0]
    logit_sums = logit_sums[0]
    ends = [d, 2 * d, 3 * d, 3 * d + hidden, 4 * d + hidden]
    g_query, g_value, g_proj_bias, g_b1, g_b2, g_router = jnp.split(small, ends)
    return (
        output,
        grad_tokens,
        grad_ada_t.T,
        grad_ada_bias,
        g_qkv,
        g_query,
        g_value,
        g_proj,
        g_proj_bias,
        g_up_t.T,
        g_b1,
        g_down_t.T,
        g_b2,
        router_t[:heads].T,
        logit_sums[:heads],
        router_t[heads : heads + groups].T,
        logit_sums[heads : heads + groups],
        g_router,
    )


def solution(mesh):
    planes = mesh.shape["wide"] // 2
    return jax.shard_map(
        functools.partial(on_device, planes),
        mesh=mesh,
        in_specs=(
            P(("narrow", "wide"), None),
            P(("narrow", "wide"), None),
            P(("narrow", "wide")),
            P(("narrow", "wide"), None),
            P(("narrow", "wide"), None),
            P(("narrow", "wide")),
            P(None, ("narrow", "wide")),
            P(("narrow", "wide")),
            P(("narrow", "wide"), None),
            P(),
            P(),
            P(("narrow", "wide"), None),
            P(),
            P("wide", "narrow"),
            P(),
            P("wide", "narrow"),
            P(),
            P(),
            P(),
            P(),
            P(),
            P(),
            P(("narrow", "wide"), None),
        ),
        out_specs=(
            P(("narrow", "wide"), None),
            P(("narrow", "wide"), None),
            P(None, ("narrow", "wide")),
            P(("narrow", "wide")),
            P(("narrow", "wide"), None),
            P(),
            P(),
            P(("narrow", "wide"), None),
            P(),
            P("wide", "narrow"),
            P(),
            P("wide", "narrow"),
            P(),
            P(),
            P(),
            P(),
            P(),
            P(),
        ),
        check_vma=False,
    )
```

```python
import functools

import jax
import jax.numpy as jnp
from jax import lax
from jax.experimental import pallas as pl
from jax.experimental.pallas import tpu as pltpu
from jax.sharding import PartitionSpec as P

HIGHEST = lax.Precision.HIGHEST
F32 = jnp.float32
BF = jnp.bfloat16
EPSILON = 1e-06
MASKED = -1e30
LOG2E = 1.4426950408889634
WINDOW = 256
NN = (((1,), (0,)), ((), ()))
NT = (((1,), (1,)), ((), ()))
TN = (((0,), (0,)), ((), ()))
VMEM_SPEC = pl.BlockSpec(memory_space=pltpu.VMEM)
ANY_SPEC = pl.BlockSpec(memory_space=pl.ANY)
MESH = pl.DeviceIdType.MESH
SMEM_SPEC = pl.BlockSpec(memory_space=pltpu.SMEM)


def dg(a, b, dims):
    return lax.dot_general(a, b, dims, preferred_element_type=F32)


def params(mib=60, collective_id=None):
    if collective_id is None:
        return pltpu.CompilerParams(vmem_limit_bytes=mib << 20)
    return pltpu.CompilerParams(
        vmem_limit_bytes=mib << 20, collective_id=collective_id, has_side_effects=True
    )


def up_to(count, multiple):
    return -(-count // multiple) * multiple


def pad_rows(x):
    return jnp.pad(x, ((0, up_to(x.shape[0], 16) - x.shape[0]), (0, 0)))


def spread_out(steps, count):
    groups = [[] for _ in range(count)]
    for i, step in enumerate(steps):
        groups[i * count // len(steps)].append(step)
    return groups


def run_at(index, groups):
    for i, group in enumerate(groups):
        if group:

            @pl.when(index == i)
            def _(group=group):
                for step in group:
                    step()


def shape(dims, dtype=F32):
    return jax.ShapeDtypeStruct(dims, dtype)


def whole(*dims):
    return pl.BlockSpec(dims, lambda i: (0,) * len(dims), pipeline_mode=pl.Buffered(1))


def rows_of(block, width):
    return pl.BlockSpec((block, width), lambda i: (i, 0))


def row_vec(width):
    return pl.BlockSpec((1, 1, width), lambda i: (i, 0, 0))


def ln_parts(x):
    centered = x - jnp.mean(x, axis=-1, keepdims=True)
    rstd = lax.rsqrt(jnp.mean(centered * centered, axis=-1, keepdims=True) + EPSILON)
    return centered * rstd, rstd


def ln_back(grad_y, normed, rstd, scale):
    m = grad_y * (1.0 + scale)
    mean_m = jnp.mean(m, axis=-1, keepdims=True)
    mean_mn = jnp.mean(m * normed, axis=-1, keepdims=True)
    return (m - mean_m - normed * mean_mn) * rstd


def col_sum(x):
    return jnp.sum(x, axis=0, keepdims=True)


def gelu_parts(x):
    k0 = 0.7978845608028654
    k1 = 0.044715
    x2 = x * x
    t = jnp.tanh(k0 * x * (1.0 + k1 * x2))
    half = 0.5 * (1.0 + t)
    return x * half, half + 0.5 * x * (1.0 - t * t) * (k0 * (1.0 + 3.0 * k1 * x2))


class Place:
    def __init__(self, planes):
        self.planes = planes
        self.n = lax.axis_index("narrow")
        w = lax.axis_index("wide")
        self.z = w // 2
        self.c = w % 2
        self.xn = self.n + 1 - 2 * (self.n % 2)
        self.yn = self.n + 2 - 4 * (self.n // 2)
        self.dn = 3 - self.n

    def dev(self, n, z, c):
        return (n, z * 2 + c)

    def greet(self):
        sem = pltpu.get_barrier_semaphore()

        def signal(n, z, c):
            pl.semaphore_signal(sem, inc=1, device_id=self.dev(n, z, c), device_id_type=MESH)

        signal(self.xn, self.z, self.c)
        signal(self.yn, self.z, self.c)
        signal(self.n, self.z, 1 - self.c)
        for k in range(1, self.planes):
            signal(self.n, lax.rem(self.z + k, self.planes), self.c)

    def meet(self):
        pl.semaphore_wait(pltpu.get_barrier_semaphore(), self.planes + 2)

    def has(self, step):
        return self.z + step >= 0 if step < 0 else self.z + step < self.planes


def plane_turn(planes, j):
    order = sorted(range(1, planes), key=lambda k: (-min(k, planes - k), k)) + [0]
    if isinstance(j, int):
        return order[j]
    return sum(jnp.where(j == i, k, 0) for i, k in enumerate(order))


def remote(src, dst, sems, idx, device):
    return pltpu.make_async_remote_copy(
        src_ref=src,
        dst_ref=dst,
        send_sem=sems.at[0, idx],
        recv_sem=sems.at[1, idx],
        device_id=device,
        device_id_type=MESH,
    )


class Gather:
    def __init__(self, place, src, out, own, zs, xs, ys, ds, cs):
        self.p, self.src, self.out = place, src, out
        self.own, self.zs, self.xs, self.ys, self.ds, self.cs = own, zs, xs, ys, ds, cs
        self.steps = [0]
        for k in range(1, place.planes):
            self.steps += [-k, k]

    def index(self, k):
        return k + self.p.planes - 1

    def at(self, n, k, c=None):
        p = self.p
        return self.out.at[n, p.z + k, p.c if c is None else c]

    def mine(self, k):
        return self.src if k == 0 else self.at(self.p.n, k)

    def via(self, k):
        p = self.p
        return (p.xn, p.yn) if k % 2 == 0 else (p.yn, p.xn)

    def copy(self, kind, k):
        p = self.p
        i = self.index(k)
        if kind == "x":
            return remote(self.mine(k), self.at(p.n, k), self.xs, i, p.dev(p.xn, p.z, p.c))
        if kind == "y":
            return remote(self.mine(k), self.at(p.n, k), self.ys, i, p.dev(p.yn, p.z, p.c))
        if kind == "d":
            via, to = self.via(k)
            return remote(self.at(via, k), self.at(via, k), self.ds, i, p.dev(to, p.z, p.c))
        if kind == "up" or kind == "down":
            step = 1 if kind == "up" else -1
            j = self.index(k - step)
            return remote(self.mine(k), self.at(p.n, k), self.zs, j, p.dev(p.n, p.z + step, p.c))
        j = ("c", "C", "d2", "D").index(kind)
        n = (p.n, p.xn, p.yn, p.dn)[j]
        shard = self.mine(k) if j == 0 else self.at(n, k)
        slot = j * (2 * p.planes - 1) + i
        return remote(shard, self.at(n, k), self.cs, slot, p.dev(p.n, p.z, 1 - p.c))

    def arrived(self, n, k, sems, idx, c=None):
        p = self.p
        dst = self.at(n, k, c)
        remote(dst, dst, sems, idx, p.dev(p.xn, p.z, p.c)).wait_recv()

    def run(self, part):
        if part == "begin":
            pltpu.make_async_copy(self.src, self.at(self.p.n, 0), self.own).start()
            self.spread(0)
        elif part == "end":
            pltpu.make_async_copy(self.src, self.at(self.p.n, 0), self.own).wait()
            for k in self.steps:
                self.when(self.p.has(k), functools.partial(self.finish, k))
        else:
            kind, k = part
            self.when(self.p.has(k), functools.partial(getattr(self, kind), k))

    def when(self, cond, do):
        pl.when(cond)(do)

    def onward(self, k, act):
        p = self.p
        if k <= 0:
            self.when(p.has(1), lambda: act(self.copy("up", k)))
        if k >= 0:
            self.when(p.has(-1), lambda: act(self.copy("down", k)))

    def spread(self, k):
        self.onward(k, lambda copy: copy.start())
        self.copy("x", k).start()
        self.copy("y", k).start()
        self.copy("c", k).start()

    def plane(self, k):
        self.arrived(self.p.n, k, self.zs, self.index(k))
        self.spread(k)

    def near(self, k):
        p = self.p
        self.arrived(p.xn, k, self.xs, self.index(k))
        if k % 2 == 0:
            self.copy("d", k).start()
        self.copy("C", k).start()
        self.arrived(p.yn, k, self.ys, self.index(k))
        if k % 2 == 1:
            self.copy("d", k).start()
        self.copy("d2", k).start()

    def far(self, k):
        self.arrived(self.p.dn, k, self.ds, self.index(k))
        self.copy("D", k).start()

    def finish(self, k):
        p = self.p
        for j, n in enumerate((p.n, p.xn, p.yn, p.dn)):
            self.arrived(n, k, self.cs, j * (2 * p.planes - 1) + self.index(k), 1 - p.c)
        for kind in ("x", "y", "d", "c", "C", "d2", "D"):
            self.copy(kind, k).wait_send()
        self.onward(k, lambda copy: copy.wait_send())

    def parts(self):
        found = ["begin"]
        rounds = [[0]] + [[-k, k] for k in range(1, self.p.planes)]
        for r in range(len(rounds) + 2):
            if 0 < r < len(rounds):
                found += [("plane", k) for k in rounds[r]]
            if 1 <= r <= len(rounds):
                found += [("near", k) for k in rounds[r - 1]]
            if 2 <= r:
                found += [("far", k) for k in rounds[r - 2]]
        return found + ["end"]

    @staticmethod
    def scratch(planes):
        dma = pltpu.SemaphoreType.DMA
        span = 2 * planes - 1
        return [dma(())] + [dma((2, span))] * 4 + [dma((2, 4 * span))]


class Scatter:
    def __init__(self, place, turn, js, source, own, r1, r2, r3, r4, own_sem, s1, s2, s3, s4):
        self.p, self.turn, self.js, self.source = place, turn, js, source
        self.own, self.r1, self.r2, self.r3, self.r4 = own, r1, r2, r3, r4
        self.own_sem, self.s1, self.s2, self.s3, self.s4 = own_sem, s1, s2, s3, s4

    def owner(self, j):
        return lax.rem(self.p.z + plane_turn(self.p.planes, j), self.p.planes)

    def moves_on(self, j):
        return j + 1 < self.p.planes

    def load(self, j):
        slot = self.js.index(j) % 2
        return pltpu.make_async_copy(
            self.source(j, self.p.c), self.own.at[slot], self.own_sem.at[slot]
        )

    def x_first(self, j):
        return (self.js.index(j) + self.turn) % 2 == 0

    def sides(self, j):
        p = self.p
        return (p.xn, p.yn) if self.x_first(j) else (p.yn, p.xn)

    def copies(self, stage, j):
        p = self.p
        i = self.js.index(j)
        side, other = self.sides(j)
        if stage == 1:
            to = p.dev(p.n, p.z, 1 - p.c)
            return [remote(self.source(j, 1 - p.c), self.r1.at[i], self.s1, i, to)]
        if stage == 2:
            to = p.dev(side, p.z, p.c)
            return [
                remote(self.r1.at[i, side], self.r2.at[i, 0], self.s2, 2 * i, to),
                remote(self.r1.at[i, p.dn], self.r2.at[i, 1], self.s2, 2 * i + 1, to),
            ]
        if stage == 3:
            to = p.dev(other, p.z, p.c)
            return [remote(self.r1.at[i, other], self.r3.at[i], self.s3, i, to)]
        to = p.dev(p.n, self.owner(j), p.c)
        return [remote(self.r1.at[i, p.n], self.r4.at[i], self.s4, i, to)]

    def issue(self, stage, j):
        for copy in self.copies(stage, j):
            copy.start()

    def sent(self, stage, j):
        for copy in self.copies(stage, j):
            copy.wait_send()

    def begin(self):
        if self.own is not None:
            self.load(self.js[0]).start()

    def take(self, stage, j):
        p = self.p
        i = self.js.index(j)
        for copy in self.copies(stage, j):
            copy.wait_recv()
        side, other = self.sides(j)

        def add(n, value):
            self.r1[i, n] = self.r1[i, n] + value

        if stage == 1:
            if self.own is None:
                mine = self.source(j, p.c)
            else:
                self.load(j).wait()
                if i + 1 < len(self.js):
                    self.load(self.js[i + 1]).start()
                mine = self.own.at[i % 2]
            for n in range(4):
                add(n, mine[n])
        elif stage == 2:
            add(p.n, self.r2[i, 0])
            add(other, self.r2[i, 1])
        else:
            add(p.n, self.r3[i])
            if self.moves_on(j):
                self.issue(4, j)

    def total(self, stages=(1, 2, 3, 4)):
        found = None
        for i, j in enumerate(self.js):
            if self.moves_on(j):
                self.copies(4, j)[0].wait_recv()
                part = self.r4[i].astype(F32)
            else:
                part = self.r1[i, self.p.n].astype(F32)
            found = part if found is None else found + part
        for j in self.js:
            for stage in stages:
                if stage < 4 or self.moves_on(j):
                    self.sent(stage, j)
        return found

    @staticmethod
    def scratch(count, rows, cols, load=True):
        dma = pltpu.SemaphoreType.DMA
        own = [pltpu.VMEM((2, 4, rows, cols), BF)] if load else []
        return own + [
            pltpu.VMEM((count, 4, rows, cols), BF),
            pltpu.VMEM((count, 2, rows, cols), BF),
            pltpu.VMEM((count, rows, cols), BF),
            pltpu.VMEM((count, rows, cols), BF),
            dma((2,)),
            dma((2, count)),
            dma((2, 2 * count)),
            dma((2, count)),
            dma((2, count)),
        ]


def scatter_steps(scatters, span=2, window=2):
    js = scatters[0].js
    units = range(len(scatters))
    queue = [(u, j) for j in js for u in units]
    x_items, y_items = [], []
    for i in range(0, len(js), span):
        pair = [(u, j) for j in js[i : i + span] for u in units]
        for stage in (2, 3):
            for u, j in pair:
                first = scatters[u].x_first(j)
                (x_items if first == (stage == 2) else y_items).append((stage, u, j))
    sent = []
    done = []

    def begin():
        for s in scatters:
            s.begin()
        for u, j in queue[:window]:
            scatters[u].issue(1, j)
            sent.append((u, j))

    def ready(stage, u, j):
        if stage == 2:
            while (u, j) not in done:
                v, i = queue[len(done)]
                scatters[v].take(1, i)
                done.append((v, i))
                if len(sent) < len(queue):
                    v, i = queue[len(sent)]
                    scatters[v].issue(1, i)
                    sent.append((v, i))

    def step(i):
        for items in (x_items, y_items):
            if window <= i < len(items) + window:
                stage, u, j = items[i - window]
                scatters[u].take(stage, j)
        for items in (x_items, y_items):
            if i < len(items):
                stage, u, j = items[i]
                ready(stage, u, j)
                scatters[u].issue(stage, j)

    count = max(len(x_items), len(y_items)) + window
    return [begin] + [functools.partial(step, i) for i in range(count)]


class Exchange:
    def __init__(self, place, src, out, sems, same):
        self.p, self.src, self.out, self.sems, self.same = place, src, out, sems, same
        self.wide = 2 * place.planes
        self.total = 4 * self.wide
        self.me = place.n * self.wide + place.z * 2 + place.c

    def device(self, i):
        other = lax.rem(self.me + i, self.total)
        return other // self.wide, lax.rem(other, self.wide)

    def greet(self):
        sem = pltpu.get_barrier_semaphore()

        def signal(i, carry):
            pl.semaphore_signal(sem, inc=1, device_id=self.device(i), device_id_type=MESH)
            return carry

        lax.fori_loop(1, self.total, signal, 0)

    def meet(self):
        pl.semaphore_wait(pltpu.get_barrier_semaphore(), self.total - 1)

    def copy(self, i):
        other = lax.rem(self.me + i, self.total)
        src = self.src if self.same else self.src.at[other]
        return remote(src, self.out.at[self.me], self.sems, i, self.device(i))

    def each(self, do):
        def body(i, carry):
            do(i)
            return carry

        lax.fori_loop(1, self.total, body, 0)

    def start(self):
        self.each(lambda i: self.copy(i).start())
        self.out[self.me] = self.src[...] if self.same else self.src[self.me]

    def arrive(self):
        def wait(i):
            dst = self.out.at[lax.rem(self.me + self.total - i, self.total)]
            remote(dst, dst, self.sems, i, self.device(i)).wait_recv()

        self.each(wait)

    def end(self):
        self.each(lambda i: self.copy(i).wait_send())

    @staticmethod
    def scratch(planes):
        return pltpu.SemaphoreType.DMA((2, 8 * planes))


class Stream:
    def __init__(self, slots, sems, out):
        self.slots, self.sems, self.out = slots, sems, out
        self.count = 0

    def copy(self, i):
        rows = self.slots.shape[1]
        return pltpu.make_async_copy(
            self.slots.at[i % 2], self.out.at[pl.ds(i * rows, rows)], self.sems.at[i % 2]
        )

    def put(self, value):
        i = self.count
        if i >= 2:
            self.copy(i - 2).wait()
        self.slots[i % 2] = value
        self.copy(i).start()
        self.count = i + 1

    def end(self):
        for i in range(max(self.count - 2, 0), self.count):
            self.copy(i).wait()

    @staticmethod
    def scratch(rows, width, dtype):
        return [pltpu.VMEM((2, rows, width), dtype), pltpu.SemaphoreType.DMA((2,))]


def head_window(h, hd, width):
    a = pl.multiple_of(jnp.minimum((h * hd) // 128, (width - WINDOW) // 128) * 128, 128)
    lane = lax.broadcasted_iota(jnp.int32, (1, WINDOW), 1) + a
    return a, (lane >= h * hd) & (lane < h * hd + hd)


QUERY_BIAS, VALUE_BIAS, PROJ_BIAS, DOWN_BIAS, ROUTER = range(5)
SHIFT1, SCALE1, GATE1, SHIFT2, SCALE2, GATE2 = range(6)


def forward_kernel(
    off_ref,
    single_ref,
    gate_ref,
    keep_ref,
    cond_ref,
    ada_ref,
    ada_bias_ref,
    qkv_shard_ref,
    proj_shard_ref,
    up_t_ref,
    down_t_ref,
    query_bias_ref,
    value_bias_ref,
    proj_bias_ref,
    down_bias_ref,
    router_ref,
    tokens_ref,
    cot_ref,
    lse_ref,
    tg_ref,
    conds_ref,
    table_ref,
    vec_ref,
    n1_ref,
    qkv_ref,
    w_ref,
    wp_ref,
    att_ref,
    gated_ref,
    attn_ref,
    after_ref,
    n2_ref,
    gm_ref,
    g_up_ref,
    g_down_ref,
    lse_sc,
    shard_ref,
    up_ref,
    down_ref,
    g_s,
    mod_local,
    mods_s,
    flat_s,
    tok_s,
    w_s,
    wp_s,
    n1_s,
    qkv_s,
    att_s,
    gated_s,
    cot_s,
    cot_sems,
    sems,
    attn_slots,
    attn_sems,
    after_slots,
    after_sems,
    n2_slots,
    n2_sems,
    gm_slots,
    gm_sems,
    cond_sems,
    mod_sems,
    *gather_sems,
    heads,
    blk,
    planes,
):
    t, d = tok_s.shape
    hd = d // heads
    nb = t // blk
    c = hd**-0.5 * LOG2E
    place = Place(planes)
    weights = Gather(place, shard_ref, g_s, *gather_sems[:6])
    gathers = [
        Gather(place, up_ref, g_up_ref, *gather_sems[6:12]),
        Gather(place, down_ref, g_down_ref, *gather_sems[12:]),
    ]
    conds = Exchange(place, cond_ref, conds_ref, cond_sems, True)
    mods = Exchange(place, mod_local, mods_s, mod_sems, False)
    conds.greet()
    rows = proj_shard_ref.shape[0]
    for b in range(3):
        shard_ref[b * rows : (b + 1) * rows, :] = qkv_shard_ref[:, b * d : (b + 1) * d]
    shard_ref[3 * rows : 4 * rows, :] = proj_shard_ref[...]
    conds.meet()
    weights.run("begin")
    conds.start()
    for src, dst in ((up_t_ref, up_ref), (down_t_ref, down_ref)):
        natural = src[...].T
        quarter = natural.shape[0] // 4
        dst[:quarter, :] = jnp.concatenate(
            [natural[k * quarter : (k + 1) * quarter] for k in range(4)], axis=1
        )
    vec_ref[...] = jnp.zeros_like(vec_ref)
    for i, ref in enumerate(
        (query_bias_ref, value_bias_ref, proj_bias_ref, down_bias_ref, router_ref)
    ):
        vec_ref[i : i + 1, :] = ref[...].astype(F32).reshape(1, d)

    def run_group(i):
        for step in groups[i]:
            step()

    moves = {
        name: pltpu.make_async_copy(src, dst, sems.at[i])
        for i, (name, src, dst) in enumerate(
            (
                ("tok", tokens_ref, tok_s),
                ("w", w_s, w_ref),
                ("wp", wp_s, wp_ref),
                ("n1", n1_s, n1_ref),
                ("qkv", qkv_s, qkv_ref),
                ("att", att_s, att_ref),
                ("gated", gated_s, gated_ref),
            )
        )
    }

    def cot_copy(i):
        return pltpu.make_async_copy(
            cot_ref.at[pl.ds(i * blk, blk)], cot_s.at[i % 2], cot_sems.at[i % 2]
        )

    moves["tok"].start()
    for i in range(2):
        cot_copy(i).start()
    parts = weights.parts()
    rest = [(g, part) for part in parts[1:-1] for g in gathers]
    mod_local[...] = jnp.zeros_like(mod_local)
    for part in parts[1:4]:
        weights.run(part)
    conds.arrive()
    devices, rows, lanes = conds_ref.shape
    width = ada_ref.shape[0]
    slots = table_ref.shape[0]
    every = conds_ref[...].reshape(devices * rows, lanes)
    columns = ada_bias_ref[...]
    for j in range(d // lanes):
        piece = dg(every, ada_ref[:, j * lanes : (j + 1) * lanes], NT).reshape(devices, rows, width)
        columns = columns + piece[:, slots * j : slots * (j + 1)]
    mod_local[:, :slots, :width] = columns.astype(BF)
    mods.start()
    middle = 9
    for part in parts[4:middle]:
        weights.run(part)
    for g in gathers:
        g.run("begin")
    late = parts[middle:-1]
    for part in late[: len(late) // 2]:
        weights.run(part)
    for g, part in rest[:4]:
        g.run(part)
    for part in late[len(late) // 2 :]:
        weights.run(part)
    at_end = (place.z == 0) | (place.z == planes - 1)
    count = 2 * nb + heads

    def only(cond, items):
        def run():
            @pl.when(cond)
            def _():
                for g, part in items:
                    g.run(part)

        return [run] if items else []

    only(at_end, rest[4:8])[0]()
    ends = spread_out(rest[8:], count - 2) + [[]] * 2
    inner = [[]] * 2 + spread_out(rest[4:], count - 2)
    groups = [
        only(at_end, ends[i]) + only(jnp.logical_not(at_end), inner[i]) for i in range(count)
    ]
    mods.arrive()
    for i in range(devices):
        flat_s[:slots, i * width : (i + 1) * width] = mods_s[i, :slots, :width].astype(F32)
    single = single_ref[0]
    flat = flat_s[:slots, :]
    flat = flat * (1.0 - single) + flat[:1] * single
    for k in range(6):
        table_ref[:, k, :] = flat[:, k * d : (k + 1) * d]
    weights.run("end")
    r = d // devices
    for i in range(devices):
        at = (i // (2 * planes), i // 2 % planes, i % 2)
        rows = slice(i * r, (i + 1) * r)
        for b in range(3):
            w_s[rows, b * d : (b + 1) * d] = g_s[at + (slice(b * r, (b + 1) * r),)]
        wp_s[rows, :] = g_s[at + (slice(3 * r, 4 * r),)]
    moves["w"].start()
    moves["wp"].start()
    moves["tok"].wait()

    def vector(i):
        return vec_ref[i : i + 1, :]

    def mod(i, k):
        return table_ref[i, k : k + 1, :]

    bias = jnp.concatenate(
        [vector(QUERY_BIAS), jnp.zeros((1, d), F32), vector(VALUE_BIAS)], axis=1
    )
    for i in range(nb):
        rows = slice(i * blk, (i + 1) * blk)
        normed, _ = ln_parts(tok_s[rows, :])
        low = (normed * (1.0 + mod(i, SCALE1)) + mod(i, SHIFT1)).astype(BF)
        n1_s[:, rows] = low.T
        qkv_s[rows, :] = (dg(low, w_s[...], NN) + bias).astype(BF)
        run_group(i)
    moves["n1"].start()
    moves["qkv"].start()
    off = off_ref[0]
    lane128 = lax.broadcasted_iota(jnp.int32, (1, 128), 1)

    def body(h, carry):
        a, mask = head_window(h, hd, d)
        keys = qkv_s[:, pl.ds(pl.multiple_of(d + a, 128), WINDOW)]
        values = qkv_s[:, pl.ds(pl.multiple_of(2 * d + a, 128), WINDOW)]
        cols = pl.ds(a, WINDOW)
        for i in range(nb):
            rows = pl.ds(i * blk, blk)
            q = qkv_s[rows, cols]
            q = jnp.where(mask, q, jnp.zeros_like(q))
            s = dg(q, keys, NT)
            cuts = [s[:, j * blk : (j + 1) * blk] for j in range(nb)]
            own = jnp.max(cuts[i], axis=1, keepdims=True) * c
            others = functools.reduce(jnp.maximum, [cuts[j] for j in range(nb) if j != i])
            m = jnp.maximum(own, jnp.max(others, axis=1, keepdims=True) * c + off)
            m_off = m - off
            ps = [jnp.exp2(cuts[j] * c - (m if j == i else m_off)) for j in range(nb)]
            total = jnp.sum(functools.reduce(jnp.add, ps), axis=1, keepdims=True)
            p = jnp.concatenate([x.astype(BF) for x in ps], axis=1)
            o = dg(p, values, NN) * (1.0 / total)
            og = (o * gate_ref[i, :, cols]).astype(BF)
            att_s[rows, cols] = jnp.where(mask, o, att_s[rows, cols])
            gated_s[rows, cols] = jnp.where(mask, og, gated_s[rows, cols])
            lse_sc[rows, :] = jnp.where(lane128 == h, m + jnp.log2(total), lse_sc[rows, :])
        run_at(h, groups[nb : nb + heads])
        return carry

    lax.fori_loop(0, heads, body, 0)
    moves["att"].start()
    moves["gated"].start()
    lse_ref[...] = lse_sc[...].T[:heads, :]
    streams = [
        Stream(attn_slots, attn_sems, attn_ref),
        Stream(after_slots, after_sems, after_ref),
        Stream(n2_slots, n2_sems, n2_ref),
        Stream(gm_slots, gm_sems, gm_ref),
    ]
    for i in range(nb):
        rows = slice(i * blk, (i + 1) * blk)
        attn = dg(gated_s[rows, :], wp_s[...], NN) + vector(PROJ_BIAS)
        streams[0].put(attn)
        after = tok_s[rows, :] + mod(i, GATE1) * attn
        streams[1].put(after)
        normed, _ = ln_parts(after)
        y = normed * (1.0 + mod(i, SCALE2)) + mod(i, SHIFT2)
        streams[2].put(y.astype(BF))
        token_gate = jax.nn.sigmoid(jnp.sum(y * vector(ROUTER), axis=1, keepdims=True))
        tg_ref[rows, :] = token_gate
        cot_copy(i).wait()
        cot = cot_s[i % 2]
        streams[3].put((cot * (mod(i, GATE2) * (keep_ref[rows, :] * token_gate))).astype(BF))
        if i + 2 < nb:
            cot_copy(i + 2).start()
        run_group(nb + heads + i)
    for g in gathers:
        g.run("end")
    for stream in streams:
        stream.end()
    for name in ("w", "wp", "n1", "qkv", "att", "gated"):
        moves[name].wait()
    conds.end()
    mods.end()


def forward_call(
    off, single, gate_rows, keep, cond, ada_t, ada_bias, qkv_w, proj_w, up_t, down_t, vectors, tokens, cot, heads, blk, planes
):
    t, d = tokens.shape
    devices = 8 * planes
    slots = t // blk
    lanes = up_to(ada_t.shape[0], 128)
    shard = (up_to(4 * proj_w.shape[0], 16), d)
    unit = (up_to(up_t.shape[1] // 4, 16), d)
    gathered = shape((4, planes, 2) + unit, BF)
    dma = pltpu.SemaphoreType.DMA
    return pl.pallas_call(
        functools.partial(forward_kernel, heads=heads, blk=blk, planes=planes),
        out_shape=(
            shape((heads, t)),
            shape((t, 1)),
            shape((devices,) + cond.shape, BF),
            shape((slots, 6, d)),
            shape((8, d)),
            shape((d, t), BF),
            shape((t, 3 * d), BF),
            shape((d, 3 * d), BF),
            shape((d, d), BF),
            shape((t, d)),
            shape((t, d), BF),
            shape((t, d)),
            shape((t, d)),
            shape((t, d), BF),
            shape((t, d), BF),
            gathered,
            gathered,
        ),
        in_specs=[SMEM_SPEC] * 2 + [VMEM_SPEC] * 14 + [ANY_SPEC] * 2,
        out_specs=(VMEM_SPEC,) * 5 + (ANY_SPEC,) * 12,
        scratch_shapes=[
            pltpu.VMEM((t, 128), F32),
            pltpu.VMEM(shard, BF),
            pltpu.VMEM(unit, BF),
            pltpu.VMEM(unit, BF),
            pltpu.VMEM((4, planes, 2) + shard, BF),
            pltpu.VMEM((devices, 16, lanes), BF),
            pltpu.VMEM((devices, 16, lanes), BF),
            pltpu.VMEM((up_to(slots, 8), 6 * d), F32),
            pltpu.VMEM((t, d), F32),
            pltpu.VMEM((d, 3 * d), BF),
            pltpu.VMEM((d, d), BF),
            pltpu.VMEM((d, t), BF),
            pltpu.VMEM((t, 3 * d), BF),
            pltpu.VMEM((t, d), F32),
            pltpu.VMEM((t, d), BF),
            pltpu.VMEM((2, blk, d), F32),
            dma((2,)),
            dma((7,)),
        ]
        + Stream.scratch(blk, d, F32) * 2
        + Stream.scratch(blk, d, BF) * 2
        + [Exchange.scratch(planes)] * 2
        + Gather.scratch(planes) * 3,
        compiler_params=params(63, collective_id=2),
        name="forward",
    )(
        off, single, gate_rows, keep, cond, ada_t, ada_bias, qkv_w, proj_w, up_t, down_t, *vectors, tokens, cot
    )


def backward_kernel(
    off_ref,
    qkv_ref,
    do_ref,
    lse_ref,
    delta_ref,
    n1t_ref,
    gp_ref,
    up_ref,
    down_ref,
    dqkv_ref,
    bias_ref,
    g_up_ref,
    g_down_ref,
    done_ref,
    part_ref,
    kt_sc,
    dqt_sc,
    part_sem,
    *rest,
    heads,
    blk,
    planes,
    cuts,
):
    t, d = do_ref.shape
    hd = d // heads
    nb = t // blk
    scale = hd**-0.5
    c = scale * LOG2E
    width = d // cuts
    devices = 8 * planes
    r = d // devices
    first = planes // 2
    place = Place(planes)
    place.greet()
    slots, rest = rest[: cuts - 1], rest[cuts - 1 :]
    each = 10
    js = list(range(first, planes))

    def kept(ref):
        return lambda j, c: ref.at[:, j - first, c]

    def local(ref):
        return lambda j, c: ref.at[:, lax.rem(place.z + plane_turn(planes, j), planes), c]

    ups = [
        Scatter(place, u, js, kept(ref), *rest[each * u : each * (u + 1)])
        for u, ref in enumerate((up_ref, down_ref))
    ]
    rest = rest[2 * each :]
    each -= 1
    chains = [
        Scatter(
            place, m, list(range(planes)), local(slots[m]), None, *rest[each * m : each * (m + 1)]
        )
        for m in range(cuts - 1)
    ]
    up_steps = scatter_steps(ups)
    chain_steps = [scatter_steps([chain], planes) for chain in chains]
    kt_sc[...] = qkv_ref[:, d : 2 * d].T
    place.meet()
    up_steps[0]()
    ends = [-(-width * (m + 1) // hd) for m in range(cuts)]
    queues = [[] for _ in range(heads + 1)]

    def place_steps(steps, start, first, stop):
        queues[start] += steps[:2]
        for i, step in enumerate(steps[2:]):
            queues[first + i * (stop - first) // max(len(steps) - 3, 1)].append(step)

    place_steps(up_steps[1:], 0, ends[0] + 1, ends[1] + 1)
    for m in range(cuts - 1):
        steps = chain_steps[m][1:]
        place_steps(steps, ends[m], min(ends[m] + 4 - m, heads), min(ends[m] + 7, heads))

    off = off_ref[0]

    def body(h, carry, start, end):
        a, mask = head_window(h, hd, d)
        cols = pl.ds(a, WINDOW)
        key_cols = pl.ds(pl.multiple_of(d + a, 128), WINDOW)
        value_cols = pl.ds(pl.multiple_of(2 * d + a, 128), WINDOW)
        keys = qkv_ref[:, key_cols]
        values = qkv_ref[:, value_cols]
        keys_t = kt_sc[cols, :]
        dk_sum = None
        dv_sum = None
        for i in range(nb):
            rows = pl.ds(i * blk, blk)
            span = slice(i * blk, (i + 1) * blk)
            q = qkv_ref[rows, cols]
            q = jnp.where(mask, q, jnp.zeros_like(q))
            do = do_ref[rows, cols]
            do = jnp.where(mask, do, jnp.zeros_like(do))
            lse = lse_ref[pl.ds(h, 1), span]
            delta = delta_ref[pl.ds(h, 1), span]
            s_t = dg(keys, q, NT)
            dp_t = dg(values, do, NT)
            ps = []
            ds = []
            for j in range(nb):
                cut = slice(j * blk, (j + 1) * blk)
                p = jnp.exp2(s_t[cut] * c - (lse if j == i else lse - off))
                ps.append(p.astype(BF))
                ds.append((p * (dp_t[cut] - delta)).astype(BF))
            p = jnp.concatenate(ps, axis=0)
            grad_s = jnp.concatenate(ds, axis=0)
            dv = dg(p, do, NN)
            dk = dg(grad_s, q, NN)
            dv_sum = dv if dv_sum is None else dv_sum + dv
            dk_sum = dk if dk_sum is None else dk_sum + dk
            dqt_sc[:, span] = (dg(keys_t, grad_s, NN) * scale).astype(BF)
        dk = (dk_sum * scale).astype(BF)
        dqkv_ref[:, key_cols] = jnp.where(mask, dk, dqkv_ref[:, key_cols])
        dqkv_ref[:, value_cols] = jnp.where(mask, dv_sum.astype(BF), dqkv_ref[:, value_cols])
        dqkv_ref[:, cols] = jnp.where(mask, dqt_sc[...].T, dqkv_ref[:, cols])
        run_at(h - start, queues[start:end])
        return carry

    def weight_part(m, out):
        dqkv = jnp.concatenate(
            [dqkv_ref[:, b * d + m * width : b * d + (m + 1) * width] for b in range(3)], axis=1
        )
        bias_ref[m] = col_sum(dqkv.astype(F32))
        grad = dg(n1t_ref[...], dqkv, NN).astype(BF)
        for i in range(devices):
            rows = slice(i * r, (i + 1) * r)
            at = (i // (2 * planes), i // 2 % planes, i % 2)
            for b in range(3):
                out[at + (slice(b * r, (b + 1) * r),)] = grad[rows, b * width : (b + 1) * width]
            out[at + (slice(3 * r, 4 * r),)] = gp_ref[rows, m * width : (m + 1) * width]

    for m in range(cuts):
        start = 0 if m == 0 else ends[m - 1]
        lax.fori_loop(start, ends[m], functools.partial(body, start=start, end=ends[m]), 0)
        if m + 1 < cuts:
            weight_part(m, slots[m])
            chain_steps[m][0]()
    for j in chains[0].js:
        chains[0].sent(1, j)
    weight_part(cuts - 1, slots[0])
    keep = pltpu.make_async_copy(slots[0], part_ref, part_sem)
    keep.start()
    for step in queues[heads]:
        step()
    g_up_ref[...] = ups[0].total()
    g_down_ref[...] = ups[1].total()
    for m, chain in enumerate(chains):
        stages = (2, 3, 4) if m == 0 else (1, 2, 3, 4)
        done_ref[:, m * width : (m + 1) * width] = chain.total(stages)
    keep.wait()


def backward_call(off, qkv, do, lse, delta, n1t, g_proj, up, down, heads, blk, planes, cuts):
    t, d = do.shape
    rows, cols = up.shape[3:]
    width = d // cuts
    part = (4, planes, 2, up_to(4 * d // (8 * planes), 16), width)
    return pl.pallas_call(
        functools.partial(backward_kernel, heads=heads, blk=blk, planes=planes, cuts=cuts),
        out_shape=(
            shape((t, 3 * d), BF),
            shape((cuts, 1, 3 * width)),
            shape((rows, cols)),
            shape((rows, cols)),
            shape((part[3], (cuts - 1) * width)),
            shape(part, BF),
        ),
        in_specs=[SMEM_SPEC] + [VMEM_SPEC] * 6 + [ANY_SPEC] * 2,
        out_specs=(VMEM_SPEC,) * 5 + (ANY_SPEC,),
        scratch_shapes=[
            pltpu.VMEM((d, t), BF),
            pltpu.VMEM((WINDOW, t), BF),
            pltpu.SemaphoreType.DMA(()),
        ]
        + [pltpu.VMEM(part, BF)] * (cuts - 1)
        + Scatter.scratch(planes - planes // 2, rows, cols) * 2
        + Scatter.scratch(planes, part[3], width, False) * (cuts - 1),
        compiler_params=params(63, collective_id=3),
        name="attention_backward",
    )(off, qkv, do, lse, delta, n1t, g_proj, up, down)


def mlp_kernel(
    n2_ref,
    gm_ref,
    b1_ref,
    cs_ref,
    g1_ref,
    g2_ref,
    mlp_ref,
    gn2_ref,
    gb1_ref,
    gch_ref,
    o1_ref,
    o2_ref,
    p1_ref,
    p2_ref,
    g1_s,
    g2_s,
    w1_s,
    w2_s,
    sc_s,
    gp_s,
    p1_s,
    p2_s,
    g_sems,
    p_sems,
    *rest,
    blk,
    planes,
):
    t, d = n2_ref.shape
    nb = t // blk
    hidden = w1_s.shape[0]
    quarter = hidden // 8
    piece = d // 4
    j = pl.program_id(0)
    place = Place(planes)
    hosted = planes // 2
    half = len(rest) // 2
    scatters = [
        Scatter(place, u, list(range(hosted)), lambda j, c, p=p: p.at[:, c], None, *scratch)
        for u, (p, scratch) in enumerate(((p1_s, rest[:half]), (p2_s, rest[half:])))
    ]

    def loads(step):
        plane = lax.rem(place.z + plane_turn(planes, step), planes)
        return [
            pltpu.make_async_copy(g.at[:, plane], slot, g_sems.at[i])
            for i, (g, slot) in enumerate(((g1_ref, g1_s), (g2_ref, g2_s)))
        ]

    def keeps(step):
        return [
            pltpu.make_async_copy(slot, p.at[:, step - hosted], p_sems.at[i])
            for i, (slot, p) in enumerate(((p1_s, p1_ref), (p2_s, p2_ref)))
        ]

    def early(step):
        for s in scatters:
            if step - 1 < hosted:
                s.take(1, step - 1)
                s.issue(2, step - 1)
        for s in scatters:
            if 0 <= step - 2 < hosted:
                s.take(3, step - 2)

    def late(step):
        for s in scatters:
            if step - 1 < hosted:
                s.take(2, step - 1)
                s.issue(3, step - 1)
                s.sent(1, step - 1)
        if step - 1 >= hosted:
            for copy in keeps(step - 1):
                copy.wait()

    def at_steps(do):
        for step in range(1, planes):
            pl.when(j == step)(functools.partial(do, step))

    def places():
        for c in range(2):
            for k in range(4):
                yield c, slice((4 * c + k) * quarter, (4 * c + k + 1) * quarter), k

    @pl.when(j == 0)
    def _():
        for copy in loads(0):
            copy.start()
        place.greet()
        mlp_ref[...] = jnp.zeros_like(mlp_ref)
        gn2_ref[...] = jnp.zeros_like(gn2_ref)

    for copy in loads(j):
        copy.wait()
    for c, rows, k in places():
        cols = slice(k * piece, (k + 1) * piece)
        for w, g in ((w1_s, g1_s), (w2_s, g2_s)):
            w[rows, :] = jnp.concatenate([g[n, c, :quarter, cols] for n in range(4)], axis=1)

    @pl.when(j + 1 < planes)
    def _():
        for copy in loads(j + 1):
            copy.start()

    pl.when(j == 0)(place.meet)
    at_steps(early)
    w1 = w1_s[...]
    w2 = w2_s[...]
    grad_bias = None
    for i in range(nb):
        rows = slice(i * blk, (i + 1) * blk)
        pre = dg(n2_ref[rows, :], w1, NT) + b1_ref[0]
        grad_scaled = dg(gm_ref[rows, :], w2, NT)
        act, slope = gelu_parts(pre)
        gate = cs_ref[0, i : i + 1]
        scaled = (act * gate).astype(BF)
        grad_pre = (grad_scaled * gate * slope).astype(BF)
        gch_ref[0, i : i + 1] = col_sum(grad_scaled * act)
        part = col_sum(grad_pre.astype(F32))
        grad_bias = part if grad_bias is None else grad_bias + part
        sc_s[rows, :] = scaled
        gp_s[rows, :] = grad_pre
        mlp_ref[rows, :] += dg(scaled, w2, NN)
        gn2_ref[rows, :] += dg(grad_pre, w1, NN)
    gb1_ref[0] = grad_bias

    at_steps(late)
    for left, right, out in ((gp_s, n2_ref, p1_s), (sc_s, gm_ref, p2_s)):
        grad = dg(left[...], right[...], TN).astype(BF)
        for c, rows, k in places():
            for n in range(4):
                out[n, c, :quarter, k * piece : (k + 1) * piece] = grad[rows, n * piece : (n + 1) * piece]
    for step in range(planes):

        @pl.when(j == step)
        def _(step=step):
            if step < hosted:
                for s in scatters:
                    s.issue(1, step)
            else:
                for copy in keeps(step):
                    copy.start()

    @pl.when(j == planes - 1)
    def _():
        o1_ref[...] = scatters[0].total((2, 3, 4))
        o2_ref[...] = scatters[1].total((2, 3, 4))
        for copy in keeps(planes - 1):
            copy.wait()


def mlp_call(n2, gm, g1, g2, b1, gates, blk):
    t, d = n2.shape
    planes, rows = g1.shape[1], g1.shape[3]
    nb, ff = gates.shape
    hb = ff // planes
    hosted = planes // 2

    def turn(j):
        return lax.rem(lax.axis_index("wide") // 2 + plane_turn(planes, j), planes)

    b_spec = pl.BlockSpec((1, 1, hb), lambda j: (turn(j), 0, 0))
    c_spec = pl.BlockSpec((1, nb, hb), lambda j: (turn(j), 0, 0))
    kept = shape((4, planes - hosted, 2, rows, d), BF)
    dma = pltpu.SemaphoreType.DMA
    mlp, gn2, gb1, gch, o1, o2, p1, p2 = pl.pallas_call(
        functools.partial(mlp_kernel, blk=blk, planes=planes),
        grid=(planes,),
        out_shape=(
            shape((t, d)),
            shape((t, d)),
            shape((planes, 1, hb)),
            shape((planes, nb, hb)),
            shape((rows, d)),
            shape((rows, d)),
            kept,
            kept,
        ),
        in_specs=[whole(t, d), whole(t, d), b_spec, c_spec, ANY_SPEC, ANY_SPEC],
        out_specs=(whole(t, d), whole(t, d), b_spec, c_spec, whole(rows, d), whole(rows, d))
        + (ANY_SPEC,) * 2,
        scratch_shapes=[pltpu.VMEM((4, 2, rows, d), BF)] * 2
        + [pltpu.VMEM((hb, d), BF)] * 2
        + [pltpu.VMEM((t, hb), BF)] * 2
        + [pltpu.VMEM((4, 2, rows, d), BF)] * 2
        + [dma((2,))] * 2
        + Scatter.scratch(hosted, rows, d, False) * 2,
        compiler_params=params(62, collective_id=5),
        name="feed_forward",
    )(n2, gm, b1.reshape(planes, 1, hb), gates.reshape(nb, planes, hb).transpose(1, 0, 2), g1, g2)
    return mlp, gn2, o1, o2, p1, p2, gb1.reshape(ff), gch.transpose(1, 0, 2).reshape(nb, ff)


def middle_back_kernel(
    mlp_ref,
    gn2_ref,
    after_ref,
    attn_ref,
    cot_ref,
    gm_ref,
    gated_ref,
    att_ref,
    tg_ref,
    keep_ref,
    w_ref,
    vec_ref,
    table_ref,
    head_ref,
    out_ref,
    ga_ref,
    do_ref,
    delta_ref,
    gw_ref,
    mod_ref,
    sums_ref,
    gw_s,
    *,
    heads,
):
    d = after_ref.shape[1]
    hd = d // heads
    first = pl.program_id(0) == 0
    after = after_ref[...]
    cot = cot_ref[...]
    gate2 = table_ref[0, GATE2 : GATE2 + 1]
    tg = tg_ref[...]
    keep = keep_ref[...]
    normed, rstd = ln_parts(after)
    scale2 = table_ref[0, SCALE2 : SCALE2 + 1]
    y = normed * (1.0 + scale2) + table_ref[0, SHIFT2 : SHIFT2 + 1]
    mlp_out = mlp_ref[...] + vec_ref[DOWN_BIAS : DOWN_BIAS + 1]
    open_gate = keep * tg
    out_ref[...] = after + (gate2 * open_gate) * mlp_out
    weighted = cot * mlp_out
    grad_tg = jnp.sum(weighted * gate2, axis=1, keepdims=True) * keep
    coef = grad_tg * tg * (1.0 - tg)
    gy = gn2_ref[...] + coef * vec_ref[ROUTER : ROUTER + 1]
    ga = cot + ln_back(gy, normed, rstd, scale2)
    ga_ref[...] = ga
    attn = attn_ref[...]
    g_attn = (ga * table_ref[0, GATE1 : GATE1 + 1]).astype(BF)
    mod_ref[0] = jnp.concatenate(
        [col_sum(ga * attn), col_sum(gy), col_sum(gy * normed), col_sum(weighted * open_gate)], axis=0
    )
    sums = jnp.concatenate(
        [
            col_sum(coef * y),
            col_sum(g_attn.astype(F32)),
            col_sum(gm_ref[...].astype(F32)),
        ],
        axis=0,
    )
    g_gated = dg(g_attn, w_ref[...], NT)
    att = att_ref[...]
    mod_ref[1] = jnp.concatenate([col_sum(g_gated * att), jnp.zeros((3, d), F32)], axis=0)
    do = (g_gated * head_ref[0]).astype(BF)
    do_ref[...] = do
    lane = lax.broadcasted_iota(jnp.int32, (heads, d), 1)
    head = lax.broadcasted_iota(jnp.int32, (heads, d), 0) * hd
    pick = jnp.where((lane >= head) & (lane < head + hd), 1.0, 0.0)
    delta_ref[...] = lax.dot_general(
        pick, do.astype(F32) * att, NT, precision=HIGHEST, preferred_element_type=F32
    )
    gw = dg(gated_ref[...], g_attn, TN)

    @pl.when(first)
    def _():
        sums_ref[...] = sums
        gw_s[...] = gw

    @pl.when(jnp.logical_not(first))
    def _():
        sums_ref[...] += sums
        gw_s[...] += gw

    @pl.when(pl.program_id(0) == pl.num_programs(0) - 1)
    def _():
        gw_ref[...] = gw_s[...].astype(BF)


def middle_back_call(
    mlp, gn2, after, attn, cot, gm, gated, att, tg, keep, w, vecs, table, head_rows, heads, blk
):
    t, d = after.shape
    nb = t // blk
    r, v, column = rows_of(blk, d), row_vec(d), rows_of(blk, 1)
    return pl.pallas_call(
        functools.partial(middle_back_kernel, heads=heads),
        grid=(nb,),
        out_shape=(
            shape((t, d)),
            shape((t, d)),
            shape((t, d), BF),
            shape((heads, t)),
            shape((d, d), BF),
            shape((nb * 2, 4, d)),
            shape((3, d)),
        ),
        in_specs=[r] * 8 + [column, column, whole(d, d), whole(*vecs.shape)]
        + [pl.BlockSpec((1,) + table.shape[1:], lambda i: (i, 0, 0)), v],
        out_specs=(
            r,
            r,
            r,
            pl.BlockSpec((heads, blk), lambda i: (0, i)),
            whole(d, d),
            pl.BlockSpec((2, 4, d), lambda i: (i, 0, 0)),
            whole(3, d),
        ),
        scratch_shapes=[pltpu.VMEM((d, d), F32)],
        compiler_params=params(),
        name="middle_backward",
    )(mlp, gn2, after, attn, cot, gm, gated, att, tg, keep, w, vecs, table, head_rows)


def final_kernel(
    single_ref,
    table_ref,
    mods_ref,
    sums_ref,
    logits_ref,
    conds_ref,
    up1_ref,
    up2_ref,
    down1_ref,
    down2_ref,
    done_ref,
    part_ref,
    dqkv_ref,
    w_ref,
    tokens_ref,
    ga_ref,
    qkv_grad_ref,
    proj_grad_ref,
    query_ref,
    value_ref,
    proj_ref,
    b1_ref,
    b2_ref,
    token_ref,
    ada_ref,
    ada_bias_ref,
    head_ref,
    chan_ref,
    logit_ref,
    up_ref,
    down_ref,
    grad_ref,
    conds_s,
    all_sums,
    own_mods,
    all_mods,
    all_logits,
    w_s,
    dq_s,
    tok_s,
    ga_s,
    w_sem,
    in_sems,
    out_slots,
    out_sems,
    mod_sems,
    logit_sems,
    *rest,
    planes,
    blk,
):
    place = Place(planes)
    mods = Exchange(place, own_mods, all_mods, mod_sems, False)
    logits = Exchange(place, logits_ref, all_logits, logit_sems, True)

    def source(j, c):
        return part_ref.at[:, lax.rem(place.z + plane_turn(planes, j), planes), c]

    sums = Gather(place, sums_ref, all_sums, *rest[:6])
    chain = Scatter(place, 0, list(range(planes)), source, *rest[6:])
    t, d = tokens_ref.shape
    nb = t // blk
    w_load = pltpu.make_async_copy(w_ref, w_s, w_sem)

    def loads(i):
        rows = pl.ds(i * blk, blk)
        return [
            pltpu.make_async_copy(src.at[rows], dst.at[i % 2], in_sems.at[k, i % 2])
            for k, (src, dst) in enumerate(((dqkv_ref, dq_s), (tokens_ref, tok_s), (ga_ref, ga_s)))
        ]

    mods.greet()
    w_load.start()
    for copy in loads(0) + loads(1):
        copy.start()
    own_mods[...] = jnp.zeros_like(own_mods)
    mods.meet()
    steps = scatter_steps([chain], planes)
    steps[0]()
    sums.run("begin")
    logits.start()
    out = Stream(out_slots, out_sems, grad_ref)
    tables = []

    def block(i):
        if i == 0:
            w_load.wait()
        for copy in loads(i):
            copy.wait()
        gy = dg(dq_s[i % 2], w_s[...], NT)
        normed, rstd = ln_parts(tok_s[i % 2])
        out.put(ga_s[i % 2] + ln_back(gy, normed, rstd, table_ref[i, SCALE1 : SCALE1 + 1]))
        tables.append([col_sum(gy), col_sum(gy * normed)] + [mods_ref[i, k : k + 1] for k in range(4)])
        if i + 2 < nb:
            for copy in loads(i + 2):
                copy.start()

    def exchange():
        single = single_ref[0]
        devices = own_mods.shape[0]
        width = ada_bias_ref.shape[1]
        flat = [jnp.concatenate(row, axis=1) for row in tables]
        rows = [(1.0 - single) * row for row in flat]
        rows[0] = flat[0] + single * functools.reduce(jnp.add, flat[1:])
        every = jnp.concatenate(rows, axis=0).astype(BF)
        for i in range(devices):
            own_mods[i, :nb, :width] = every[:, i * width : (i + 1) * width]
        mods.start()

    def products():
        mods.arrive()
        logits.arrive()
        devices, rows, _ = conds_s.shape
        conds = conds_s[...].reshape(devices * rows, d)
        got = all_mods[...].reshape(devices * rows, -1)
        columns = ada_bias_ref.shape[1]
        ada_ref[...] = dg(got, conds, TN)[:columns]
        ada_bias_ref[...] = col_sum(got.astype(F32))[:, :columns]
        got = all_logits[...].reshape(devices * rows, -1)
        router = lax.dot_general(
            got, conds.astype(F32), TN, precision=HIGHEST, preferred_element_type=F32
        )
        heads = head_ref.shape[0]
        head_ref[...] = router[:heads]
        chan_ref[...] = router[heads : heads + chan_ref.shape[0]]
        logit_ref[...] = col_sum(got)

    def local_work():
        lanes = conds_ref.shape[2]
        conds_s[...] = jnp.zeros_like(conds_s)
        for j in range(d // lanes):
            rows = slice(nb * j, nb * (j + 1))
            conds_s[:, :nb, j * lanes : (j + 1) * lanes] = conds_ref[:, rows, :]
        piece = up_ref.shape[0]
        quarter = up_ref.shape[1] // 4
        for a, b, to in ((up1_ref, up2_ref, up_ref), (down1_ref, down2_ref, down_ref)):
            both = a[...] + b[...]
            rows = [both[:quarter, k * piece : (k + 1) * piece] for k in range(4)]
            to[...] = jnp.concatenate(rows, axis=0).T

    parts = [functools.partial(sums.run, part) for part in sums.parts()[1:-1]]
    rest = steps[3:]
    work = [
        [functools.partial(block, 0)],
        steps[1:3],
        [functools.partial(block, i) for i in range(1, nb - 1)],
        rest[:1],
        [functools.partial(block, nb - 1), exchange],
        rest[1:2],
        [local_work],
        rest[2:],
    ]
    work = [do for group in work for do in group]
    for do, group in zip(work, spread_out(parts, len(work))):
        do()
        for part in group:
            part()
    products()
    sums.run("end")
    total = jnp.sum(all_sums[...].reshape((8 * planes,) + sums_ref.shape), axis=0)
    start = 0
    for to in (query_ref, value_ref, proj_ref, b1_ref, b2_ref, token_ref):
        stop = start + to.shape[0]
        to[...] = total[start:stop]
        start = stop
    last = chain.total()
    r = proj_grad_ref.shape[0]
    ready = done_ref.shape[1]
    for b in range(4):
        rows = slice(b * r, (b + 1) * r)
        to, start = (qkv_grad_ref, b * d) if b < 3 else (proj_grad_ref, 0)
        to[:, start : start + ready] = done_ref[rows, :]
        to[:, start + ready : start + d] = last[rows]
    out.end()
    mods.end()
    logits.end()


def final_call(
    single, table, mods, sums, logits, conds, pairs, done, part, dqkv, w, tokens, ga, mod_width, hidden, ff, heads, groups, planes, blk
):
    rows, width = part.shape[3:]
    t, d = tokens.shape
    devices = 8 * planes
    spread = (4, planes, 2)
    padded = logits.shape[0]
    blocks = (devices, padded, up_to(mod_width, 128))
    piece = shape((d // 4, hidden))
    dma = pltpu.SemaphoreType.DMA
    return pl.pallas_call(
        functools.partial(final_kernel, planes=planes, blk=blk),
        out_shape=(
            shape((d // devices, 3 * d)),
            shape((d // devices, d)),
            shape((d // 128, 128)),
            shape((d // 128, 128)),
            shape((d // 128, 128)),
            shape((ff // 128, 128)),
            shape((d // 128, 128)),
            shape((d // 128, 128)),
            shape((mod_width, d)),
            shape((1, mod_width)),
            shape((heads, d)),
            shape((groups, d)),
            shape((1, logits.shape[1])),
            piece,
            piece,
            shape((t, d)),
        ),
        in_specs=[SMEM_SPEC] + [VMEM_SPEC] * 10 + [ANY_SPEC] * 5,
        out_specs=(VMEM_SPEC,) * 15 + (ANY_SPEC,),
        scratch_shapes=[
            pltpu.VMEM((devices, padded, d), BF),
            pltpu.VMEM(spread + sums.shape, F32),
            pltpu.VMEM(blocks, BF),
            pltpu.VMEM(blocks, BF),
            pltpu.VMEM((devices,) + logits.shape, F32),
            pltpu.VMEM(w.shape, BF),
            pltpu.VMEM((2, blk, 3 * d), BF),
            pltpu.VMEM((2, blk, d), F32),
            pltpu.VMEM((2, blk, d), F32),
            dma(()),
            dma((3, 2)),
        ]
        + Stream.scratch(blk, d, F32)
        + [Exchange.scratch(planes)] * 2
        + Gather.scratch(planes)
        + Scatter.scratch(planes, rows, width),
        compiler_params=params(collective_id=4),
        name="last_sums",
    )(single, table, mods, sums, logits, conds, *pairs, done, part, dqkv, w, tokens, ga)


def on_device(
    planes,
    tokens,
    conditioning,
    row_items,
    head_mask,
    chan_mask,
    skip_mask,
    ada_weight,
    ada_bias,
    qkv_weight,
    query_bias,
    value_bias,
    proj_weight,
    proj_bias,
    fc1_weight,
    fc1_bias,
    fc2_weight,
    fc2_bias,
    head_router,
    head_router_bias,
    chan_router,
    chan_router_bias,
    token_router,
    cotangent,
):
    t, d = tokens.shape
    slots = conditioning.shape[0]
    heads = head_mask.shape[1]
    groups = chan_mask.shape[1]
    hidden = fc1_bias.shape[0]
    hd = d // heads
    unit = hidden // groups
    blk = t // slots
    single = row_items[0] == 1
    off = jnp.where(single, 0.0, MASKED).astype(F32).reshape(1)

    def per_block(table):
        return jnp.where(single, table[:1], table)

    def per_slot(blocks):
        total = jnp.sum(blocks, axis=0, keepdims=True)
        first = (jnp.arange(slots) == 0).reshape((slots,) + (1,) * (blocks.ndim - 1))
        return jnp.where(single, jnp.where(first, total, 0.0), blocks)

    devices = 8 * planes
    silu_cond = jax.nn.silu(conditioning.astype(F32)).astype(BF)
    conds_pad = pad_rows(silu_cond.reshape(slots, -1, 128).transpose(1, 0, 2).reshape(-1, 128))
    mod_width = ada_bias.shape[0]
    alone = jnp.where(single, 1.0, 0.0).astype(F32).reshape(1)

    def router(weight, bias, mask):
        gate = jax.nn.sigmoid(dg(silu_cond, weight, NN) + bias.astype(F32))
        mask = mask.astype(F32)
        return mask * gate, mask * gate * (1.0 - gate)

    head_gate, head_slope = router(head_router, head_router_bias, head_mask)
    chan_gate, chan_slope = router(chan_router, chan_router_bias, chan_mask)
    head_rows = jnp.repeat(per_block(head_gate), hd, axis=1)[:, None, :]
    chan_rows = jnp.repeat(per_block(chan_gate), unit, axis=1)
    keep = (1.0 - skip_mask.astype(F32))[:, None]

    (
        lse,
        tg,
        conds,
        table,
        vecs,
        n1t,
        qkv,
        full_qkv,
        full_proj,
        att,
        gated,
        attn,
        after,
        n2,
        gm,
        g_up,
        g_down,
    ) = forward_call(
        off,
        alone,
        head_rows,
        keep,
        conds_pad,
        ada_weight.T,
        ada_bias.astype(F32)[None],
        qkv_weight,
        proj_weight,
        fc1_weight.T,
        fc2_weight.T,
        (query_bias, value_bias, proj_bias, fc2_bias, token_router),
        tokens,
        cotangent,
        heads,
        blk,
        planes,
    )
    mlp, gn2, o_up, o_down, p_up, p_down, gb1, gch = mlp_call(
        n2, gm, g_up, g_down, fc1_bias.astype(F32), chan_rows, blk
    )
    output, ga, do, delta, g_proj, mods, sums = middle_back_call(
        mlp,
        gn2,
        after,
        attn,
        cotangent,
        gm,
        gated,
        att,
        tg,
        keep,
        full_proj,
        vecs,
        table,
        head_rows,
        heads,
        blk,
    )
    mods = mods.reshape(slots, 8, d)
    dqkv, qkv_sums, g_up, g_down, g_done, part = backward_call(
        off, qkv, do, lse, delta, n1t, g_proj, p_up, p_down, heads, blk, planes, 3
    )
    qkv_sums = qkv_sums.reshape(3, 3, d // 3).transpose(1, 0, 2).reshape(3, d)
    g_head = per_slot(jnp.sum(mods[:, 4].reshape(slots, heads, hd), axis=2)) * head_slope
    g_chan = per_slot(jnp.sum(gch.reshape(slots, groups, unit), axis=2)) * chan_slope
    logits = jnp.pad(
        jnp.concatenate([g_head, g_chan], axis=1),
        ((0, up_to(slots, 16) - slots), (0, up_to(heads + groups, 128) - heads - groups)),
    )
    vector = jnp.concatenate([qkv_sums[0], qkv_sums[2], sums[1], gb1, sums[2], sums[0]])
    length = vector.shape[0]
    vector = jnp.pad(vector, (0, up_to(length, 1024) - length)).reshape(-1, 128)
    (
        g_qkv,
        g_proj,
        g_query,
        g_value,
        g_proj_bias,
        g_b1,
        g_b2,
        g_router,
        grad_ada_t,
        grad_ada_bias,
        head_t,
        chan_t,
        logit_sums,
        g_up_t,
        g_down_t,
        grad_tokens,
    ) = final_call(
        alone,
        table,
        mods,
        vector,
        logits,
        conds,
        (g_up, o_up, g_down, o_down),
        g_done,
        part,
        dqkv,
        full_qkv,
        tokens,
        ga,
        mod_width,
        fc1_weight.shape[0],
        hidden,
        heads,
        groups,
        planes,
        blk,
    )
    grad_ada_bias = grad_ada_bias[0]
    logit_sums = logit_sums[0]
    g_query, g_value, g_proj_bias, g_b1, g_b2, g_router = [
        x.reshape(-1) for x in (g_query, g_value, g_proj_bias, g_b1, g_b2, g_router)
    ]
    return (
        output,
        grad_tokens,
        grad_ada_t.T,
        grad_ada_bias,
        g_qkv,
        g_query,
        g_value,
        g_proj,
        g_proj_bias,
        g_up_t.T,
        g_b1,
        g_down_t.T,
        g_b2,
        head_t.T,
        logit_sums[:heads],
        chan_t.T,
        logit_sums[heads : heads + groups],
        g_router,
    )


def solution(mesh):
    planes = mesh.shape["wide"] // 2
    return jax.shard_map(
        functools.partial(on_device, planes),
        mesh=mesh,
        in_specs=(
            P(("narrow", "wide"), None),
            P(("narrow", "wide"), None),
            P(("narrow", "wide")),
            P(("narrow", "wide"), None),
            P(("narrow", "wide"), None),
            P(("narrow", "wide")),
            P(None, ("narrow", "wide")),
            P(("narrow", "wide")),
            P(("narrow", "wide"), None),
            P(),
            P(),
            P(("narrow", "wide"), None),
            P(),
            P("wide", "narrow"),
            P(),
            P("wide", "narrow"),
            P(),
            P(),
            P(),
            P(),
            P(),
            P(),
            P(("narrow", "wide"), None),
        ),
        out_specs=(
            P(("narrow", "wide"), None),
            P(("narrow", "wide"), None),
            P(None, ("narrow", "wide")),
            P(("narrow", "wide")),
            P(("narrow", "wide"), None),
            P(),
            P(),
            P(("narrow", "wide"), None),
            P(),
            P("wide", "narrow"),
            P(),
            P("wide", "narrow"),
            P(),
            P(),
            P(),
            P(),
            P(),
            P(),
        ),
        check_vma=False,
    )
```
